512 devices in a mesh: cls: 8 (over x, core), pix: 32 (over z_lo, y), rep: 2 (over z_hi).
Axes of the slice: x: 4, y: 4, z: 16 (z_hi: 2, z_lo: 8; z = z_hi * 8 + z_lo), core: 2. Of those that a mesh axis runs over, the one named last changes fastest.
Arguments:
- particles: float32 [1024, 128, 2, 256], P(('cls', 'rep'), 'pix'), may hold values from -24 to 24
- references: float32 [200, 128, 2, 256], P('cls', 'pix'), may hold values from -10 to 10
- ctf_table: float32 [16, 128], P(None, 'pix'), may hold values from -1 to 1
- defocus_ids: int32 [1024], P(('cls', 'rep')), may hold values from 0 to 15, as said below
- rotation_ids: int32 [36], replicated, may hold values from 0 to 359, as said below
Outputs:
- new_references: float32 [200, 128, 2, 256], P('cls', 'pix')
The draws below stay inside these ranges and needn't reach their ends.
Inputs may be any that keep to these rules, and one draw needn't show every extreme that they name: `defocus_ids`: the id of particle i is i * 16 // 1024 or one more, at most 15; the first particle's id is 0. `rotation_ids`: rotation a lies in [a * 10, (a + 1) * 10); the first is 0 and the last is 359.
All inputs are finite; a program needn't handle non-finite values.
Results may differ from the reference program's by a relative error of at most 0.0035.
Values may be sent and summed in bfloat16 or wider, within the bound.
A program may use at most 64 MiB of HBM per device.

```python
import math
import jax
import jax.numpy as jnp
from jax import lax

CYCLES = 128
SAMPLES = 256
CLASSES = 200
ANGLES = 36
TURN_STEPS = 360
DEFOCI = 16
PARTICLES = 1024


def common_draws(key):
    subkeys = jax.random.split(key, 11)
    cycle_pos = (jnp.arange(CYCLES, dtype=jnp.float32) + 0.5) / CYCLES
    cycle_jitter = jnp.exp(jax.random.uniform(subkeys[0], (CYCLES,), jnp.float32, -0.5, 0.5))
    ref_shape = (CLASSES, CYCLES, 2, SAMPLES)
    ref_normal = jnp.clip(jax.random.normal(subkeys[1], ref_shape, jnp.float32), -4.0, 4.0)
    ref_even = jax.random.uniform(subkeys[2], ref_shape, jnp.float32, -1.7, 1.7)
    sector = TURN_STEPS // ANGLES
    angle_slots = jnp.arange(ANGLES, dtype=jnp.int32)
    offsets = jax.random.randint(subkeys[3], (ANGLES,), 0, sector)
    offsets = jnp.where(angle_slots == 0, 0, jnp.where(angle_slots == ANGLES - 1, sector - 1, offsets))
    rotations = (angle_slots * sector + offsets).astype(jnp.int32)
    particle_order = jnp.arange(PARTICLES, dtype=jnp.int32)
    jitter = jax.random.randint(subkeys[4], (PARTICLES,), 0, 2) * (particle_order > 0).astype(jnp.int32)
    defocus = jnp.minimum(particle_order * DEFOCI // PARTICLES + jitter, DEFOCI - 1).astype(jnp.int32)
    defocus_value = 1.0 + jax.random.uniform(subkeys[5], (DEFOCI, 1), jnp.float32)
    damping = 4.0 * jnp.arange(DEFOCI, dtype=jnp.float32)[:, None] / max(DEFOCI - 1, 1)
    radius = cycle_pos[None, :] * cycle_pos[None, :]
    ctf_curves = -jnp.sin(40.0 * math.pi * defocus_value * radius + 0.1) * jnp.exp(-damping * radius)
    picked_class = jax.random.randint(subkeys[6], (PARTICLES,), 0, CLASSES)
    picked_angle = jax.random.randint(subkeys[7], (PARTICLES,), 0, ANGLES)
    unit_scale = jax.random.uniform(subkeys[8], (PARTICLES,), jnp.float32)
    part_shape = (PARTICLES, CYCLES, 2, SAMPLES)
    noise_normal = jnp.clip(jax.random.normal(subkeys[9], part_shape, jnp.float32), -4.0, 4.0)
    noise_even = jax.random.uniform(subkeys[10], part_shape, jnp.float32, -1.7, 1.7)
    return (cycle_pos, cycle_jitter, ref_normal, ref_even, rotations, defocus, ctf_curves, picked_class, picked_angle, unit_scale, noise_normal, noise_even)


def cycle_profile(shared):
    return shared[1] * (0.6 + 1.2 * shared[0])


def shaped_references(shared, ref_base):
    profile = cycle_profile(shared)
    return jnp.clip(ref_base * profile[None, :, None, None], -10.0, 10.0)


def draw_references(key, part):
    shared = common_draws(key)
    ref_base = shared[2]
    return shaped_references(shared, ref_base)


def draw_particles(key, part):
    shared = common_draws(key)
    ref_base = shared[2]
    part_noise = shared[10]
    spread = 2.5
    references = shaped_references(shared, ref_base)
    profile = cycle_profile(shared)
    turn_shift = shared[4][shared[8]] * SAMPLES // TURN_STEPS
    positions = (jnp.arange(SAMPLES, dtype=jnp.int32)[None, :] - turn_shift[:, None]) % SAMPLES
    chosen = references[shared[7]]
    turned = jnp.take_along_axis(chosen, jnp.broadcast_to(positions[:, None, None, :], chosen.shape), axis=3)
    ctf_rows = shared[6][shared[5]]
    scaling = jnp.exp(math.log(spread) * (2.0 * shared[9] - 1.0))
    signal = 0.6 * ctf_rows[:, :, None, None] * turned
    combined = scaling[:, None, None, None] * (signal + profile[None, :, None, None] * part_noise)
    return jnp.clip(combined, -24.0, 24.0)


def draw_ctf_table(key, part):
    shared = common_draws(key)
    return shared[6]


def draw_defocus_ids(key, part):
    shared = common_draws(key)
    return shared[5]


def draw_rotation_ids(key, part):
    shared = common_draws(key)
    return shared[4]


def setup_inputs(seed: int = 0) -> dict:
    arg_keys = jax.random.split(jax.random.key(seed), 6)
    particles = draw_particles(jax.random.fold_in(arg_keys[5], 71), 0)
    references = draw_references(jax.random.fold_in(arg_keys[5], 71), 0)
    ctf_table = draw_ctf_table(jax.random.fold_in(arg_keys[5], 71), 0)
    defocus_ids = draw_defocus_ids(jax.random.fold_in(arg_keys[5], 71), 0)
    rotation_ids = draw_rotation_ids(jax.random.fold_in(arg_keys[5], 71), 0)
    return dict(particles=particles, references=references, ctf_table=ctf_table, defocus_ids=defocus_ids, rotation_ids=rotation_ids)


EPSILON = 1e-06
SHARPNESS = 30.0
PRIOR_WEIGHT = 1.0

def dft_matrix_of(size):
    positions = jnp.arange(size, dtype=jnp.int32)
    turn_count = positions[:, None] * positions[None, :] % size
    radians = turn_count.astype(jnp.float32) * (2.0 * math.pi / size)
    cosine = jnp.cos(radians) / math.sqrt(size)
    sine_part = jnp.sin(radians) / math.sqrt(size)
    top_half = jnp.concatenate([cosine, -sine_part], axis=1)
    bottom_half = jnp.concatenate([sine_part, cosine], axis=1)
    return jnp.concatenate([top_half, bottom_half], axis=0)

def rotation_phases(rotation_ids, size):
    positions = jnp.arange(size, dtype=jnp.int32)
    signed = jnp.where(positions < size // 2, positions, positions - size)
    turn_count = rotation_ids[:, None].astype(jnp.int32) * signed[None, :] % TURN_STEPS
    radians = turn_count.astype(jnp.float32) * (2.0 * math.pi / TURN_STEPS)
    return (jnp.cos(radians), jnp.sin(radians))

def turned_spectra(weighted, cosine, sine_part):
    real_part = weighted[:, :, 0, :]
    imag_part = weighted[:, :, 1, :]
    turned_re = real_part * cosine - imag_part * sine_part
    turned_im = real_part * sine_part + imag_part * cosine
    return jnp.stack([turned_re, turned_im], axis=2).astype(jnp.bfloat16)

def reference(particles, references, ctf_table, defocus_ids, rotation_ids):
    highest = lax.Precision.HIGHEST
    part_total = particles.shape[0]
    row_width = CYCLES * 2 * SAMPLES
    dft_matrix = dft_matrix_of(SAMPLES)
    spectra = jnp.dot(particles.reshape(part_total * CYCLES, 2 * SAMPLES), dft_matrix, precision=highest)
    spectra = spectra.reshape(part_total, CYCLES, 2, SAMPLES)
    ctf_rows = ctf_table[defocus_ids]
    weighted = ctf_rows[:, :, None, None] * spectra
    ref_spectra = jnp.dot(references.reshape(CLASSES * CYCLES, 2 * SAMPLES), dft_matrix, precision=highest).astype(jnp.bfloat16)
    ref_flat = ref_spectra.reshape(CLASSES, row_width)
    cycle_power = lax.optimization_barrier(jnp.sum(jnp.square(ref_spectra.astype(jnp.float32)).reshape(CLASSES, CYCLES, 2 * SAMPLES), axis=2))
    ref_norm = jnp.dot(ctf_table * ctf_table, cycle_power.T, precision=highest)
    part_norm = lax.optimization_barrier(jnp.sum(particles * particles, axis=(1, 2, 3)))
    cosine, sine_part = rotation_phases(rotation_ids, SAMPLES)

    def correlate(phases):
        turned = turned_spectra(weighted, phases[0][None, None, :], phases[1][None, None, :])
        return jnp.dot(turned.reshape(part_total, row_width), ref_flat.T, preferred_element_type=jnp.float32)
    products = lax.map(correlate, (cosine, sine_part))
    scaling = lax.rsqrt(part_norm + EPSILON)[None, :, None] * lax.rsqrt(ref_norm[defocus_ids] + EPSILON)[None, :, :]
    scores = SHARPNESS * products * scaling
    raised = jnp.exp(scores)
    weights = (raised / lax.optimization_barrier(jnp.sum(raised, axis=(0, 2), keepdims=True))).astype(jnp.bfloat16)

    def accumulate(running, inputs):
        turned = turned_spectra(weighted, inputs[0][None, None, :], inputs[1][None, None, :])
        update = jnp.dot(inputs[2].T, turned.reshape(part_total, row_width), preferred_element_type=jnp.float32)
        return (running + update, None)
    numerator = lax.scan(accumulate, jnp.zeros((CLASSES, row_width), jnp.float32), (cosine, sine_part, weights))[0]
    presence = lax.optimization_barrier(jnp.sum(weights.astype(jnp.float32), axis=0))
    density = jnp.dot(presence.T, ctf_rows * ctf_rows, precision=highest)
    new_spectra = numerator.reshape(CLASSES, CYCLES, 2 * SAMPLES) / (density[:, :, None] + PRIOR_WEIGHT)
    new_rows = jnp.dot(new_spectra.reshape(CLASSES * CYCLES, 2 * SAMPLES), dft_matrix.T, precision=highest)
    return new_rows.reshape(CLASSES, CYCLES, 2, SAMPLES)
```

```python
import math

import jax
import jax.numpy as jnp
import numpy as np
from jax import lax
from jax.experimental import pallas as pl
from jax.experimental.pallas import tpu as pltpu
from jax.sharding import PartitionSpec as P

TURN_STEPS = 360
DEFOCI = 16
EPSILON = 1e-06
SHARPNESS = 30.0
PRIOR_WEIGHT = 1.0

F32 = jnp.float32
BF16 = jnp.bfloat16
MESH = pl.DeviceIdType.MESH

SAMPLES = 256
ANGLES = 36
TURN_ROWS = 40
PAIR_ROWS = 2 * TURN_ROWS
PARTICLES_HERE = 64
CYCLES_HERE = 4
CLASSES_HERE = 25
BLOCK = 32
NX, NY, NZ = 4, 4, 8
ALL_CLASSES = 2 * NX * BLOCK
SIDE = 128
ROW_WIDTH = SIDE + CYCLES_HERE * 2 * SAMPLES
GROUPS = 4
Y_ROWS = 2 * PAIR_ROWS
GROUP_ROWS = NY * Y_ROWS
ALL_ROWS = GROUPS * GROUP_ROWS

NN = (((1,), (0,)), ((), ()))
NT = (((1,), (1,)), ((), ()))
TN = (((0,), (0,)), ((), ()))


def dft_matrix():
    positions = np.arange(SAMPLES)
    radians = (positions[:, None] * positions[None, :] % SAMPLES) * (2.0 * math.pi / SAMPLES)
    cosine = np.cos(radians) / math.sqrt(SAMPLES)
    sine = np.sin(radians) / math.sqrt(SAMPLES)
    return np.block([[cosine, -sine], [sine, cosine]]).astype(np.float32)


def walsh_matrix():
    matrix = np.ones((1, 1), np.float32)
    while matrix.shape[0] < ALL_CLASSES:
        matrix = np.block([[matrix, matrix], [matrix, -matrix]])
    return matrix


def split(values):
    high = values.astype(BF16)
    return high, (values - high.astype(F32)).astype(BF16)


def walsh(values, walsh_ref):
    high, low = split(values)
    return lax.dot_general(high, walsh_ref[...], NN, preferred_element_type=F32) + lax.dot_general(
        low, walsh_ref[...], NN, preferred_element_type=F32
    )


def dft(values, high_ref, low_ref):
    high, low = split(values)
    return (
        lax.dot_general(high, high_ref[...], NN, preferred_element_type=F32)
        + lax.dot_general(low, high_ref[...], NN, preferred_element_type=F32)
        + lax.dot_general(high, low_ref[...], NN, preferred_element_type=F32)
    )


def body(
    x_hbm, r_hbm, dft_hbm, walsh_hbm, ctf_hbm, ids_hbm, turns_hbm, out_ref,
    x_ref, r_ref, dft_ref, walsh_f, ctf_in, ids_ref, turns_ref,
    high_ref, low_ref, walsh_ref, ctf_ref, phase_ref,
    padded, x_rows, r_rows, spectra, weighted, power_rows, norm_rows, turned,
    partial_f, partial, far_in, near_in, near_out, z_out, z_in, z_sum, pair_out, pair_in, weights,
    sums, core_out, core_in, xfar_out, xfar_in, xnear_out, xnear_in, rep_out, rep_via, rep_in,
    in_sem, rx_s, rx_r, rf_s, rf_r, rc_s, rc_r,
    fs, fr, ns, nr, zs, zr, zps, zpr, wps, wpr, wzs, wzr, wys, wyr, wfs, wfr,
    cs, cr, xfs, xfr, xns, xnr, p1s, p1r, p2s, p2r,
):
    loads = [
        pltpu.make_async_copy(src, dst, in_sem.at[n])
        for n, (src, dst) in enumerate(
            [
                (r_hbm, r_ref), (dft_hbm, dft_ref), (x_hbm, x_ref), (ids_hbm, ids_ref),
                (turns_hbm, turns_ref), (ctf_hbm, ctf_in), (walsh_hbm, walsh_f),
            ]
        )
    ]
    for load in loads:
        load.start()
    cls = lax.axis_index("cls")
    pix = lax.axis_index("pix")
    rep = lax.axis_index("rep")
    x, core = cls // 2, cls % 2
    z, y = pix // NY, pix % NY
    other = 1 - core
    sibling = {"cls": x * 2 + other}

    def x_peer(d):
        return {"cls": (x + d) % NX * 2 + core}

    def y_peer(d):
        return {"pix": z * NY + (y + d) % NY}

    q, zh = z % 4, z // 4

    def q_peer(q_to):
        return {"pix": (zh * 4 + q_to) * NY + y}

    z_pair = {"pix": (z + 4) % NZ * NY + y}

    far_z = (z + 4) % NZ
    up = (z + 4) // NZ
    via = (
        {"pix": far_z * NY + y, "rep": (rep + up) % 2},
        {"pix": far_z * NY + y, "rep": (rep + 1 - up) % 2},
    )
    partners = (
        [sibling, {"pix": far_z * NY + y, "rep": 1 - rep}]
        + [x_peer(d) for d in (1, 3)]
        + [y_peer(d) for d in (1, 3)]
        + [q_peer((q + d) % 4) for d in range(1, 4)]
        + [z_pair]
    )

    def remote(src, dst, send, recv, device):
        return pltpu.make_async_remote_copy(
            src_ref=src, dst_ref=dst, send_sem=send, recv_sem=recv,
            device_id=device, device_id_type=MESH,
        )

    sent = []

    def start_copy(*args):
        remote(*args).start()

    def send(*args):
        copy = remote(*args)
        copy.start()
        sent.append(copy)

    barrier = pltpu.get_barrier_semaphore()
    for partner in partners:
        pl.semaphore_signal(barrier, inc=1, device_id=partner, device_id_type=MESH)

    loads[0].wait()
    loads[1].wait()
    high, low = split(dft_ref[...])
    high_ref[...] = high
    low_ref[...] = low
    padded[...] = jnp.zeros_like(padded)
    padded[0 : CLASSES_HERE * 16, :] = r_ref[...]
    for r in range(CYCLES_HERE):
        for p in range(2):
            for h in range(2):
                r_rows[r * BLOCK : (r + 1) * BLOCK, p * 256 + h * 128 : p * 256 + h * 128 + 128] = padded[
                    pl.ds(r * 4 + h * 2 + p, BLOCK, stride=16), :
                ]
    own = dft(r_rows[...], high_ref, low_ref).astype(BF16)
    own_rows = pl.ds(pl.multiple_of(cls * BLOCK, BLOCK), BLOCK)
    wide = own.astype(F32)
    power = jnp.sum(wide * wide, axis=1, keepdims=True)
    power_high, power_low = split(power)
    side_lane = lax.broadcasted_iota(jnp.int32, (BLOCK, SIDE), 1)
    side = jnp.zeros((BLOCK, SIDE), F32)
    for r in range(CYCLES_HERE):
        rows = slice(r * BLOCK, (r + 1) * BLOCK)
        spectra[own_rows, SIDE + r * 512 : SIDE + (r + 1) * 512] = own[rows, :]
        side = jnp.where(side_lane == r, power_high.astype(F32)[rows, :], side)
        side = jnp.where(side_lane == CYCLES_HERE + r, power_low.astype(F32)[rows, :], side)
    spectra[own_rows, 0:SIDE] = side.astype(BF16)

    pl.semaphore_wait(barrier, len(partners))
    steps = (1, 3)
    for way in range(2):
        send(
            spectra.at[own_rows, :], spectra.at[own_rows, :],
            rx_s.at[way], rx_r.at[way], x_peer(steps[way]),
        )
    send(spectra.at[own_rows, :], spectra.at[own_rows, :], rc_s.at[0], rc_r.at[0], sibling)

    def class_rows(x_of, core_of):
        return pl.ds(pl.multiple_of((x_of * 2 + core_of) * BLOCK, BLOCK), BLOCK)

    def half_rows(x_of, core_of, half):
        start = (x_of * 2 + core_of) * BLOCK + half * (BLOCK // 2)
        return pl.ds(pl.multiple_of(start, BLOCK // 2), BLOCK // 2)

    for load in loads[2:]:
        load.wait()
    walsh_ref[...] = walsh_f[...].astype(BF16)
    select = (
        lax.broadcasted_iota(jnp.int32, (CYCLES_HERE, 128), 1)
        - lax.broadcasted_iota(jnp.int32, (CYCLES_HERE, 128), 0)
    )
    select = ((select == 0) | (select == CYCLES_HERE)).astype(F32)
    ctf_ref[...] = lax.dot_general(
        ctf_in[...], select, TN, precision=lax.Precision.HIGHEST, preferred_element_type=F32
    )
    shape = (TURN_ROWS, ANGLES)
    on_row = lax.broadcasted_iota(jnp.int32, shape, 0) == lax.broadcasted_iota(jnp.int32, shape, 1)
    turns = jnp.sum(
        jnp.where(on_row, jnp.broadcast_to(turns_ref[...].astype(F32), shape), 0.0),
        axis=1, keepdims=True,
    )
    place = lax.broadcasted_iota(jnp.int32, (TURN_ROWS, SAMPLES), 1)
    signed = jnp.where(place < SAMPLES // 2, place, place - SAMPLES).astype(F32)
    count = turns * signed
    count = count - TURN_STEPS * jnp.floor(count * (1.0 / TURN_STEPS))
    count = jnp.where(count < 0, count + TURN_STEPS, count)
    count = jnp.where(count >= TURN_STEPS, count - TURN_STEPS, count)
    radians = count * (2.0 * math.pi / TURN_STEPS)
    phase_ref[0:TURN_ROWS, :] = jnp.cos(radians)
    phase_ref[TURN_ROWS : 2 * TURN_ROWS, :] = jnp.sin(radians)

    for r in range(CYCLES_HERE):
        for p in range(2):
            for h in range(2):
                x_rows[r * 64 : (r + 1) * 64, p * 256 + h * 128 : p * 256 + h * 128 + 128] = x_ref[
                    pl.ds(r * 4 + h * 2 + p, PARTICLES_HERE, stride=16), :
                ]
    part_square = jnp.zeros((PARTICLES_HERE, 128), F32)
    for r in range(CYCLES_HERE):
        for h in range(4):
            piece = x_rows[r * 64 : (r + 1) * 64, h * 128 : (h + 1) * 128]
            part_square += piece * piece
    part_norm = jnp.sum(part_square, axis=1, keepdims=True)
    picks = (
        lax.broadcasted_iota(jnp.int32, (DEFOCI, PARTICLES_HERE), 0) == ids_ref[...]
    ).astype(F32)
    ctf_rows = lax.dot_general(
        picks, ctf_ref[...], TN, precision=lax.Precision.HIGHEST, preferred_element_type=F32
    )
    particle_spectra = dft(x_rows[...], high_ref, low_ref)
    for r in range(CYCLES_HERE):
        weighted[:, r * 512 : (r + 1) * 512] = (
            ctf_rows[:, r : r + 1] * particle_spectra[r * 64 : (r + 1) * 64, :]
        )
    squared = ctf_rows * ctf_rows
    square_high = squared.astype(BF16).astype(F32)
    lane = lax.broadcasted_iota(jnp.int32, squared.shape, 1)
    power_rows[...] = jnp.where(lane < CYCLES_HERE, square_high, squared - square_high)

    for way in range(2):
        x_of = (x + NX - steps[way]) % NX
        rows = spectra.at[class_rows(x_of, core), :]
        remote(rows, rows, rx_s.at[way], rx_r.at[way], x_peer(steps[way])).wait_recv()
        half = spectra.at[half_rows(x_of, core, way), :]
        send(half, half, rf_s.at[way], rf_r.at[way], x_peer(steps[way]))
        send(rows, rows, rc_s.at[way + 1], rc_r.at[way + 1], sibling)

    cosine = phase_ref[0:TURN_ROWS, :]
    sine = phase_ref[TURN_ROWS : 2 * TURN_ROWS, :]

    def turn_pair(pair, carry):
        rows = pl.ds(pl.multiple_of(pair * PAIR_ROWS, 16), PAIR_ROWS)
        for r in range(CYCLES_HERE):
            real, imag = [], []
            for e in range(2):
                w_re = weighted[pl.ds(pair * 2 + e, 1), r * 512 : r * 512 + 256]
                w_im = weighted[pl.ds(pair * 2 + e, 1), r * 512 + 256 : r * 512 + 512]
                real.append(w_re * cosine - w_im * sine)
                imag.append(w_re * sine + w_im * cosine)
            start = SIDE + r * 512
            turned[rows, start : start + 256] = jnp.concatenate(real, axis=0).astype(BF16)
            turned[rows, start + 256 : start + 512] = jnp.concatenate(imag, axis=0).astype(BF16)
        tail = [
            jnp.broadcast_to(power_rows[pl.ds(pair * 2 + e, 1), :], (TURN_ROWS, 128)) for e in range(2)
        ]
        turned[rows, 0:SIDE] = jnp.concatenate(tail, axis=0).astype(BF16)
        return carry

    lax.fori_loop(0, PARTICLES_HERE // 4, turn_pair, 0)
    x_far = (x + 2) % NX
    for way in range(2):
        half = spectra.at[half_rows(x_far, core, way), :]
        remote(half, half, rf_s.at[way], rf_r.at[way], x_peer(steps[way])).wait_recv()
    rows = spectra.at[class_rows(x_far, core), :]
    send(rows, rows, rc_s.at[3], rc_r.at[3], sibling)
    lax.fori_loop(PARTICLES_HERE // 4, PARTICLES_HERE // 2, turn_pair, 0)

    for n, x_of in enumerate((x, (x + 3) % NX, (x + 1) % NX, x_far)):
        rows = spectra.at[class_rows(x_of, other), :]
        remote(rows, rows, rc_s.at[n], rc_r.at[n], sibling).wait_recv()

    ctf_high, ctf_low = split(ctf_ref[...] * ctf_ref[...])
    ref_norm = lax.dot_general(
        ctf_high, spectra[:, 0:SIDE], NT, preferred_element_type=F32
    ) + lax.dot_general(ctf_low, spectra[:, 0:SIDE], NT, preferred_element_type=F32)
    picked = lax.dot_general(
        picks, ref_norm, TN, precision=lax.Precision.HIGHEST, preferred_element_type=F32
    )
    picked_high = picked.astype(BF16).astype(F32)
    wide_norm = jnp.broadcast_to(part_norm, (PARTICLES_HERE, ALL_CLASSES))
    wide_high = wide_norm.astype(BF16).astype(F32)
    norm_rows[0] = picked_high
    norm_rows[1] = picked - picked_high
    norm_rows[2] = wide_high
    norm_rows[3] = wide_norm - wide_high
    sub = lax.broadcasted_iota(jnp.int32, (8, ALL_CLASSES), 0)

    def z_group(step):
        return (q + 1 + step) % GROUPS

    def y_rows_of(group, y_to):
        return pl.ds(pl.multiple_of(group * GROUP_ROWS + y_to * Y_ROWS, Y_ROWS), Y_ROWS)

    def y_half_of(group, y_to, half):
        start = group * GROUP_ROWS + y_to * Y_ROWS + half * PAIR_ROWS
        return pl.ds(pl.multiple_of(start, PAIR_ROWS), PAIR_ROWS)

    def correlate(step):
        group = z_group(step)
        rows = pl.ds(pl.multiple_of(group * GROUP_ROWS, GROUP_ROWS), GROUP_ROWS)
        partial_f[...] = walsh(
            lax.dot_general(turned[rows, SIDE:], spectra[:, SIDE:], NT, preferred_element_type=F32), walsh_ref
        )

        def patch(pair, carry):
            pieces = []
            for e in range(2):
                start = pl.multiple_of(pair * PAIR_ROWS + e * TURN_ROWS, 8)
                pieces.append(partial_f[pl.ds(start, 32), :])
                last = partial_f[pl.ds(start + 32, 8), :]
                particle = group * 16 + pair * 2 + e
                for n in range(4):
                    last = jnp.where(sub == 4 + n, norm_rows[n, pl.ds(particle, 1), :], last)
                pieces.append(last)
            start = pl.multiple_of(group * GROUP_ROWS + pair * PAIR_ROWS, 16)
            partial[pl.ds(start, PAIR_ROWS), :] = jnp.concatenate(pieces, axis=0).astype(BF16)
            return carry

        lax.fori_loop(0, NY * 2, patch, 0)
        for way in range(2):
            start_copy(
                partial.at[y_half_of(group, (y + 2) % NY, way), :],
                far_in.at[step, way], fs.at[step, way], fr.at[step, way], y_peer(steps[way]),
            )
        for way in range(2):
            start_copy(
                partial.at[y_half_of(group, (y + steps[way]) % NY, 1 - way), :],
                near_in.at[step, way, 1 - way],
                ns.at[step, way, 1 - way], nr.at[step, way, 1 - way], y_peer(steps[way]),
            )

    odd_row = sub % 2 == 1

    def product_rounded(total):
        pieces = []
        for e in range(2):
            start = e * TURN_ROWS
            pieces.append(total[start : start + 32, :])
            last = total[start + 32 : start + 40, :]
            whole = last + pltpu.roll(last, 7, 0)
            high = whole.astype(BF16).astype(F32)
            low = pltpu.roll(whole - high, 1, 0)
            pieces.append(jnp.where(sub < 4, last, jnp.where(odd_row, low, high)))
        return jnp.concatenate(pieces, axis=0).astype(BF16)

    def relay(step):
        group = z_group(step)
        for way in range(2):
            own = partial.at[y_half_of(group, (y + steps[way]) % NY, way), :]
            remote(
                own, far_in.at[step, way], fs.at[step, way], fr.at[step, way], y_peer(steps[way])
            ).wait_recv()
            near_out[step, way] = product_rounded(
                own[...].astype(F32) + far_in[step, way].astype(F32)
            )
            start_copy(
                near_out.at[step, way], near_in.at[step, way, way],
                ns.at[step, way, way], nr.at[step, way, way], y_peer(steps[way]),
            )

    def reduce_y(step):
        group = z_group(step)
        for half in range(2):
            own = partial.at[y_half_of(group, y, half), :]
            total = own[...].astype(F32)
            for way in range(2):
                remote(
                    own, near_in.at[step, way, half],
                    ns.at[step, way, half], nr.at[step, way, half], y_peer(steps[way]),
                ).wait_recv()
                total += near_in[step, way, half].astype(F32)
            z_out[step, half * PAIR_ROWS : (half + 1) * PAIR_ROWS, :] = product_rounded(total)

        @pl.when(step < GROUPS - 1)
        def _():
            start_copy(
                z_out.at[step], z_in.at[step], zs.at[step], zr.at[step], q_peer(group)
            )

    def product_step(step, carry):
        pl.when(step < GROUPS)(lambda: correlate(step))
        pl.when((step > 0) & (step <= GROUPS))(lambda: relay(step - 1))
        pl.when(step > 1)(lambda: reduce_y(step - 2))
        return carry

    lax.fori_loop(0, GROUPS + 2, product_step, 0)

    total = z_out[GROUPS - 1].astype(F32)
    for n in range(GROUPS - 1):
        remote(z_out.at[n], z_in.at[n], zs.at[n], zr.at[n], z_pair).wait_recv()
        total += z_in[n].astype(F32)
    z_sum[...] = total
    pair_out[...] = product_rounded(
        z_sum[pl.ds(pl.multiple_of((1 - zh) * PAIR_ROWS, 16), PAIR_ROWS), :]
    )
    send(pair_out, pair_in, zps, zpr, z_pair)
    mine = z_sum[pl.ds(pl.multiple_of(zh * PAIR_ROWS, 16), PAIR_ROWS), :]
    sums[...] = jnp.zeros_like(sums)
    remote(pair_out, pair_in, zps, zpr, z_pair).wait_recv()
    mine += pair_in[...].astype(F32)

    shape = (TURN_ROWS, ALL_CLASSES)
    valid = (lax.broadcasted_iota(jnp.int32, shape, 0) < ANGLES) & (
        lax.broadcasted_iota(jnp.int32, shape, 1) % BLOCK < CLASSES_HERE
    )
    products = walsh(mine, walsh_ref) * (1.0 / ALL_CLASSES)
    pieces = []
    for e in range(2):
        rows = mine[e * TURN_ROWS : (e + 1) * TURN_ROWS, :]
        ref_row = rows[36:37, :] + rows[37:38, :]
        part_row = rows[38:39, :] + rows[39:40, :]
        scaling = lax.rsqrt(part_row + EPSILON) * lax.rsqrt(ref_row + EPSILON)
        scores = jnp.where(
            valid, SHARPNESS * products[e * TURN_ROWS : (e + 1) * TURN_ROWS, :] * scaling, 0.0
        )
        raised = jnp.where(valid, jnp.exp(scores), 0.0)
        total = jnp.sum(jnp.sum(raised, axis=0, keepdims=True), axis=1, keepdims=True)
        pieces.append(raised / total)

    own_pair = weights.at[y_half_of(q, y, zh), :]
    own_pair[...] = jnp.concatenate(pieces, axis=0).astype(BF16)
    send(own_pair, own_pair, wps, wpr, z_pair)
    pair = weights.at[y_half_of(q, y, 1 - zh), :]
    remote(pair, pair, wps, wpr, z_pair).wait_recv()
    group_rows = weights.at[y_rows_of(q, y), :]
    for d in (1, 3, 2):
        send(group_rows, group_rows, wzs.at[d], wzr.at[d], q_peer((q + d) % 4))

    def w_group(step):
        return (q + GROUPS - step) % GROUPS

    def spread(step):
        group = w_group(step)
        rows = weights.at[y_rows_of(group, y), :]

        @pl.when(step > 0)
        def _():
            remote(rows, rows, wzs.at[step], wzr.at[step], z_pair).wait_recv()

        for way in range(2):
            start_copy(rows, rows, wys.at[step, way], wyr.at[step, way], y_peer(steps[way]))

    def pass_on(step):
        group = w_group(step)
        for way in range(2):
            y_of = (y + NY - steps[way]) % NY
            rows = weights.at[y_rows_of(group, y_of), :]
            remote(
                rows, rows, wys.at[step, way], wyr.at[step, way], y_peer(steps[way])
            ).wait_recv()
            half = weights.at[y_half_of(group, y_of, way), :]
            start_copy(half, half, wfs.at[step, way], wfr.at[step, way], y_peer(steps[way]))

    def add_group(step):
        group = w_group(step)
        for way in range(2):
            half = weights.at[y_half_of(group, (y + 2) % NY, way), :]
            remote(
                half, half, wfs.at[step, way], wfr.at[step, way], y_peer(steps[way])
            ).wait_recv()
        rows = pl.ds(pl.multiple_of(group * GROUP_ROWS, GROUP_ROWS), GROUP_ROWS)
        picked_weights = weights[rows, :].T
        sums[:, 0:SIDE] += lax.dot_general(
            picked_weights, turned[rows, 0:SIDE], NN, preferred_element_type=F32
        )
        for r in range(CYCLES_HERE):
            lanes = slice(SIDE + r * 512, SIDE + (r + 1) * 512)
            sums[:, lanes] += lax.dot_general(
                picked_weights, turned[rows, lanes], NN, preferred_element_type=F32
            )

    def weight_step(step, carry):
        pl.when(step < GROUPS)(lambda: spread(step))
        pl.when((step > 0) & (step <= GROUPS))(lambda: pass_on(step - 1))
        pl.when(step > 1)(lambda: add_group(step - 2))
        return carry

    lax.fori_loop(0, GROUPS + 2, weight_step, 0)

    HALF = BLOCK // 2
    parts = (0, 1)
    part_lanes = (slice(0, SIDE + 1024), slice(SIDE + 1024, ROW_WIDTH))
    widths = (SIDE + 1024, 1024)

    def cut(part, buffer, *index):
        return buffer.at[(part, *index, slice(None), slice(0, widths[part]))]

    half_lane = lax.broadcasted_iota(jnp.int32, (HALF, SIDE), 1)

    def rounded(part, total):
        if part == 1:
            return total.astype(BF16)
        whole = total[:, 0:SIDE]
        whole = whole + pltpu.roll(whole, SIDE - CYCLES_HERE, 1)
        high = whole.astype(BF16).astype(F32)
        low = pltpu.roll(whole - high, CYCLES_HERE, 1)
        side = jnp.where(half_lane < CYCLES_HERE, high, jnp.where(half_lane < 2 * CYCLES_HERE, low, 0.0))
        return jnp.concatenate([side, total[:, SIDE:]], axis=1).astype(BF16)

    for part in parts:
        out_buf, in_buf = cut(part, core_out), cut(part, core_in)
        for d in range(NX):
            out_buf[d * BLOCK : (d + 1) * BLOCK, :] = sums[class_rows(d, other), part_lanes[part]]
        send(out_buf, in_buf, cs.at[part], cr.at[part], sibling)

    def core_sum(part, x_to, half):
        start = pl.multiple_of(x_to * BLOCK + half * HALF, HALF)
        return (
            sums[half_rows(x_to, core, half), part_lanes[part]]
            + core_in[part, pl.ds(start, HALF), 0 : widths[part]]
        )

    for part in parts:
        remote(
            cut(part, core_out), cut(part, core_in), cs.at[part], cr.at[part], sibling
        ).wait_recv()
        for way in range(2):
            far = cut(part, xfar_out, way)
            far[...] = rounded(part, core_sum(part, (x + 2) % NX, way))
            send(
                far, cut(part, xfar_in, way), xfs.at[part, way], xfr.at[part, way],
                x_peer(steps[way]),
            )
        for way in range(2):
            near = cut(part, xnear_out, way, 1 - way)
            near[...] = rounded(part, core_sum(part, (x + steps[way]) % NX, 1 - way))
            send(
                near, cut(part, xnear_in, way, 1 - way),
                xns.at[part, way, 1 - way], xnr.at[part, way, 1 - way], x_peer(steps[way]),
            )

    for part in parts:
        for way in range(2):
            far = cut(part, xfar_in, way)
            remote(
                cut(part, xfar_out, way), far, xfs.at[part, way], xfr.at[part, way],
                x_peer(steps[way]),
            ).wait_recv()
            near = cut(part, xnear_out, way, way)
            near[...] = rounded(
                part, core_sum(part, (x + steps[way]) % NX, way) + far[...].astype(F32)
            )
            send(
                near, cut(part, xnear_in, way, way),
                xns.at[part, way, way], xnr.at[part, way, way], x_peer(steps[way]),
            )

    for part in parts:
        for half in range(2):
            total = core_sum(part, x, half)
            for way in range(2):
                near = cut(part, xnear_in, way, half)
                remote(
                    cut(part, xnear_out, way, half), near,
                    xns.at[part, way, half], xnr.at[part, way, half], x_peer(steps[way]),
                ).wait_recv()
                total += near[...].astype(F32)
            out_buf = cut(part, rep_out, half)
            out_buf[...] = rounded(part, total)
            send(
                out_buf, cut(part, rep_via, half),
                p1s.at[part, half], p1r.at[part, half], via[half],
            )

    for part in parts:
        for half in range(2):
            via_buf = cut(part, rep_via, half)
            remote(
                cut(part, rep_out, half), via_buf,
                p1s.at[part, half], p1r.at[part, half], via[half],
            ).wait_recv()
            send(
                via_buf, cut(part, rep_in, half), p2s.at[part, half], p2r.at[part, half], via[half]
            )

    density = None
    for part in parts:
        halves = []
        for half in range(2):
            in_buf = cut(part, rep_in, half)
            remote(
                cut(part, rep_via, half), in_buf,
                p2s.at[part, half], p2r.at[part, half], via[half],
            ).wait_recv()
            halves.append(cut(part, rep_out, half)[...].astype(F32) + in_buf[...].astype(F32))
        total = jnp.concatenate(halves, axis=0)
        if part == 0:
            density = total[:, 0:SIDE]
            total = total[:, SIDE:]
        flipped = []
        for n in range(2):
            r = part * 2 + n
            whole = density[:, r : r + 1] + density[:, r + 4 : r + 5]
            piece = total[:, n * 512 : (n + 1) * 512] / (whole + PRIOR_WEIGHT)
            flipped.append(jnp.concatenate([piece[:, 0:256], -piece[:, 256:512]], axis=1))
        result = dft(jnp.concatenate(flipped, axis=0), high_ref, low_ref)
        for n in range(2):
            for p in range(2):
                for h in range(2):
                    lanes = slice(p * 256 + h * 128, p * 256 + h * 128 + 128)
                    piece = result[n * BLOCK : (n + 1) * BLOCK, lanes]
                    start = (part * 2 + n) * 4 + h * 2 + p
                    padded[pl.ds(start, BLOCK, stride=16), :] = piece if p == 0 else -piece
    out_ref[...] = padded[0 : CLASSES_HERE * 16, :]

    for copy in sent:
        copy.wait_send()

    def drain(step, carry):
        for way in range(2):
            piece = near_out.at[step, way]
            remote(piece, piece, fs.at[step, way], fr.at[step, way], z_pair).wait_send()
            for half in range(2):
                remote(
                    piece, piece, ns.at[step, way, half], nr.at[step, way, half], z_pair
                ).wait_send()
            rows = weights.at[0:Y_ROWS, :]
            remote(rows, rows, wys.at[step, way], wyr.at[step, way], z_pair).wait_send()
            half = weights.at[0:PAIR_ROWS, :]
            remote(half, half, wfs.at[step, way], wfr.at[step, way], z_pair).wait_send()

        @pl.when(step < GROUPS - 1)
        def _():
            remote(z_out.at[step], z_in.at[step], zs.at[step], zr.at[step], z_pair).wait_send()

        return carry

    lax.fori_loop(0, GROUPS, drain, 0)


def to_rows(values):
    count = values.shape[0]
    return values.reshape(count, CYCLES_HERE, 2, 2, 128).transpose(0, 1, 3, 2, 4).reshape(count * 16, 128)


def from_rows(rows):
    return (
        rows.reshape(CLASSES_HERE, CYCLES_HERE, 2, 2, 128)
        .transpose(0, 1, 3, 2, 4)
        .reshape(CLASSES_HERE, CYCLES_HERE, 2, 256)
    )


def per_device(particles, references, ctf_table, defocus_ids, rotation_ids):
    vmem = pl.BlockSpec(memory_space=pltpu.VMEM)
    dma = pltpu.SemaphoreType.DMA
    out = pl.pallas_call(
        body,
        out_shape=jax.ShapeDtypeStruct((CLASSES_HERE * 16, 128), F32),
        in_specs=[pl.BlockSpec(memory_space=pl.ANY)] * 7,
        out_specs=vmem,
        scratch_shapes=[
            pltpu.VMEM((PARTICLES_HERE * 16, 128), F32),
            pltpu.VMEM((CLASSES_HERE * 16, 128), F32),
            pltpu.VMEM((512, 512), F32),
            pltpu.VMEM((ALL_CLASSES, ALL_CLASSES), F32),
            pltpu.VMEM((CYCLES_HERE, DEFOCI), F32),
            pltpu.VMEM((1, PARTICLES_HERE), jnp.int32),
            pltpu.VMEM((1, ANGLES), jnp.int32),
            pltpu.VMEM((512, 512), BF16),
            pltpu.VMEM((512, 512), BF16),
            pltpu.VMEM((ALL_CLASSES, ALL_CLASSES), BF16),
            pltpu.VMEM((DEFOCI, 128), F32),
            pltpu.VMEM((2 * TURN_ROWS, SAMPLES), F32),
            pltpu.VMEM((BLOCK * 16, 128), F32),
            pltpu.VMEM((CYCLES_HERE * PARTICLES_HERE, 512), F32),
            pltpu.VMEM((CYCLES_HERE * BLOCK, 512), F32),
            pltpu.VMEM((ALL_CLASSES, ROW_WIDTH), BF16),
            pltpu.VMEM((PARTICLES_HERE, ROW_WIDTH - SIDE), F32),
            pltpu.VMEM((PARTICLES_HERE, 128), F32),
            pltpu.VMEM((4, PARTICLES_HERE, ALL_CLASSES), F32),
            pltpu.VMEM((ALL_ROWS, ROW_WIDTH), BF16),
            pltpu.VMEM((GROUP_ROWS, ALL_CLASSES), F32),
            pltpu.VMEM((ALL_ROWS, ALL_CLASSES), BF16),
            pltpu.VMEM((GROUPS, 2, PAIR_ROWS, ALL_CLASSES), BF16),
            pltpu.VMEM((GROUPS, 2, 2, PAIR_ROWS, ALL_CLASSES), BF16),
            pltpu.VMEM((GROUPS, 2, PAIR_ROWS, ALL_CLASSES), BF16),
            pltpu.VMEM((GROUPS, Y_ROWS, ALL_CLASSES), BF16),
            pltpu.VMEM((GROUPS - 1, Y_ROWS, ALL_CLASSES), BF16),
            pltpu.VMEM((Y_ROWS, ALL_CLASSES), F32),
            pltpu.VMEM((PAIR_ROWS, ALL_CLASSES), BF16),
            pltpu.VMEM((PAIR_ROWS, ALL_CLASSES), BF16),
            pltpu.VMEM((ALL_ROWS, ALL_CLASSES), BF16),
            pltpu.VMEM((ALL_CLASSES, ROW_WIDTH), F32),
            pltpu.VMEM((2, NX * BLOCK, SIDE + 1024), F32),
            pltpu.VMEM((2, NX * BLOCK, SIDE + 1024), F32),
            pltpu.VMEM((2, 2, BLOCK // 2, SIDE + 1024), BF16),
            pltpu.VMEM((2, 2, BLOCK // 2, SIDE + 1024), BF16),
            pltpu.VMEM((2, 2, 2, BLOCK // 2, SIDE + 1024), BF16),
            pltpu.VMEM((2, 2, 2, BLOCK // 2, SIDE + 1024), BF16),
            pltpu.VMEM((2, 2, BLOCK // 2, SIDE + 1024), BF16),
            pltpu.VMEM((2, 2, BLOCK // 2, SIDE + 1024), BF16),
            pltpu.VMEM((2, 2, BLOCK // 2, SIDE + 1024), BF16),
            dma((7,)),
            dma((2,)), dma((2,)), dma((2,)), dma((2,)),
            dma((NX,)), dma((NX,)),
            dma((GROUPS, 2)), dma((GROUPS, 2)),
            dma((GROUPS, 2, 2)), dma((GROUPS, 2, 2)),
            dma((GROUPS - 1,)), dma((GROUPS - 1,)),
            dma(()), dma(()), dma(()), dma(()),
            dma((GROUPS,)), dma((GROUPS,)),
            dma((GROUPS, 2)), dma((GROUPS, 2)),
            dma((GROUPS, 2)), dma((GROUPS, 2)),
            dma((2,)), dma((2,)),
            dma((2, 2)), dma((2, 2)),
            dma((2, 2, 2)), dma((2, 2, 2)),
            dma((2, 2)), dma((2, 2)), dma((2, 2)), dma((2, 2)),
        ],
        compiler_params=pltpu.CompilerParams(
            collective_id=0, has_side_effects=True, vmem_limit_bytes=56 * 1024 * 1024
        ),
    )(
        to_rows(particles), to_rows(references), jnp.asarray(dft_matrix()), jnp.asarray(walsh_matrix()),
        ctf_table.T, defocus_ids.reshape(1, PARTICLES_HERE), rotation_ids.reshape(1, ANGLES),
    )
    return from_rows(out)


def solution(mesh):
    in_specs = (
        P(("cls", "rep"), "pix", None, None),
        P("cls", "pix", None, None),
        P(None, "pix"),
        P(("cls", "rep")),
        P(),
    )
    out_specs = P("cls", "pix", None, None)
    return jax.shard_map(
        per_device, mesh=mesh, in_specs=in_specs, out_specs=out_specs, check_vma=False
    )
```

```python
import math

import jax
import jax.numpy as jnp
import numpy as np
from jax import lax
from jax.experimental import pallas as pl
from jax.experimental.pallas import tpu as pltpu
from jax.sharding import PartitionSpec as P

TURN_STEPS = 360
DEFOCI = 16
EPSILON = 1e-06
SHARPNESS = 30.0
PRIOR_WEIGHT = 1.0

F32 = jnp.float32
BF16 = jnp.bfloat16
MESH = pl.DeviceIdType.MESH

SAMPLES = 256
ANGLES = 36
TURN_ROWS = 40
PAIR_ROWS = 2 * TURN_ROWS
PARTICLES_HERE = 64
CYCLES_HERE = 4
CLASSES_HERE = 25
BLOCK = 32
NX, NY, NZ = 4, 4, 8
ALL_CLASSES = 2 * NX * BLOCK
SIDE = 128
ROW_WIDTH = SIDE + CYCLES_HERE * 2 * SAMPLES
GROUPS = 4
Y_ROWS = 2 * PAIR_ROWS
GROUP_ROWS = NY * Y_ROWS
ALL_ROWS = GROUPS * GROUP_ROWS

NN = (((1,), (0,)), ((), ()))
NT = (((1,), (1,)), ((), ()))
TN = (((0,), (0,)), ((), ()))


def dft_matrix():
    positions = np.arange(SAMPLES)
    radians = (positions[:, None] * positions[None, :] % SAMPLES) * (2.0 * math.pi / SAMPLES)
    cosine = np.cos(radians) / math.sqrt(SAMPLES)
    sine = np.sin(radians) / math.sqrt(SAMPLES)
    return np.block([[cosine, -sine], [sine, cosine]]).astype(np.float32)


def walsh_matrix():
    matrix = np.ones((1, 1), np.float32)
    while matrix.shape[0] < ALL_CLASSES:
        matrix = np.block([[matrix, matrix], [matrix, -matrix]])
    return matrix


def split(values):
    high = values.astype(BF16)
    return high, (values - high.astype(F32)).astype(BF16)


def walsh(values, walsh_ref):
    high, low = split(values)
    return lax.dot_general(high, walsh_ref[...], NN, preferred_element_type=F32) + lax.dot_general(
        low, walsh_ref[...], NN, preferred_element_type=F32
    )


def dft(values, high_ref, low_ref):
    high, low = split(values)
    return (
        lax.dot_general(high, high_ref[...], NN, preferred_element_type=F32)
        + lax.dot_general(low, high_ref[...], NN, preferred_element_type=F32)
        + lax.dot_general(high, low_ref[...], NN, preferred_element_type=F32)
    )


def body(
    x_hbm, r_hbm, dft_hbm, walsh_hbm, ctf_hbm, ids_hbm, turns_hbm, out_ref,
    x_ref, r_ref, dft_ref, walsh_f, ctf_in, ids_ref, turns_ref,
    high_ref, low_ref, walsh_ref, ctf_ref, phase_ref,
    padded, x_rows, r_rows, spectra, weighted, power_rows, norm_rows, turned,
    partial_f, partial, far_in, near_in, near_out, z_out, z_in, pair_out, pair_in, weights,
    sums, core_out, core_in, xfar_out, xfar_in, xnear_out, xnear_in, rep_out, rep_via, rep_in,
    in_sem, rx_s, rx_r, rf_s, rf_r, rc_s, rc_r,
    fs, fr, ns, nr, zs, zr, zps, zpr, wzs, wzr, wys, wyr, wfs, wfr,
    cs, cr, xfs, xfr, xns, xnr, p1s, p1r, p2s, p2r,
):
    loads = [
        pltpu.make_async_copy(src, dst, in_sem.at[n])
        for n, (src, dst) in enumerate(
            [
                (r_hbm, r_ref), (dft_hbm, dft_ref), (x_hbm, x_ref), (ids_hbm, ids_ref),
                (turns_hbm, turns_ref), (ctf_hbm, ctf_in), (walsh_hbm, walsh_f),
            ]
        )
    ]
    for load in loads:
        load.start()
    cls = lax.axis_index("cls")
    pix = lax.axis_index("pix")
    rep = lax.axis_index("rep")
    x, core = cls // 2, cls % 2
    z, y = pix // NY, pix % NY
    other = 1 - core
    sibling = {"cls": x * 2 + other}

    def x_peer(d):
        return {"cls": (x + d) % NX * 2 + core}

    def y_peer(d):
        return {"pix": z * NY + (y + d) % NY}

    q, zh = z % 4, z // 4

    def q_peer(q_to):
        return {"pix": (zh * 4 + q_to) * NY + y}

    z_pair = {"pix": (z + 4) % NZ * NY + y}

    far_z = (z + 4) % NZ
    up = (z + 4) // NZ
    via = (
        {"pix": far_z * NY + y, "rep": (rep + up) % 2},
        {"pix": far_z * NY + y, "rep": (rep + 1 - up) % 2},
    )
    partners = (
        [sibling, {"pix": far_z * NY + y, "rep": 1 - rep}]
        + [x_peer(d) for d in (1, 3)]
        + [y_peer(d) for d in (1, 3)]
        + [q_peer((q + d) % 4) for d in range(1, 4)]
        + [z_pair]
    )

    def remote(src, dst, send, recv, device):
        return pltpu.make_async_remote_copy(
            src_ref=src, dst_ref=dst, send_sem=send, recv_sem=recv,
            device_id=device, device_id_type=MESH,
        )

    sent = []

    def start_copy(*args):
        remote(*args).start()

    def send(*args):
        copy = remote(*args)
        copy.start()
        sent.append(copy)

    barrier = pltpu.get_barrier_semaphore()
    for partner in partners:
        pl.semaphore_signal(barrier, inc=1, device_id=partner, device_id_type=MESH)

    loads[0].wait()
    loads[1].wait()
    high, low = split(dft_ref[...])
    high_ref[...] = high
    low_ref[...] = low
    padded[...] = jnp.zeros_like(padded)
    padded[0 : CLASSES_HERE * 16, :] = r_ref[...]
    for r in range(CYCLES_HERE):
        for p in range(2):
            for h in range(2):
                r_rows[r * BLOCK : (r + 1) * BLOCK, p * 256 + h * 128 : p * 256 + h * 128 + 128] = padded[
                    pl.ds(r * 4 + h * 2 + p, BLOCK, stride=16), :
                ]
    own = dft(r_rows[...], high_ref, low_ref).astype(BF16)
    own_rows = pl.ds(pl.multiple_of(cls * BLOCK, BLOCK), BLOCK)
    wide = own.astype(F32)
    power = jnp.sum(wide * wide, axis=1, keepdims=True)
    power_high, power_low = split(power)
    side_lane = lax.broadcasted_iota(jnp.int32, (BLOCK, SIDE), 1)
    side = jnp.zeros((BLOCK, SIDE), F32)
    for r in range(CYCLES_HERE):
        rows = slice(r * BLOCK, (r + 1) * BLOCK)
        spectra[own_rows, SIDE + r * 512 : SIDE + (r + 1) * 512] = own[rows, :]
        side = jnp.where(side_lane == r, power_high.astype(F32)[rows, :], side)
        side = jnp.where(side_lane == CYCLES_HERE + r, power_low.astype(F32)[rows, :], side)
    spectra[own_rows, 0:SIDE] = side.astype(BF16)

    pl.semaphore_wait(barrier, len(partners))
    steps = (1, 3)
    for way in range(2):
        send(
            spectra.at[own_rows, :], spectra.at[own_rows, :],
            rx_s.at[way], rx_r.at[way], x_peer(steps[way]),
        )
    send(spectra.at[own_rows, :], spectra.at[own_rows, :], rc_s.at[0], rc_r.at[0], sibling)

    def class_rows(x_of, core_of):
        return pl.ds(pl.multiple_of((x_of * 2 + core_of) * BLOCK, BLOCK), BLOCK)

    def half_rows(x_of, core_of, half):
        start = (x_of * 2 + core_of) * BLOCK + half * (BLOCK // 2)
        return pl.ds(pl.multiple_of(start, BLOCK // 2), BLOCK // 2)

    for load in loads[2:]:
        load.wait()
    walsh_ref[...] = walsh_f[...].astype(BF16)
    select = (
        lax.broadcasted_iota(jnp.int32, (CYCLES_HERE, 128), 1)
        - lax.broadcasted_iota(jnp.int32, (CYCLES_HERE, 128), 0)
    )
    select = ((select == 0) | (select == CYCLES_HERE)).astype(F32)
    ctf_ref[...] = lax.dot_general(
        ctf_in[...], select, TN, precision=lax.Precision.HIGHEST, preferred_element_type=F32
    )
    shape = (TURN_ROWS, ANGLES)
    on_row = lax.broadcasted_iota(jnp.int32, shape, 0) == lax.broadcasted_iota(jnp.int32, shape, 1)
    turns = jnp.sum(
        jnp.where(on_row, jnp.broadcast_to(turns_ref[...].astype(F32), shape), 0.0),
        axis=1, keepdims=True,
    )
    place = lax.broadcasted_iota(jnp.int32, (TURN_ROWS, SAMPLES), 1)
    signed = jnp.where(place < SAMPLES // 2, place, place - SAMPLES).astype(F32)
    count = turns * signed
    count = count - TURN_STEPS * jnp.floor(count * (1.0 / TURN_STEPS))
    count = jnp.where(count < 0, count + TURN_STEPS, count)
    count = jnp.where(count >= TURN_STEPS, count - TURN_STEPS, count)
    radians = count * (2.0 * math.pi / TURN_STEPS)
    phase_ref[0:TURN_ROWS, :] = jnp.cos(radians)
    phase_ref[TURN_ROWS : 2 * TURN_ROWS, :] = jnp.sin(radians)

    for r in range(CYCLES_HERE):
        for p in range(2):
            for h in range(2):
                x_rows[r * 64 : (r + 1) * 64, p * 256 + h * 128 : p * 256 + h * 128 + 128] = x_ref[
                    pl.ds(r * 4 + h * 2 + p, PARTICLES_HERE, stride=16), :
                ]
    part_square = jnp.zeros((PARTICLES_HERE, 128), F32)
    for r in range(CYCLES_HERE):
        for h in range(4):
            piece = x_rows[r * 64 : (r + 1) * 64, h * 128 : (h + 1) * 128]
            part_square += piece * piece
    part_norm = jnp.sum(part_square, axis=1, keepdims=True)
    picks = (
        lax.broadcasted_iota(jnp.int32, (DEFOCI, PARTICLES_HERE), 0) == ids_ref[...]
    ).astype(F32)
    ctf_rows = lax.dot_general(
        picks, ctf_ref[...], TN, precision=lax.Precision.HIGHEST, preferred_element_type=F32
    )
    particle_spectra = dft(x_rows[...], high_ref, low_ref)
    for r in range(CYCLES_HERE):
        weighted[:, r * 512 : (r + 1) * 512] = (
            ctf_rows[:, r : r + 1] * particle_spectra[r * 64 : (r + 1) * 64, :]
        )
    squared = ctf_rows * ctf_rows
    square_high = squared.astype(BF16).astype(F32)
    lane = lax.broadcasted_iota(jnp.int32, squared.shape, 1)
    power_rows[...] = jnp.where(lane < CYCLES_HERE, square_high, squared - square_high)

    for way in range(2):
        x_of = (x + NX - steps[way]) % NX
        rows = spectra.at[class_rows(x_of, core), :]
        remote(rows, rows, rx_s.at[way], rx_r.at[way], x_peer(steps[way])).wait_recv()
        half = spectra.at[half_rows(x_of, core, way), :]
        send(half, half, rf_s.at[way], rf_r.at[way], x_peer(steps[way]))
        send(rows, rows, rc_s.at[way + 1], rc_r.at[way + 1], sibling)

    cosine = phase_ref[0:TURN_ROWS, :]
    sine = phase_ref[TURN_ROWS : 2 * TURN_ROWS, :]

    def turn_pair(pair, carry):
        rows = pl.ds(pl.multiple_of(pair * PAIR_ROWS, 16), PAIR_ROWS)
        for r in range(CYCLES_HERE):
            real, imag = [], []
            for e in range(2):
                w_re = weighted[pl.ds(pair * 2 + e, 1), r * 512 : r * 512 + 256]
                w_im = weighted[pl.ds(pair * 2 + e, 1), r * 512 + 256 : r * 512 + 512]
                real.append(w_re * cosine - w_im * sine)
                imag.append(w_re * sine + w_im * cosine)
            start = SIDE + r * 512
            turned[rows, start : start + 256] = jnp.concatenate(real, axis=0).astype(BF16)
            turned[rows, start + 256 : start + 512] = jnp.concatenate(imag, axis=0).astype(BF16)
        tail = [
            jnp.broadcast_to(power_rows[pl.ds(pair * 2 + e, 1), :], (TURN_ROWS, 128)) for e in range(2)
        ]
        turned[rows, 0:SIDE] = jnp.concatenate(tail, axis=0).astype(BF16)
        return carry

    lax.fori_loop(0, PARTICLES_HERE // 4, turn_pair, 0)
    x_far = (x + 2) % NX
    for way in range(2):
        half = spectra.at[half_rows(x_far, core, way), :]
        remote(half, half, rf_s.at[way], rf_r.at[way], x_peer(steps[way])).wait_recv()
    rows = spectra.at[class_rows(x_far, core), :]
    send(rows, rows, rc_s.at[3], rc_r.at[3], sibling)
    lax.fori_loop(PARTICLES_HERE // 4, PARTICLES_HERE // 2, turn_pair, 0)

    for n, x_of in enumerate((x, (x + 3) % NX, (x + 1) % NX, x_far)):
        rows = spectra.at[class_rows(x_of, other), :]
        remote(rows, rows, rc_s.at[n], rc_r.at[n], sibling).wait_recv()

    ctf_high, ctf_low = split(ctf_ref[...] * ctf_ref[...])
    ref_norm = lax.dot_general(
        ctf_high, spectra[:, 0:SIDE], NT, preferred_element_type=F32
    ) + lax.dot_general(ctf_low, spectra[:, 0:SIDE], NT, preferred_element_type=F32)
    picked = lax.dot_general(
        picks, ref_norm, TN, precision=lax.Precision.HIGHEST, preferred_element_type=F32
    )
    picked_high = picked.astype(BF16).astype(F32)
    wide_norm = jnp.broadcast_to(part_norm, (PARTICLES_HERE, ALL_CLASSES))
    wide_high = wide_norm.astype(BF16).astype(F32)
    norm_rows[0] = picked_high
    norm_rows[1] = picked - picked_high
    norm_rows[2] = wide_high
    norm_rows[3] = wide_norm - wide_high
    sub = lax.broadcasted_iota(jnp.int32, (8, ALL_CLASSES), 0)

    def z_group(step):
        return (q + 1 + step) % GROUPS

    def y_rows_of(group, y_to):
        return pl.ds(pl.multiple_of(group * GROUP_ROWS + y_to * Y_ROWS, Y_ROWS), Y_ROWS)

    def y_half_of(group, y_to, half):
        start = group * GROUP_ROWS + y_to * Y_ROWS + half * PAIR_ROWS
        return pl.ds(pl.multiple_of(start, PAIR_ROWS), PAIR_ROWS)

    def correlate(step):
        group = z_group(step)
        rows = pl.ds(pl.multiple_of(group * GROUP_ROWS, GROUP_ROWS), GROUP_ROWS)
        partial_f[...] = walsh(
            lax.dot_general(turned[rows, SIDE:], spectra[:, SIDE:], NT, preferred_element_type=F32), walsh_ref
        )

        def patch(pair, carry):
            pieces = []
            for e in range(2):
                start = pl.multiple_of(pair * PAIR_ROWS + e * TURN_ROWS, 8)
                pieces.append(partial_f[pl.ds(start, 32), :])
                last = partial_f[pl.ds(start + 32, 8), :]
                particle = group * 16 + pair * 2 + e
                for n in range(4):
                    last = jnp.where(sub == 4 + n, norm_rows[n, pl.ds(particle, 1), :], last)
                pieces.append(last)
            start = pl.multiple_of(group * GROUP_ROWS + pair * PAIR_ROWS, 16)
            partial[pl.ds(start, PAIR_ROWS), :] = jnp.concatenate(pieces, axis=0).astype(BF16)
            return carry

        lax.fori_loop(0, NY * 2, patch, 0)
        for way in range(2):
            start_copy(
                partial.at[y_half_of(group, (y + 2) % NY, way), :],
                far_in.at[step, way], fs.at[step, way], fr.at[step, way], y_peer(steps[way]),
            )
        for way in range(2):
            start_copy(
                partial.at[y_half_of(group, (y + steps[way]) % NY, 1 - way), :],
                near_in.at[step, way, 1 - way],
                ns.at[step, way, 1 - way], nr.at[step, way, 1 - way], y_peer(steps[way]),
            )

    odd_row = sub % 2 == 1

    def product_rounded(total):
        pieces = []
        for e in range(2):
            start = e * TURN_ROWS
            pieces.append(total[start : start + 32, :])
            last = total[start + 32 : start + 40, :]
            whole = last + pltpu.roll(last, 7, 0)
            high = whole.astype(BF16).astype(F32)
            low = pltpu.roll(whole - high, 1, 0)
            pieces.append(jnp.where(sub < 4, last, jnp.where(odd_row, low, high)))
        return jnp.concatenate(pieces, axis=0).astype(BF16)

    def relay(step):
        group = z_group(step)
        for way in range(2):
            own = partial.at[y_half_of(group, (y + steps[way]) % NY, way), :]
            remote(
                own, far_in.at[step, way], fs.at[step, way], fr.at[step, way], y_peer(steps[way])
            ).wait_recv()
            near_out[step, way] = product_rounded(
                own[...].astype(F32) + far_in[step, way].astype(F32)
            )
            start_copy(
                near_out.at[step, way], near_in.at[step, way, way],
                ns.at[step, way, way], nr.at[step, way, way], y_peer(steps[way]),
            )

    def reduce_y(step):
        group = z_group(step)
        for half in range(2):
            own = partial.at[y_half_of(group, y, half), :]
            total = own[...].astype(F32)
            for way in range(2):
                remote(
                    own, near_in.at[step, way, half],
                    ns.at[step, way, half], nr.at[step, way, half], y_peer(steps[way]),
                ).wait_recv()
                total += near_in[step, way, half].astype(F32)
            z_out[step, half * PAIR_ROWS : (half + 1) * PAIR_ROWS, :] = product_rounded(total)

        @pl.when(step < GROUPS - 1)
        def _():
            start_copy(
                z_out.at[step], z_in.at[step], zs.at[step], zr.at[step], q_peer(group)
            )

    def product_step(step, carry):
        pl.when(step < GROUPS)(lambda: correlate(step))
        pl.when((step > 0) & (step <= GROUPS))(lambda: relay(step - 1))
        pl.when(step > 1)(lambda: reduce_y(step - 2))
        return carry

    lax.fori_loop(0, GROUPS + 2, product_step, 0)

    total = z_out[GROUPS - 1].astype(F32)
    for n in range(GROUPS - 1):
        remote(z_out.at[n], z_in.at[n], zs.at[n], zr.at[n], z_pair).wait_recv()
        total += z_in[n].astype(F32)
    for half in range(2):
        rows = slice(half * PAIR_ROWS, (half + 1) * PAIR_ROWS)
        pair_out[rows, :] = product_rounded(total[rows, :])
    send(pair_out, pair_in, zps, zpr, z_pair)
    sums[...] = jnp.zeros_like(sums)
    remote(pair_out, pair_in, zps, zpr, z_pair).wait_recv()
    mine = total + pair_in[...].astype(F32)

    shape = (TURN_ROWS, ALL_CLASSES)
    valid = (lax.broadcasted_iota(jnp.int32, shape, 0) < ANGLES) & (
        lax.broadcasted_iota(jnp.int32, shape, 1) % BLOCK < CLASSES_HERE
    )
    products = walsh(mine, walsh_ref) * (1.0 / ALL_CLASSES)
    pieces = []
    for e in range(4):
        rows = mine[e * TURN_ROWS : (e + 1) * TURN_ROWS, :]
        ref_row = rows[36:37, :] + rows[37:38, :]
        part_row = rows[38:39, :] + rows[39:40, :]
        scaling = lax.rsqrt(part_row + EPSILON) * lax.rsqrt(ref_row + EPSILON)
        scores = jnp.where(
            valid, SHARPNESS * products[e * TURN_ROWS : (e + 1) * TURN_ROWS, :] * scaling, 0.0
        )
        raised = jnp.where(valid, jnp.exp(scores), 0.0)
        total = jnp.sum(jnp.sum(raised, axis=0, keepdims=True), axis=1, keepdims=True)
        pieces.append(raised / total)

    group_rows = weights.at[y_rows_of(q, y), :]
    group_rows[...] = jnp.concatenate(pieces, axis=0).astype(BF16)
    for d in (1, 3, 2):
        send(group_rows, group_rows, wzs.at[d], wzr.at[d], q_peer((q + d) % 4))

    def w_group(step):
        return (q + GROUPS - step) % GROUPS

    def spread(step):
        group = w_group(step)
        rows = weights.at[y_rows_of(group, y), :]

        @pl.when(step > 0)
        def _():
            remote(rows, rows, wzs.at[step], wzr.at[step], z_pair).wait_recv()

        for way in range(2):
            start_copy(rows, rows, wys.at[step, way], wyr.at[step, way], y_peer(steps[way]))

    def pass_on(step):
        group = w_group(step)
        for way in range(2):
            y_of = (y + NY - steps[way]) % NY
            rows = weights.at[y_rows_of(group, y_of), :]
            remote(
                rows, rows, wys.at[step, way], wyr.at[step, way], y_peer(steps[way])
            ).wait_recv()
            half = weights.at[y_half_of(group, y_of, way), :]
            start_copy(half, half, wfs.at[step, way], wfr.at[step, way], y_peer(steps[way]))

    def add_group(step):
        group = w_group(step)
        for way in range(2):
            half = weights.at[y_half_of(group, (y + 2) % NY, way), :]
            remote(
                half, half, wfs.at[step, way], wfr.at[step, way], y_peer(steps[way])
            ).wait_recv()
        rows = pl.ds(pl.multiple_of(group * GROUP_ROWS, GROUP_ROWS), GROUP_ROWS)
        picked_weights = weights[rows, :].T
        sums[:, 0:SIDE] += lax.dot_general(
            picked_weights, turned[rows, 0:SIDE], NN, preferred_element_type=F32
        )
        for r in range(CYCLES_HERE):
            lanes = slice(SIDE + r * 512, SIDE + (r + 1) * 512)
            sums[:, lanes] += lax.dot_general(
                picked_weights, turned[rows, lanes], NN, preferred_element_type=F32
            )

    def weight_step(step, carry):
        pl.when(step < GROUPS)(lambda: spread(step))
        pl.when((step > 0) & (step <= GROUPS))(lambda: pass_on(step - 1))
        pl.when(step > 1)(lambda: add_group(step - 2))
        return carry

    lax.fori_loop(0, GROUPS + 2, weight_step, 0)

    HALF = BLOCK // 2
    parts = (0, 1)
    part_lanes = (slice(0, SIDE + 1024), slice(SIDE + 1024, ROW_WIDTH))
    widths = (SIDE + 1024, 1024)

    def cut(part, buffer, *index):
        return buffer.at[(part, *index, slice(None), slice(0, widths[part]))]

    def rounded(part, total):
        if part == 1:
            return total.astype(BF16)
        whole = total[:, 0:SIDE]
        half_lane = lax.broadcasted_iota(jnp.int32, whole.shape, 1)
        whole = whole + pltpu.roll(whole, SIDE - CYCLES_HERE, 1)
        high = whole.astype(BF16).astype(F32)
        low = pltpu.roll(whole - high, CYCLES_HERE, 1)
        side = jnp.where(half_lane < CYCLES_HERE, high, jnp.where(half_lane < 2 * CYCLES_HERE, low, 0.0))
        return jnp.concatenate([side, total[:, SIDE:]], axis=1).astype(BF16)

    for part in parts:
        out_buf, in_buf = cut(part, core_out), cut(part, core_in)
        for d in range(NX):
            out_buf[d * BLOCK : (d + 1) * BLOCK, :] = rounded(
                part, sums[class_rows(d, other), part_lanes[part]]
            )
        send(out_buf, in_buf, cs.at[part], cr.at[part], sibling)

    def core_sum(part, x_to, half):
        start = pl.multiple_of(x_to * BLOCK + half * HALF, HALF)
        return (
            sums[half_rows(x_to, core, half), part_lanes[part]]
            + core_in[part, pl.ds(start, HALF), 0 : widths[part]].astype(F32)
        )

    for part in parts:
        remote(
            cut(part, core_out), cut(part, core_in), cs.at[part], cr.at[part], sibling
        ).wait_recv()
        for way in range(2):
            far = cut(part, xfar_out, way)
            far[...] = rounded(part, core_sum(part, (x + 2) % NX, way))
            send(
                far, cut(part, xfar_in, way), xfs.at[part, way], xfr.at[part, way],
                x_peer(steps[way]),
            )
        for way in range(2):
            near = cut(part, xnear_out, way, 1 - way)
            near[...] = rounded(part, core_sum(part, (x + steps[way]) % NX, 1 - way))
            send(
                near, cut(part, xnear_in, way, 1 - way),
                xns.at[part, way, 1 - way], xnr.at[part, way, 1 - way], x_peer(steps[way]),
            )

    for part in parts:
        for way in range(2):
            far = cut(part, xfar_in, way)
            remote(
                cut(part, xfar_out, way), far, xfs.at[part, way], xfr.at[part, way],
                x_peer(steps[way]),
            ).wait_recv()
            near = cut(part, xnear_out, way, way)
            near[...] = rounded(
                part, core_sum(part, (x + steps[way]) % NX, way) + far[...].astype(F32)
            )
            send(
                near, cut(part, xnear_in, way, way),
                xns.at[part, way, way], xnr.at[part, way, way], x_peer(steps[way]),
            )

    for part in parts:
        for half in range(2):
            total = core_sum(part, x, half)
            for way in range(2):
                near = cut(part, xnear_in, way, half)
                remote(
                    cut(part, xnear_out, way, half), near,
                    xns.at[part, way, half], xnr.at[part, way, half], x_peer(steps[way]),
                ).wait_recv()
                total += near[...].astype(F32)
            out_buf = cut(part, rep_out, half)
            out_buf[...] = rounded(part, total)
            send(
                out_buf, cut(part, rep_via, half),
                p1s.at[part, half], p1r.at[part, half], via[half],
            )

    for part in parts:
        for half in range(2):
            via_buf = cut(part, rep_via, half)
            remote(
                cut(part, rep_out, half), via_buf,
                p1s.at[part, half], p1r.at[part, half], via[half],
            ).wait_recv()
            send(
                via_buf, cut(part, rep_in, half), p2s.at[part, half], p2r.at[part, half], via[half]
            )

    density = None
    for part in parts:
        halves = []
        for half in range(2):
            in_buf = cut(part, rep_in, half)
            remote(
                cut(part, rep_via, half), in_buf,
                p2s.at[part, half], p2r.at[part, half], via[half],
            ).wait_recv()
            halves.append(cut(part, rep_out, half)[...].astype(F32) + in_buf[...].astype(F32))
        total = jnp.concatenate(halves, axis=0)
        if part == 0:
            density = total[:, 0:SIDE]
            total = total[:, SIDE:]
        flipped = []
        for n in range(2):
            r = part * 2 + n
            whole = density[:, r : r + 1] + density[:, r + 4 : r + 5]
            piece = total[:, n * 512 : (n + 1) * 512] / (whole + PRIOR_WEIGHT)
            flipped.append(jnp.concatenate([piece[:, 0:256], -piece[:, 256:512]], axis=1))
        result = dft(jnp.concatenate(flipped, axis=0), high_ref, low_ref)
        for n in range(2):
            for p in range(2):
                for h in range(2):
                    lanes = slice(p * 256 + h * 128, p * 256 + h * 128 + 128)
                    piece = result[n * BLOCK : (n + 1) * BLOCK, lanes]
                    start = (part * 2 + n) * 4 + h * 2 + p
                    padded[pl.ds(start, BLOCK, stride=16), :] = piece if p == 0 else -piece
    out_ref[...] = padded[0 : CLASSES_HERE * 16, :]

    for copy in sent:
        copy.wait_send()

    def drain(step, carry):
        for way in range(2):
            piece = near_out.at[step, way]
            remote(piece, piece, fs.at[step, way], fr.at[step, way], z_pair).wait_send()
            for half in range(2):
                remote(
                    piece, piece, ns.at[step, way, half], nr.at[step, way, half], z_pair
                ).wait_send()
            rows = weights.at[0:Y_ROWS, :]
            remote(rows, rows, wys.at[step, way], wyr.at[step, way], z_pair).wait_send()
            half = weights.at[0:PAIR_ROWS, :]
            remote(half, half, wfs.at[step, way], wfr.at[step, way], z_pair).wait_send()

        @pl.when(step < GROUPS - 1)
        def _():
            remote(z_out.at[step], z_in.at[step], zs.at[step], zr.at[step], z_pair).wait_send()

        return carry

    lax.fori_loop(0, GROUPS, drain, 0)


def to_rows(values):
    count = values.shape[0]
    return values.reshape(count, CYCLES_HERE, 2, 2, 128).transpose(0, 1, 3, 2, 4).reshape(count * 16, 128)


def from_rows(rows):
    return (
        rows.reshape(CLASSES_HERE, CYCLES_HERE, 2, 2, 128)
        .transpose(0, 1, 3, 2, 4)
        .reshape(CLASSES_HERE, CYCLES_HERE, 2, 256)
    )


def per_device(particles, references, ctf_table, defocus_ids, rotation_ids):
    vmem = pl.BlockSpec(memory_space=pltpu.VMEM)
    dma = pltpu.SemaphoreType.DMA
    out = pl.pallas_call(
        body,
        out_shape=jax.ShapeDtypeStruct((CLASSES_HERE * 16, 128), F32),
        in_specs=[pl.BlockSpec(memory_space=pl.ANY)] * 7,
        out_specs=vmem,
        scratch_shapes=[
            pltpu.VMEM((PARTICLES_HERE * 16, 128), F32),
            pltpu.VMEM((CLASSES_HERE * 16, 128), F32),
            pltpu.VMEM((512, 512), F32),
            pltpu.VMEM((ALL_CLASSES, ALL_CLASSES), F32),
            pltpu.VMEM((CYCLES_HERE, DEFOCI), F32),
            pltpu.VMEM((1, PARTICLES_HERE), jnp.int32),
            pltpu.VMEM((1, ANGLES), jnp.int32),
            pltpu.VMEM((512, 512), BF16),
            pltpu.VMEM((512, 512), BF16),
            pltpu.VMEM((ALL_CLASSES, ALL_CLASSES), BF16),
            pltpu.VMEM((DEFOCI, 128), F32),
            pltpu.VMEM((2 * TURN_ROWS, SAMPLES), F32),
            pltpu.VMEM((BLOCK * 16, 128), F32),
            pltpu.VMEM((CYCLES_HERE * PARTICLES_HERE, 512), F32),
            pltpu.VMEM((CYCLES_HERE * BLOCK, 512), F32),
            pltpu.VMEM((ALL_CLASSES, ROW_WIDTH), BF16),
            pltpu.VMEM((PARTICLES_HERE, ROW_WIDTH - SIDE), F32),
            pltpu.VMEM((PARTICLES_HERE, 128), F32),
            pltpu.VMEM((4, PARTICLES_HERE, ALL_CLASSES), F32),
            pltpu.VMEM((ALL_ROWS, ROW_WIDTH), BF16),
            pltpu.VMEM((GROUP_ROWS, ALL_CLASSES), F32),
            pltpu.VMEM((ALL_ROWS, ALL_CLASSES), BF16),
            pltpu.VMEM((GROUPS, 2, PAIR_ROWS, ALL_CLASSES), BF16),
            pltpu.VMEM((GROUPS, 2, 2, PAIR_ROWS, ALL_CLASSES), BF16),
            pltpu.VMEM((GROUPS, 2, PAIR_ROWS, ALL_CLASSES), BF16),
            pltpu.VMEM((GROUPS, Y_ROWS, ALL_CLASSES), BF16),
            pltpu.VMEM((GROUPS - 1, Y_ROWS, ALL_CLASSES), BF16),
            pltpu.VMEM((Y_ROWS, ALL_CLASSES), BF16),
            pltpu.VMEM((Y_ROWS, ALL_CLASSES), BF16),
            pltpu.VMEM((ALL_ROWS, ALL_CLASSES), BF16),
            pltpu.VMEM((ALL_CLASSES, ROW_WIDTH), F32),
            pltpu.VMEM((2, NX * BLOCK, SIDE + 1024), BF16),
            pltpu.VMEM((2, NX * BLOCK, SIDE + 1024), BF16),
            pltpu.VMEM((2, 2, BLOCK // 2, SIDE + 1024), BF16),
            pltpu.VMEM((2, 2, BLOCK // 2, SIDE + 1024), BF16),
            pltpu.VMEM((2, 2, 2, BLOCK // 2, SIDE + 1024), BF16),
            pltpu.VMEM((2, 2, 2, BLOCK // 2, SIDE + 1024), BF16),
            pltpu.VMEM((2, 2, BLOCK // 2, SIDE + 1024), BF16),
            pltpu.VMEM((2, 2, BLOCK // 2, SIDE + 1024), BF16),
            pltpu.VMEM((2, 2, BLOCK // 2, SIDE + 1024), BF16),
            dma((7,)),
            dma((2,)), dma((2,)), dma((2,)), dma((2,)),
            dma((NX,)), dma((NX,)),
            dma((GROUPS, 2)), dma((GROUPS, 2)),
            dma((GROUPS, 2, 2)), dma((GROUPS, 2, 2)),
            dma((GROUPS - 1,)), dma((GROUPS - 1,)),
            dma(()), dma(()),
            dma((GROUPS,)), dma((GROUPS,)),
            dma((GROUPS, 2)), dma((GROUPS, 2)),
            dma((GROUPS, 2)), dma((GROUPS, 2)),
            dma((2,)), dma((2,)),
            dma((2, 2)), dma((2, 2)),
            dma((2, 2, 2)), dma((2, 2, 2)),
            dma((2, 2)), dma((2, 2)), dma((2, 2)), dma((2, 2)),
        ],
        compiler_params=pltpu.CompilerParams(
            collective_id=0, has_side_effects=True, vmem_limit_bytes=56 * 1024 * 1024
        ),
    )(
        to_rows(particles), to_rows(references), jnp.asarray(dft_matrix()), jnp.asarray(walsh_matrix()),
        ctf_table.T, defocus_ids.reshape(1, PARTICLES_HERE), rotation_ids.reshape(1, ANGLES),
    )
    return from_rows(out)


def solution(mesh):
    in_specs = (
        P(("cls", "rep"), "pix", None, None),
        P("cls", "pix", None, None),
        P(None, "pix"),
        P(("cls", "rep")),
        P(),
    )
    out_specs = P("cls", "pix", None, None)
    return jax.shard_map(
        per_device, mesh=mesh, in_specs=in_specs, out_specs=out_specs, check_vma=False
    )
```

```python
import math

import jax
import jax.numpy as jnp
import numpy as np
from jax import lax
from jax.experimental import pallas as pl
from jax.experimental.pallas import tpu as pltpu
from jax.sharding import PartitionSpec as P

TURN_STEPS = 360
DEFOCI = 16
EPSILON = 1e-06
SHARPNESS = 30.0
PRIOR_WEIGHT = 1.0

F32 = jnp.float32
BF16 = jnp.bfloat16
MESH = pl.DeviceIdType.MESH

SAMPLES = 256
ANGLES = 36
TURN_ROWS = 40
PAIR_ROWS = 2 * TURN_ROWS
PARTICLES_HERE = 64
CYCLES_HERE = 4
CLASSES_HERE = 25
BLOCK = 32
NX, NY, NZ = 4, 4, 8
ALL_CLASSES = 2 * NX * BLOCK
SIDE = 128
ROW_WIDTH = SIDE + CYCLES_HERE * 2 * SAMPLES
GROUPS = 4
Y_ROWS = 2 * PAIR_ROWS
GROUP_ROWS = NY * Y_ROWS
ALL_ROWS = GROUPS * GROUP_ROWS

NN = (((1,), (0,)), ((), ()))
NT = (((1,), (1,)), ((), ()))
TN = (((0,), (0,)), ((), ()))


def dft_matrix():
    positions = np.arange(SAMPLES)
    radians = (positions[:, None] * positions[None, :] % SAMPLES) * (2.0 * math.pi / SAMPLES)
    cosine = np.cos(radians) / math.sqrt(SAMPLES)
    sine = np.sin(radians) / math.sqrt(SAMPLES)
    return np.block([[cosine, -sine], [sine, cosine]]).astype(np.float32)


def walsh_matrix():
    matrix = np.ones((1, 1), np.float32)
    while matrix.shape[0] < ALL_CLASSES:
        matrix = np.block([[matrix, matrix], [matrix, -matrix]])
    return matrix


def split(values):
    high = values.astype(BF16)
    return high, (values - high.astype(F32)).astype(BF16)


def walsh(values, walsh_ref):
    high, low = split(values)
    return lax.dot_general(high, walsh_ref[...], NN, preferred_element_type=F32) + lax.dot_general(
        low, walsh_ref[...], NN, preferred_element_type=F32
    )


def dft(values, high_ref, low_ref):
    high, low = split(values)
    return (
        lax.dot_general(high, high_ref[...], NN, preferred_element_type=F32)
        + lax.dot_general(low, high_ref[...], NN, preferred_element_type=F32)
        + lax.dot_general(high, low_ref[...], NN, preferred_element_type=F32)
    )


def body(
    x_hbm, r_hbm, dft_hbm, walsh_hbm, ctf_hbm, ids_hbm, turns_hbm, out_ref,
    x_ref, r_ref, dft_ref, walsh_f, ctf_in, ids_ref, turns_ref,
    high_ref, low_ref, walsh_ref, ctf_ref, phase_ref,
    padded, x_rows, r_rows, spectra, weighted, power_rows, norm_rows, turned,
    partial_f, partial, far_in, near_in, near_out, z_out, z_in, pair_out, pair_in, weights,
    sums, core_out, core_in, xfar_out, xfar_in, xnear_out, xnear_in, rep_out, rep_via, rep_in,
    in_sem, rx_s, rx_r, rf_s, rf_r, rc_s, rc_r,
    fs, fr, ns, nr, zs, zr, zps, zpr, wzs, wzr, wys, wyr, wfs, wfr,
    cs, cr, xfs, xfr, xns, xnr, p1s, p1r, p2s, p2r,
):
    loads = [
        pltpu.make_async_copy(src, dst, in_sem.at[n])
        for n, (src, dst) in enumerate(
            [
                (r_hbm, r_ref), (dft_hbm, dft_ref), (x_hbm, x_ref), (ids_hbm, ids_ref),
                (turns_hbm, turns_ref), (ctf_hbm, ctf_in), (walsh_hbm, walsh_f),
            ]
        )
    ]
    for load in loads:
        load.start()
    cls = lax.axis_index("cls")
    pix = lax.axis_index("pix")
    rep = lax.axis_index("rep")
    x, core = cls // 2, cls % 2
    z, y = pix // NY, pix % NY
    other = 1 - core
    sibling = {"cls": x * 2 + other}

    def x_peer(d):
        return {"cls": (x + d) % NX * 2 + core}

    def y_peer(d):
        return {"pix": z * NY + (y + d) % NY}

    q, zh = z % 4, z // 4

    def q_peer(q_to):
        return {"pix": (zh * 4 + q_to) * NY + y}

    z_pair = {"pix": (z + 4) % NZ * NY + y}

    far_z = (z + 4) % NZ
    up = (z + 4) // NZ
    via = (
        {"pix": far_z * NY + y, "rep": (rep + up) % 2},
        {"pix": far_z * NY + y, "rep": (rep + 1 - up) % 2},
    )
    partners = (
        [sibling, {"pix": far_z * NY + y, "rep": 1 - rep}]
        + [x_peer(d) for d in (1, 3)]
        + [y_peer(d) for d in (1, 3)]
        + [q_peer((q + d) % 4) for d in range(1, 4)]
        + [z_pair]
    )

    def remote(src, dst, send, recv, device):
        return pltpu.make_async_remote_copy(
            src_ref=src, dst_ref=dst, send_sem=send, recv_sem=recv,
            device_id=device, device_id_type=MESH,
        )

    sent = []

    def start_copy(*args):
        remote(*args).start()

    def send(*args):
        copy = remote(*args)
        copy.start()
        sent.append(copy)

    barrier = pltpu.get_barrier_semaphore()
    for partner in partners:
        pl.semaphore_signal(barrier, inc=1, device_id=partner, device_id_type=MESH)

    loads[0].wait()
    loads[1].wait()
    high, low = split(dft_ref[...])
    high_ref[...] = high
    low_ref[...] = low
    padded[...] = jnp.zeros_like(padded)
    padded[0 : CLASSES_HERE * 16, :] = r_ref[...]
    for r in range(CYCLES_HERE):
        for p in range(2):
            for h in range(2):
                r_rows[r * BLOCK : (r + 1) * BLOCK, p * 256 + h * 128 : p * 256 + h * 128 + 128] = padded[
                    pl.ds(r * 4 + h * 2 + p, BLOCK, stride=16), :
                ]
    own = dft(r_rows[...], high_ref, low_ref).astype(BF16)
    own_rows = pl.ds(pl.multiple_of(cls * BLOCK, BLOCK), BLOCK)
    wide = own.astype(F32)
    power = jnp.sum(wide * wide, axis=1, keepdims=True)
    power_high, power_low = split(power)
    side_lane = lax.broadcasted_iota(jnp.int32, (BLOCK, SIDE), 1)
    side = jnp.zeros((BLOCK, SIDE), F32)
    for r in range(CYCLES_HERE):
        rows = slice(r * BLOCK, (r + 1) * BLOCK)
        spectra[own_rows, SIDE + r * 512 : SIDE + (r + 1) * 512] = own[rows, :]
        side = jnp.where(side_lane == r, power_high.astype(F32)[rows, :], side)
        side = jnp.where(side_lane == CYCLES_HERE + r, power_low.astype(F32)[rows, :], side)
    spectra[own_rows, 0:SIDE] = side.astype(BF16)

    pl.semaphore_wait(barrier, len(partners))
    steps = (1, 3)
    for way in range(2):
        send(
            spectra.at[own_rows, :], spectra.at[own_rows, :],
            rx_s.at[way], rx_r.at[way], x_peer(steps[way]),
        )
    send(spectra.at[own_rows, :], spectra.at[own_rows, :], rc_s.at[0], rc_r.at[0], sibling)

    def class_rows(x_of, core_of):
        return pl.ds(pl.multiple_of((x_of * 2 + core_of) * BLOCK, BLOCK), BLOCK)

    def half_rows(x_of, core_of, half):
        start = (x_of * 2 + core_of) * BLOCK + half * (BLOCK // 2)
        return pl.ds(pl.multiple_of(start, BLOCK // 2), BLOCK // 2)

    for load in loads[2:]:
        load.wait()
    walsh_ref[...] = walsh_f[...].astype(BF16)
    select = (
        lax.broadcasted_iota(jnp.int32, (CYCLES_HERE, 128), 1)
        - lax.broadcasted_iota(jnp.int32, (CYCLES_HERE, 128), 0)
    )
    select = ((select == 0) | (select == CYCLES_HERE)).astype(F32)
    ctf_ref[...] = lax.dot_general(
        ctf_in[...], select, TN, precision=lax.Precision.HIGHEST, preferred_element_type=F32
    )
    shape = (TURN_ROWS, ANGLES)
    on_row = lax.broadcasted_iota(jnp.int32, shape, 0) == lax.broadcasted_iota(jnp.int32, shape, 1)
    turns = jnp.sum(
        jnp.where(on_row, jnp.broadcast_to(turns_ref[...].astype(F32), shape), 0.0),
        axis=1, keepdims=True,
    )
    place = lax.broadcasted_iota(jnp.int32, (TURN_ROWS, SAMPLES), 1)
    signed = jnp.where(place < SAMPLES // 2, place, place - SAMPLES).astype(F32)
    count = turns * signed
    count = count - TURN_STEPS * jnp.floor(count * (1.0 / TURN_STEPS))
    count = jnp.where(count < 0, count + TURN_STEPS, count)
    count = jnp.where(count >= TURN_STEPS, count - TURN_STEPS, count)
    radians = count * (2.0 * math.pi / TURN_STEPS)
    phase_ref[0:TURN_ROWS, :] = jnp.cos(radians)
    phase_ref[TURN_ROWS : 2 * TURN_ROWS, :] = jnp.sin(radians)

    for r in range(CYCLES_HERE):
        for p in range(2):
            for h in range(2):
                x_rows[r * 64 : (r + 1) * 64, p * 256 + h * 128 : p * 256 + h * 128 + 128] = x_ref[
                    pl.ds(r * 4 + h * 2 + p, PARTICLES_HERE, stride=16), :
                ]
    part_square = jnp.zeros((PARTICLES_HERE, 128), F32)
    for r in range(CYCLES_HERE):
        for h in range(4):
            piece = x_rows[r * 64 : (r + 1) * 64, h * 128 : (h + 1) * 128]
            part_square += piece * piece
    part_norm = jnp.sum(part_square, axis=1, keepdims=True)
    picks = (
        lax.broadcasted_iota(jnp.int32, (DEFOCI, PARTICLES_HERE), 0) == ids_ref[...]
    ).astype(F32)
    ctf_rows = lax.dot_general(
        picks, ctf_ref[...], TN, precision=lax.Precision.HIGHEST, preferred_element_type=F32
    )
    particle_spectra = dft(x_rows[...], high_ref, low_ref)
    for r in range(CYCLES_HERE):
        weighted[:, r * 512 : (r + 1) * 512] = (
            ctf_rows[:, r : r + 1] * particle_spectra[r * 64 : (r + 1) * 64, :]
        )
    squared = ctf_rows * ctf_rows
    square_high = squared.astype(BF16).astype(F32)
    lane = lax.broadcasted_iota(jnp.int32, squared.shape, 1)
    power_rows[...] = jnp.where(lane < CYCLES_HERE, square_high, squared - square_high)

    for way in range(2):
        x_of = (x + NX - steps[way]) % NX
        rows = spectra.at[class_rows(x_of, core), :]
        remote(rows, rows, rx_s.at[way], rx_r.at[way], x_peer(steps[way])).wait_recv()
        half = spectra.at[half_rows(x_of, core, way), :]
        send(half, half, rf_s.at[way], rf_r.at[way], x_peer(steps[way]))
        send(rows, rows, rc_s.at[way + 1], rc_r.at[way + 1], sibling)

    cosine = phase_ref[0:TURN_ROWS, :]
    sine = phase_ref[TURN_ROWS : 2 * TURN_ROWS, :]

    def turn_pair(pair, carry):
        rows = pl.ds(pl.multiple_of(pair * PAIR_ROWS, 16), PAIR_ROWS)
        for r in range(CYCLES_HERE):
            real, imag = [], []
            for e in range(2):
                w_re = weighted[pl.ds(pair * 2 + e, 1), r * 512 : r * 512 + 256]
                w_im = weighted[pl.ds(pair * 2 + e, 1), r * 512 + 256 : r * 512 + 512]
                real.append(w_re * cosine - w_im * sine)
                imag.append(w_re * sine + w_im * cosine)
            start = SIDE + r * 512
            turned[rows, start : start + 256] = jnp.concatenate(real, axis=0).astype(BF16)
            turned[rows, start + 256 : start + 512] = jnp.concatenate(imag, axis=0).astype(BF16)
        tail = [
            jnp.broadcast_to(power_rows[pl.ds(pair * 2 + e, 1), :], (TURN_ROWS, 128)) for e in range(2)
        ]
        turned[rows, 0:SIDE] = jnp.concatenate(tail, axis=0).astype(BF16)
        return carry

    lax.fori_loop(0, PARTICLES_HERE // 4, turn_pair, 0)
    x_far = (x + 2) % NX
    for way in range(2):
        half = spectra.at[half_rows(x_far, core, way), :]
        remote(half, half, rf_s.at[way], rf_r.at[way], x_peer(steps[way])).wait_recv()
    rows = spectra.at[class_rows(x_far, core), :]
    send(rows, rows, rc_s.at[3], rc_r.at[3], sibling)
    lax.fori_loop(PARTICLES_HERE // 4, PARTICLES_HERE // 2, turn_pair, 0)

    for n, x_of in enumerate((x, (x + 3) % NX, (x + 1) % NX, x_far)):
        rows = spectra.at[class_rows(x_of, other), :]
        remote(rows, rows, rc_s.at[n], rc_r.at[n], sibling).wait_recv()

    ctf_high, ctf_low = split(ctf_ref[...] * ctf_ref[...])
    ref_norm = lax.dot_general(
        ctf_high, spectra[:, 0:SIDE], NT, preferred_element_type=F32
    ) + lax.dot_general(ctf_low, spectra[:, 0:SIDE], NT, preferred_element_type=F32)
    picked = lax.dot_general(
        picks, ref_norm, TN, precision=lax.Precision.HIGHEST, preferred_element_type=F32
    )
    picked_high = picked.astype(BF16).astype(F32)
    wide_norm = jnp.broadcast_to(part_norm, (PARTICLES_HERE, ALL_CLASSES))
    wide_high = wide_norm.astype(BF16).astype(F32)
    norm_rows[0] = picked_high
    norm_rows[1] = picked - picked_high
    norm_rows[2] = wide_high
    norm_rows[3] = wide_norm - wide_high
    sub = lax.broadcasted_iota(jnp.int32, (8, ALL_CLASSES), 0)

    def z_group(step):
        return (q + 1 + step) % GROUPS

    def y_rows_of(group, y_to):
        return pl.ds(pl.multiple_of(group * GROUP_ROWS + y_to * Y_ROWS, Y_ROWS), Y_ROWS)

    def y_half_of(group, y_to, half):
        start = group * GROUP_ROWS + y_to * Y_ROWS + half * PAIR_ROWS
        return pl.ds(pl.multiple_of(start, PAIR_ROWS), PAIR_ROWS)

    def correlate(step):
        group = z_group(step)
        rows = pl.ds(pl.multiple_of(group * GROUP_ROWS, GROUP_ROWS), GROUP_ROWS)
        partial_f[...] = walsh(
            lax.dot_general(turned[rows, SIDE:], spectra[:, SIDE:], NT, preferred_element_type=F32), walsh_ref
        )

        def patch(pair, carry):
            pieces = []
            for e in range(2):
                start = pl.multiple_of(pair * PAIR_ROWS + e * TURN_ROWS, 8)
                pieces.append(partial_f[pl.ds(start, 32), :])
                last = partial_f[pl.ds(start + 32, 8), :]
                particle = group * 16 + pair * 2 + e
                for n in range(4):
                    last = jnp.where(sub == 4 + n, norm_rows[n, pl.ds(particle, 1), :], last)
                pieces.append(last)
            start = pl.multiple_of(group * GROUP_ROWS + pair * PAIR_ROWS, 16)
            partial[pl.ds(start, PAIR_ROWS), :] = jnp.concatenate(pieces, axis=0).astype(BF16)
            return carry

        lax.fori_loop(0, NY * 2, patch, 0)
        for way in range(2):
            start_copy(
                partial.at[y_half_of(group, (y + 2) % NY, way), :],
                far_in.at[step, way], fs.at[step, way], fr.at[step, way], y_peer(steps[way]),
            )

    odd_row = sub % 2 == 1

    def product_rounded(total):
        pieces = []
        for e in range(2):
            start = e * TURN_ROWS
            pieces.append(total[start : start + 32, :])
            last = total[start + 32 : start + 40, :]
            whole = last + pltpu.roll(last, 7, 0)
            high = whole.astype(BF16).astype(F32)
            low = pltpu.roll(whole - high, 1, 0)
            pieces.append(jnp.where(sub < 4, last, jnp.where(odd_row, low, high)))
        return jnp.concatenate(pieces, axis=0).astype(BF16)

    def relay(step):
        group = z_group(step)
        for way in range(2):
            own = partial.at[y_half_of(group, (y + steps[way]) % NY, way), :]
            remote(
                own, far_in.at[step, way], fs.at[step, way], fr.at[step, way], y_peer(steps[way])
            ).wait_recv()
            near_out[step, way, way] = product_rounded(
                own[...].astype(F32) + far_in[step, way].astype(F32)
            )
            near_out[step, way, 1 - way] = partial[
                y_half_of(group, (y + steps[way]) % NY, 1 - way), :
            ]
            start_copy(
                near_out.at[step, way], near_in.at[step, way],
                ns.at[step, way], nr.at[step, way], y_peer(steps[way]),
            )

    def reduce_y(step):
        group = z_group(step)
        for way in range(2):
            remote(
                near_out.at[step, way], near_in.at[step, way],
                ns.at[step, way], nr.at[step, way], y_peer(steps[way]),
            ).wait_recv()
        for half in range(2):
            total = partial[y_half_of(group, y, half), :].astype(F32)
            for way in range(2):
                total += near_in[step, way, half].astype(F32)
            z_out[step, half * PAIR_ROWS : (half + 1) * PAIR_ROWS, :] = product_rounded(total)

        @pl.when(step < GROUPS - 1)
        def _():
            start_copy(
                z_out.at[step], z_in.at[step], zs.at[step], zr.at[step], q_peer(group)
            )

    def product_step(step, carry):
        pl.when(step < GROUPS)(lambda: correlate(step))
        pl.when((step > 0) & (step <= GROUPS))(lambda: relay(step - 1))
        pl.when(step > 1)(lambda: reduce_y(step - 2))
        return carry

    lax.fori_loop(0, GROUPS + 2, product_step, 0)

    total = z_out[GROUPS - 1].astype(F32)
    for n in range(GROUPS - 1):
        remote(z_out.at[n], z_in.at[n], zs.at[n], zr.at[n], z_pair).wait_recv()
        total += z_in[n].astype(F32)
    for half in range(2):
        rows = slice(half * PAIR_ROWS, (half + 1) * PAIR_ROWS)
        pair_out[rows, :] = product_rounded(total[rows, :])
    send(pair_out, pair_in, zps, zpr, z_pair)
    sums[...] = jnp.zeros_like(sums)
    remote(pair_out, pair_in, zps, zpr, z_pair).wait_recv()
    mine = total + pair_in[...].astype(F32)

    shape = (TURN_ROWS, ALL_CLASSES)
    valid = (lax.broadcasted_iota(jnp.int32, shape, 0) < ANGLES) & (
        lax.broadcasted_iota(jnp.int32, shape, 1) % BLOCK < CLASSES_HERE
    )
    products = walsh(mine, walsh_ref) * (1.0 / ALL_CLASSES)
    pieces = []
    for e in range(4):
        rows = mine[e * TURN_ROWS : (e + 1) * TURN_ROWS, :]
        ref_row = rows[36:37, :] + rows[37:38, :]
        part_row = rows[38:39, :] + rows[39:40, :]
        scaling = lax.rsqrt(part_row + EPSILON) * lax.rsqrt(ref_row + EPSILON)
        scores = jnp.where(
            valid, SHARPNESS * products[e * TURN_ROWS : (e + 1) * TURN_ROWS, :] * scaling, 0.0
        )
        raised = jnp.where(valid, jnp.exp(scores), 0.0)
        total = jnp.sum(jnp.sum(raised, axis=0, keepdims=True), axis=1, keepdims=True)
        pieces.append(raised / total)

    group_rows = weights.at[y_rows_of(q, y), :]
    group_rows[...] = jnp.concatenate(pieces, axis=0).astype(BF16)
    for d in (1, 3, 2):
        send(group_rows, group_rows, wzs.at[d], wzr.at[d], q_peer((q + d) % 4))

    def w_group(step):
        return (q + GROUPS - step) % GROUPS

    def spread(step):
        group = w_group(step)
        rows = weights.at[y_rows_of(group, y), :]

        @pl.when(step > 0)
        def _():
            remote(rows, rows, wzs.at[step], wzr.at[step], z_pair).wait_recv()

        for way in range(2):
            start_copy(rows, rows, wys.at[step, way], wyr.at[step, way], y_peer(steps[way]))

    def pass_on(step):
        group = w_group(step)
        for way in range(2):
            y_of = (y + NY - steps[way]) % NY
            rows = weights.at[y_rows_of(group, y_of), :]
            remote(
                rows, rows, wys.at[step, way], wyr.at[step, way], y_peer(steps[way])
            ).wait_recv()
            half = weights.at[y_half_of(group, y_of, way), :]
            start_copy(half, half, wfs.at[step, way], wfr.at[step, way], y_peer(steps[way]))

    def await_group(step):
        group = w_group(step)
        for way in range(2):
            half = weights.at[y_half_of(group, (y + 2) % NY, way), :]
            remote(
                half, half, wfs.at[step, way], wfr.at[step, way], y_peer(steps[way])
            ).wait_recv()
        return pl.ds(pl.multiple_of(group * GROUP_ROWS, GROUP_ROWS), GROUP_ROWS)

    def add_group(step):
        rows = await_group(step)
        picked_weights = weights[rows, :].T
        for r in range(CYCLES_HERE):
            lanes = slice(SIDE + r * 512 if r else 0, SIDE + (r + 1) * 512)
            sums[:, lanes] += lax.dot_general(
                picked_weights, turned[rows, lanes], NN, preferred_element_type=F32
            )

    def weight_step(step, carry):
        pl.when(step < GROUPS)(lambda: spread(step))
        pl.when((step > 0) & (step <= GROUPS))(lambda: pass_on(step - 1))
        pl.when(step > 1)(lambda: add_group(step - 2))
        return carry

    lax.fori_loop(0, GROUPS + 2, weight_step, 0)

    HALF = BLOCK // 2
    def rounded(total):
        whole = total[:, 0:SIDE]
        side_lane = lax.broadcasted_iota(jnp.int32, whole.shape, 1)
        whole = whole + pltpu.roll(whole, SIDE - CYCLES_HERE, 1)
        high = whole.astype(BF16).astype(F32)
        low = pltpu.roll(whole - high, CYCLES_HERE, 1)
        side = jnp.where(side_lane < CYCLES_HERE, high, jnp.where(side_lane < 2 * CYCLES_HERE, low, 0.0))
        return jnp.concatenate([side, total[:, SIDE:]], axis=1).astype(BF16)

    def core_block(d, carry):
        core_out[pl.ds(pl.multiple_of(d * BLOCK, BLOCK), BLOCK), :] = rounded(
            sums[class_rows(d, other), :]
        )
        return carry

    lax.fori_loop(0, NX, core_block, 0)
    send(core_out, core_in, cs, cr, sibling)

    def core_sum(x_to, half):
        start = pl.multiple_of(x_to * BLOCK + half * HALF, HALF)
        return sums[half_rows(x_to, core, half), :] + core_in[pl.ds(start, HALF), :].astype(F32)

    remote(core_out, core_in, cs, cr, sibling).wait_recv()
    for way in range(2):
        xfar_out[way] = rounded(core_sum((x + 2) % NX, way))
        send(xfar_out.at[way], xfar_in.at[way], xfs.at[way], xfr.at[way], x_peer(steps[way]))
    for way in range(2):
        xnear_out[way, 1 - way] = rounded(core_sum((x + steps[way]) % NX, 1 - way))
    for way in range(2):
        remote(
            xfar_out.at[way], xfar_in.at[way], xfs.at[way], xfr.at[way], x_peer(steps[way])
        ).wait_recv()
        xnear_out[way, way] = rounded(
            core_sum((x + steps[way]) % NX, way) + xfar_in[way].astype(F32)
        )
        send(xnear_out.at[way], xnear_in.at[way], xns.at[way], xnr.at[way], x_peer(steps[way]))
    for way in range(2):
        remote(
            xnear_out.at[way], xnear_in.at[way], xns.at[way], xnr.at[way], x_peer(steps[way])
        ).wait_recv()

    for half in range(2):
        total = core_sum(x, half)
        for way in range(2):
            total += xnear_in[way, half].astype(F32)
        rep_out[half] = rounded(total)
        send(rep_out.at[half], rep_via.at[half], p1s.at[half], p1r.at[half], via[half])
    for half in range(2):
        remote(
            rep_out.at[half], rep_via.at[half], p1s.at[half], p1r.at[half], via[half]
        ).wait_recv()
        send(rep_via.at[half], rep_in.at[half], p2s.at[half], p2r.at[half], via[half])
    halves = []
    for half in range(2):
        remote(
            rep_via.at[half], rep_in.at[half], p2s.at[half], p2r.at[half], via[half]
        ).wait_recv()
        halves.append(rep_out[half].astype(F32) + rep_in[half].astype(F32))
    total = jnp.concatenate(halves, axis=0)
    for r in range(CYCLES_HERE):
        density = total[:, r : r + 1] + total[:, r + CYCLES_HERE : r + CYCLES_HERE + 1]
        piece = total[:, SIDE + r * 512 : SIDE + (r + 1) * 512] / (density + PRIOR_WEIGHT)
        r_rows[r * BLOCK : (r + 1) * BLOCK, 0:256] = piece[:, 0:256]
        r_rows[r * BLOCK : (r + 1) * BLOCK, 256:512] = -piece[:, 256:512]
    result = dft(r_rows[...], high_ref, low_ref)
    for r in range(CYCLES_HERE):
        for p in range(2):
            for h in range(2):
                piece = result[
                    r * BLOCK : (r + 1) * BLOCK, p * 256 + h * 128 : p * 256 + h * 128 + 128
                ]
                padded[pl.ds(r * 4 + h * 2 + p, BLOCK, stride=16), :] = piece if p == 0 else -piece
    out_ref[...] = padded[0 : CLASSES_HERE * 16, :]

    for copy in sent:
        copy.wait_send()

    def drain(step, carry):
        for way in range(2):
            piece = far_in.at[step, way]
            remote(piece, piece, fs.at[step, way], fr.at[step, way], z_pair).wait_send()
            piece = near_out.at[step, way]
            remote(piece, piece, ns.at[step, way], nr.at[step, way], z_pair).wait_send()
            rows = weights.at[0:Y_ROWS, :]
            remote(rows, rows, wys.at[step, way], wyr.at[step, way], z_pair).wait_send()
            half = weights.at[0:PAIR_ROWS, :]
            remote(half, half, wfs.at[step, way], wfr.at[step, way], z_pair).wait_send()

        @pl.when(step < GROUPS - 1)
        def _():
            remote(z_out.at[step], z_in.at[step], zs.at[step], zr.at[step], z_pair).wait_send()

        return carry

    lax.fori_loop(0, GROUPS, drain, 0)


def to_rows(values):
    count = values.shape[0]
    return values.reshape(count, CYCLES_HERE, 2, 2, 128).transpose(0, 1, 3, 2, 4).reshape(count * 16, 128)


def from_rows(rows):
    return (
        rows.reshape(CLASSES_HERE, CYCLES_HERE, 2, 2, 128)
        .transpose(0, 1, 3, 2, 4)
        .reshape(CLASSES_HERE, CYCLES_HERE, 2, 256)
    )


def per_device(particles, references, ctf_table, defocus_ids, rotation_ids):
    vmem = pl.BlockSpec(memory_space=pltpu.VMEM)
    dma = pltpu.SemaphoreType.DMA
    out = pl.pallas_call(
        body,
        out_shape=jax.ShapeDtypeStruct((CLASSES_HERE * 16, 128), F32),
        in_specs=[pl.BlockSpec(memory_space=pl.ANY)] * 7,
        out_specs=vmem,
        scratch_shapes=[
            pltpu.VMEM((PARTICLES_HERE * 16, 128), F32),
            pltpu.VMEM((CLASSES_HERE * 16, 128), F32),
            pltpu.VMEM((512, 512), F32),
            pltpu.VMEM((ALL_CLASSES, ALL_CLASSES), F32),
            pltpu.VMEM((CYCLES_HERE, DEFOCI), F32),
            pltpu.VMEM((1, PARTICLES_HERE), jnp.int32),
            pltpu.VMEM((1, ANGLES), jnp.int32),
            pltpu.VMEM((512, 512), BF16),
            pltpu.VMEM((512, 512), BF16),
            pltpu.VMEM((ALL_CLASSES, ALL_CLASSES), BF16),
            pltpu.VMEM((DEFOCI, 128), F32),
            pltpu.VMEM((2 * TURN_ROWS, SAMPLES), F32),
            pltpu.VMEM((BLOCK * 16, 128), F32),
            pltpu.VMEM((CYCLES_HERE * PARTICLES_HERE, 512), F32),
            pltpu.VMEM((CYCLES_HERE * BLOCK, 512), F32),
            pltpu.VMEM((ALL_CLASSES, ROW_WIDTH), BF16),
            pltpu.VMEM((PARTICLES_HERE, ROW_WIDTH - SIDE), F32),
            pltpu.VMEM((PARTICLES_HERE, 128), F32),
            pltpu.VMEM((4, PARTICLES_HERE, ALL_CLASSES), F32),
            pltpu.VMEM((ALL_ROWS, ROW_WIDTH), BF16),
            pltpu.VMEM((GROUP_ROWS, ALL_CLASSES), F32),
            pltpu.VMEM((ALL_ROWS, ALL_CLASSES), BF16),
            pltpu.VMEM((GROUPS, 2, PAIR_ROWS, ALL_CLASSES), BF16),
            pltpu.VMEM((GROUPS, 2, 2, PAIR_ROWS, ALL_CLASSES), BF16),
            pltpu.VMEM((GROUPS, 2, 2, PAIR_ROWS, ALL_CLASSES), BF16),
            pltpu.VMEM((GROUPS, Y_ROWS, ALL_CLASSES), BF16),
            pltpu.VMEM((GROUPS - 1, Y_ROWS, ALL_CLASSES), BF16),
            pltpu.VMEM((Y_ROWS, ALL_CLASSES), BF16),
            pltpu.VMEM((Y_ROWS, ALL_CLASSES), BF16),
            pltpu.VMEM((ALL_ROWS, ALL_CLASSES), BF16),
            pltpu.VMEM((ALL_CLASSES, ROW_WIDTH), F32),
            pltpu.VMEM((NX * BLOCK, ROW_WIDTH), BF16),
            pltpu.VMEM((NX * BLOCK, ROW_WIDTH), BF16),
            pltpu.VMEM((2, BLOCK // 2, ROW_WIDTH), BF16),
            pltpu.VMEM((2, BLOCK // 2, ROW_WIDTH), BF16),
            pltpu.VMEM((2, 2, BLOCK // 2, ROW_WIDTH), BF16),
            pltpu.VMEM((2, 2, BLOCK // 2, ROW_WIDTH), BF16),
            pltpu.VMEM((2, BLOCK // 2, ROW_WIDTH), BF16),
            pltpu.VMEM((2, BLOCK // 2, ROW_WIDTH), BF16),
            pltpu.VMEM((2, BLOCK // 2, ROW_WIDTH), BF16),
            dma((7,)),
            dma((2,)), dma((2,)), dma((2,)), dma((2,)),
            dma((NX,)), dma((NX,)),
            dma((GROUPS, 2)), dma((GROUPS, 2)),
            dma((GROUPS, 2)), dma((GROUPS, 2)),
            dma((GROUPS - 1,)), dma((GROUPS - 1,)),
            dma(()), dma(()),
            dma((GROUPS,)), dma((GROUPS,)),
            dma((GROUPS, 2)), dma((GROUPS, 2)),
            dma((GROUPS, 2)), dma((GROUPS, 2)),
            dma(()), dma(()),
            dma((2,)), dma((2,)), dma((2,)), dma((2,)),
            dma((2,)), dma((2,)), dma((2,)), dma((2,)),
        ],
        compiler_params=pltpu.CompilerParams(
            collective_id=0, has_side_effects=True, vmem_limit_bytes=56 * 1024 * 1024
        ),
    )(
        to_rows(particles), to_rows(references), jnp.asarray(dft_matrix()), jnp.asarray(walsh_matrix()),
        ctf_table.T, defocus_ids.reshape(1, PARTICLES_HERE), rotation_ids.reshape(1, ANGLES),
    )
    return from_rows(out)


def solution(mesh):
    in_specs = (
        P(("cls", "rep"), "pix", None, None),
        P("cls", "pix", None, None),
        P(None, "pix"),
        P(("cls", "rep")),
        P(),
    )
    out_specs = P("cls", "pix", None, None)
    return jax.shard_map(
        per_device, mesh=mesh, in_specs=in_specs, out_specs=out_specs, check_vma=False
    )
```

```python
import math

import jax
import jax.numpy as jnp
import numpy as np
from jax import lax
from jax.experimental import pallas as pl
from jax.experimental.pallas import tpu as pltpu
from jax.sharding import PartitionSpec as P

TURN_STEPS = 360
DEFOCI = 16
EPSILON = 1e-06
SHARPNESS = 30.0
PRIOR_WEIGHT = 1.0

F32 = jnp.float32
BF16 = jnp.bfloat16
MESH = pl.DeviceIdType.MESH

SAMPLES = 256
ANGLES = 36
TURN_ROWS = 40
PAIR_ROWS = 2 * TURN_ROWS
PARTICLES_HERE = 64
CYCLES_HERE = 4
CLASSES_HERE = 25
BLOCK = 32
NX, NY, NZ = 4, 4, 8
ALL_CLASSES = 2 * NX * BLOCK
SIDE = 128
ROW_WIDTH = SIDE + CYCLES_HERE * 2 * SAMPLES
GROUPS = 4
Y_ROWS = 2 * PAIR_ROWS
GROUP_ROWS = NY * Y_ROWS
ALL_ROWS = GROUPS * GROUP_ROWS

NN = (((1,), (0,)), ((), ()))
NT = (((1,), (1,)), ((), ()))
TN = (((0,), (0,)), ((), ()))


def dft_matrix():
    positions = np.arange(SAMPLES)
    radians = (positions[:, None] * positions[None, :] % SAMPLES) * (2.0 * math.pi / SAMPLES)
    cosine = np.cos(radians) / math.sqrt(SAMPLES)
    sine = np.sin(radians) / math.sqrt(SAMPLES)
    return np.block([[cosine, -sine], [sine, cosine]]).astype(np.float32)


def walsh_matrix():
    matrix = np.ones((1, 1), np.float32)
    while matrix.shape[0] < ALL_CLASSES:
        matrix = np.block([[matrix, matrix], [matrix, -matrix]])
    return matrix


def split(values):
    high = values.astype(BF16)
    return high, (values - high.astype(F32)).astype(BF16)


def walsh(values, walsh_ref):
    high, low = split(values)
    return lax.dot_general(high, walsh_ref[...], NN, preferred_element_type=F32) + lax.dot_general(
        low, walsh_ref[...], NN, preferred_element_type=F32
    )


def dft(values, high_ref, low_ref):
    high, low = split(values)
    return (
        lax.dot_general(high, high_ref[...], NN, preferred_element_type=F32)
        + lax.dot_general(low, high_ref[...], NN, preferred_element_type=F32)
        + lax.dot_general(high, low_ref[...], NN, preferred_element_type=F32)
    )


def body(
    x_hbm, r_hbm, dft_hbm, walsh_hbm, ctf_hbm, ids_hbm, turns_hbm, out_ref,
    x_ref, r_ref, dft_ref, walsh_f, ctf_in, ids_ref, turns_ref,
    high_ref, low_ref, walsh_ref, ctf_ref, phase_ref,
    padded, x_rows, r_rows, spectra, mixed, weighted, power_rows, norm_rows, turned,
    partial_f, partial, far_in, near_in, near_out, z_out, z_in, pair_out, pair_in, weights,
    sums, core_out, core_in, xfar_out, xfar_in, xnear_out, xnear_in, rep_out, rep_via, rep_in,
    in_sem, rx_s, rx_r, rf_s, rf_r, rc_s, rc_r,
    fs, fr, ns, nr, zs, zr, zps, zpr, wzs, wzr, wys, wyr, wfs, wfr,
    cs, cr, xfs, xfr, xns, xnr, p1s, p1r, p2s, p2r,
):
    loads = [
        pltpu.make_async_copy(src, dst, in_sem.at[n])
        for n, (src, dst) in enumerate(
            [
                (r_hbm, r_ref), (dft_hbm, dft_ref), (x_hbm, x_ref), (ids_hbm, ids_ref),
                (turns_hbm, turns_ref), (ctf_hbm, ctf_in), (walsh_hbm, walsh_f),
            ]
        )
    ]
    for load in loads:
        load.start()
    cls = lax.axis_index("cls")
    pix = lax.axis_index("pix")
    rep = lax.axis_index("rep")
    x, core = cls // 2, cls % 2
    z, y = pix // NY, pix % NY
    other = 1 - core
    sibling = {"cls": x * 2 + other}

    def x_peer(d):
        return {"cls": (x + d) % NX * 2 + core}

    def y_peer(d):
        return {"pix": z * NY + (y + d) % NY}

    q, zh = z % 4, z // 4

    def q_peer(q_to):
        return {"pix": (zh * 4 + q_to) * NY + y}

    z_pair = {"pix": (z + 4) % NZ * NY + y}

    far_z = (z + 4) % NZ
    up = (z + 4) // NZ
    via = (
        {"pix": far_z * NY + y, "rep": (rep + up) % 2},
        {"pix": far_z * NY + y, "rep": (rep + 1 - up) % 2},
    )
    partners = (
        [sibling, {"pix": far_z * NY + y, "rep": 1 - rep}]
        + [x_peer(d) for d in (1, 3)]
        + [y_peer(d) for d in (1, 3)]
        + [q_peer((q + d) % 4) for d in range(1, 4)]
        + [z_pair]
    )

    def remote(src, dst, send, recv, device):
        return pltpu.make_async_remote_copy(
            src_ref=src, dst_ref=dst, send_sem=send, recv_sem=recv,
            device_id=device, device_id_type=MESH,
        )

    sent = []

    def start_copy(*args):
        remote(*args).start()

    def send(*args):
        copy = remote(*args)
        copy.start()
        sent.append(copy)

    barrier = pltpu.get_barrier_semaphore()
    for partner in partners:
        pl.semaphore_signal(barrier, inc=1, device_id=partner, device_id_type=MESH)

    loads[0].wait()
    loads[1].wait()
    high, low = split(dft_ref[...])
    high_ref[...] = high
    low_ref[...] = low
    padded[...] = jnp.zeros_like(padded)
    padded[0 : CLASSES_HERE * 16, :] = r_ref[...]
    for r in range(CYCLES_HERE):
        for p in range(2):
            for h in range(2):
                r_rows[r * BLOCK : (r + 1) * BLOCK, p * 256 + h * 128 : p * 256 + h * 128 + 128] = padded[
                    pl.ds(r * 4 + h * 2 + p, BLOCK, stride=16), :
                ]
    own = dft(r_rows[...], high_ref, low_ref).astype(BF16)
    own_rows = pl.ds(pl.multiple_of(cls * BLOCK, BLOCK), BLOCK)
    wide = own.astype(F32)
    power = jnp.sum(wide * wide, axis=1, keepdims=True)
    power_high, power_low = split(power)
    side_lane = lax.broadcasted_iota(jnp.int32, (BLOCK, SIDE), 1)
    side = jnp.zeros((BLOCK, SIDE), F32)
    for r in range(CYCLES_HERE):
        rows = slice(r * BLOCK, (r + 1) * BLOCK)
        spectra[own_rows, SIDE + r * 512 : SIDE + (r + 1) * 512] = own[rows, :]
        side = jnp.where(side_lane == r, power_high.astype(F32)[rows, :], side)
        side = jnp.where(side_lane == CYCLES_HERE + r, power_low.astype(F32)[rows, :], side)
    spectra[own_rows, 0:SIDE] = side.astype(BF16)

    pl.semaphore_wait(barrier, len(partners))
    steps = (1, 3)
    for way in range(2):
        send(
            spectra.at[own_rows, :], spectra.at[own_rows, :],
            rx_s.at[way], rx_r.at[way], x_peer(steps[way]),
        )
    send(spectra.at[own_rows, :], spectra.at[own_rows, :], rc_s.at[0], rc_r.at[0], sibling)

    def class_rows(x_of, core_of):
        return pl.ds(pl.multiple_of((x_of * 2 + core_of) * BLOCK, BLOCK), BLOCK)

    def half_rows(x_of, core_of, half):
        start = (x_of * 2 + core_of) * BLOCK + half * (BLOCK // 2)
        return pl.ds(pl.multiple_of(start, BLOCK // 2), BLOCK // 2)

    for load in loads[2:]:
        load.wait()
    walsh_ref[...] = walsh_f[...].astype(BF16)
    select = (
        lax.broadcasted_iota(jnp.int32, (CYCLES_HERE, 128), 1)
        - lax.broadcasted_iota(jnp.int32, (CYCLES_HERE, 128), 0)
    )
    select = ((select == 0) | (select == CYCLES_HERE)).astype(F32)
    ctf_ref[...] = lax.dot_general(
        ctf_in[...], select, TN, precision=lax.Precision.HIGHEST, preferred_element_type=F32
    )
    shape = (TURN_ROWS, ANGLES)
    on_row = lax.broadcasted_iota(jnp.int32, shape, 0) == lax.broadcasted_iota(jnp.int32, shape, 1)
    turns = jnp.sum(
        jnp.where(on_row, jnp.broadcast_to(turns_ref[...].astype(F32), shape), 0.0),
        axis=1, keepdims=True,
    )
    place = lax.broadcasted_iota(jnp.int32, (TURN_ROWS, SAMPLES), 1)
    signed = jnp.where(place < SAMPLES // 2, place, place - SAMPLES).astype(F32)
    count = turns * signed
    count = count - TURN_STEPS * jnp.floor(count * (1.0 / TURN_STEPS))
    count = jnp.where(count < 0, count + TURN_STEPS, count)
    count = jnp.where(count >= TURN_STEPS, count - TURN_STEPS, count)
    radians = count * (2.0 * math.pi / TURN_STEPS)
    phase_ref[0:TURN_ROWS, :] = jnp.cos(radians)
    phase_ref[TURN_ROWS : 2 * TURN_ROWS, :] = jnp.sin(radians)

    for r in range(CYCLES_HERE):
        for p in range(2):
            for h in range(2):
                x_rows[r * 64 : (r + 1) * 64, p * 256 + h * 128 : p * 256 + h * 128 + 128] = x_ref[
                    pl.ds(r * 4 + h * 2 + p, PARTICLES_HERE, stride=16), :
                ]
    part_square = jnp.zeros((PARTICLES_HERE, 128), F32)
    for r in range(CYCLES_HERE):
        for h in range(4):
            piece = x_rows[r * 64 : (r + 1) * 64, h * 128 : (h + 1) * 128]
            part_square += piece * piece
    part_norm = jnp.sum(part_square, axis=1, keepdims=True)
    picks = (
        lax.broadcasted_iota(jnp.int32, (DEFOCI, PARTICLES_HERE), 0) == ids_ref[...]
    ).astype(F32)
    ctf_rows = lax.dot_general(
        picks, ctf_ref[...], TN, precision=lax.Precision.HIGHEST, preferred_element_type=F32
    )
    particle_spectra = dft(x_rows[...], high_ref, low_ref)
    for r in range(CYCLES_HERE):
        weighted[:, r * 512 : (r + 1) * 512] = (
            ctf_rows[:, r : r + 1] * particle_spectra[r * 64 : (r + 1) * 64, :]
        )
    squared = ctf_rows * ctf_rows
    square_high = squared.astype(BF16).astype(F32)
    lane = lax.broadcasted_iota(jnp.int32, squared.shape, 1)
    power_rows[...] = jnp.where(lane < CYCLES_HERE, square_high, squared - square_high)

    for way in range(2):
        x_of = (x + NX - steps[way]) % NX
        rows = spectra.at[class_rows(x_of, core), :]
        remote(rows, rows, rx_s.at[way], rx_r.at[way], x_peer(steps[way])).wait_recv()
        half = spectra.at[half_rows(x_of, core, way), :]
        send(half, half, rf_s.at[way], rf_r.at[way], x_peer(steps[way]))
        send(rows, rows, rc_s.at[way + 1], rc_r.at[way + 1], sibling)

    cosine = phase_ref[0:TURN_ROWS, :]
    sine = phase_ref[TURN_ROWS : 2 * TURN_ROWS, :]

    def turn_pair(pair, carry):
        rows = pl.ds(pl.multiple_of(pair * PAIR_ROWS, 16), PAIR_ROWS)
        for r in range(CYCLES_HERE):
            real, imag = [], []
            for e in range(2):
                w_re = weighted[pl.ds(pair * 2 + e, 1), r * 512 : r * 512 + 256]
                w_im = weighted[pl.ds(pair * 2 + e, 1), r * 512 + 256 : r * 512 + 512]
                real.append(w_re * cosine - w_im * sine)
                imag.append(w_re * sine + w_im * cosine)
            start = SIDE + r * 512
            turned[rows, start : start + 256] = jnp.concatenate(real, axis=0).astype(BF16)
            turned[rows, start + 256 : start + 512] = jnp.concatenate(imag, axis=0).astype(BF16)
        tail = [
            jnp.broadcast_to(power_rows[pl.ds(pair * 2 + e, 1), :], (TURN_ROWS, 128)) for e in range(2)
        ]
        turned[rows, 0:SIDE] = jnp.concatenate(tail, axis=0).astype(BF16)
        return carry

    lax.fori_loop(0, PARTICLES_HERE // 4, turn_pair, 0)
    x_far = (x + 2) % NX
    for way in range(2):
        half = spectra.at[half_rows(x_far, core, way), :]
        remote(half, half, rf_s.at[way], rf_r.at[way], x_peer(steps[way])).wait_recv()
    rows = spectra.at[class_rows(x_far, core), :]
    send(rows, rows, rc_s.at[3], rc_r.at[3], sibling)
    lax.fori_loop(PARTICLES_HERE // 4, PARTICLES_HERE // 2, turn_pair, 0)

    for n, x_of in enumerate((x, (x + 3) % NX, (x + 1) % NX, x_far)):
        rows = spectra.at[class_rows(x_of, other), :]
        remote(rows, rows, rc_s.at[n], rc_r.at[n], sibling).wait_recv()

    for r in range(CYCLES_HERE):
        mixed[:, r * 512 : (r + 1) * 512] = lax.dot_general(
            walsh_ref[...], spectra[:, SIDE + r * 512 : SIDE + (r + 1) * 512], NN,
            preferred_element_type=F32,
        ).astype(BF16)

    ctf_high, ctf_low = split(ctf_ref[...] * ctf_ref[...])
    ref_norm = lax.dot_general(
        ctf_high, spectra[:, 0:SIDE], NT, preferred_element_type=F32
    ) + lax.dot_general(ctf_low, spectra[:, 0:SIDE], NT, preferred_element_type=F32)
    picked = lax.dot_general(
        picks, ref_norm, TN, precision=lax.Precision.HIGHEST, preferred_element_type=F32
    )
    picked_high = picked.astype(BF16).astype(F32)
    wide_norm = jnp.broadcast_to(part_norm, (PARTICLES_HERE, ALL_CLASSES))
    wide_high = wide_norm.astype(BF16).astype(F32)
    norm_rows[0] = picked_high
    norm_rows[1] = picked - picked_high
    norm_rows[2] = wide_high
    norm_rows[3] = wide_norm - wide_high
    sub = lax.broadcasted_iota(jnp.int32, (8, ALL_CLASSES), 0)

    def z_group(step):
        return (q + 1 + step) % GROUPS

    def y_rows_of(group, y_to):
        return pl.ds(pl.multiple_of(group * GROUP_ROWS + y_to * Y_ROWS, Y_ROWS), Y_ROWS)

    def y_half_of(group, y_to, half):
        start = group * GROUP_ROWS + y_to * Y_ROWS + half * PAIR_ROWS
        return pl.ds(pl.multiple_of(start, PAIR_ROWS), PAIR_ROWS)

    def correlate(step):
        group = z_group(step)
        rows = pl.ds(pl.multiple_of(group * GROUP_ROWS, GROUP_ROWS), GROUP_ROWS)
        partial_f[...] = lax.dot_general(
            turned[rows, SIDE:], mixed[...], NT, preferred_element_type=F32
        )

        def patch(pair, carry):
            pieces = []
            for e in range(2):
                start = pl.multiple_of(pair * PAIR_ROWS + e * TURN_ROWS, 8)
                pieces.append(partial_f[pl.ds(start, 32), :])
                last = partial_f[pl.ds(start + 32, 8), :]
                particle = group * 16 + pair * 2 + e
                for n in range(4):
                    last = jnp.where(sub == 4 + n, norm_rows[n, pl.ds(particle, 1), :], last)
                pieces.append(last)
            start = pl.multiple_of(group * GROUP_ROWS + pair * PAIR_ROWS, 16)
            partial[pl.ds(start, PAIR_ROWS), :] = jnp.concatenate(pieces, axis=0).astype(BF16)
            return carry

        lax.fori_loop(0, NY * 2, patch, 0)
        for way in range(2):
            start_copy(
                partial.at[y_half_of(group, (y + 2) % NY, way), :],
                far_in.at[step, way], fs.at[step, way], fr.at[step, way], y_peer(steps[way]),
            )
        for way in range(2):
            start_copy(
                partial.at[y_half_of(group, (y + steps[way]) % NY, 1 - way), :],
                near_in.at[step, way, 1 - way],
                ns.at[step, way, 1 - way], nr.at[step, way, 1 - way], y_peer(steps[way]),
            )

    odd_row = sub % 2 == 1

    def product_rounded(total):
        pieces = []
        for e in range(2):
            start = e * TURN_ROWS
            pieces.append(total[start : start + 32, :])
            last = total[start + 32 : start + 40, :]
            whole = last + pltpu.roll(last, 7, 0)
            high = whole.astype(BF16).astype(F32)
            low = pltpu.roll(whole - high, 1, 0)
            pieces.append(jnp.where(sub < 4, last, jnp.where(odd_row, low, high)))
        return jnp.concatenate(pieces, axis=0).astype(BF16)

    def relay(step):
        group = z_group(step)
        for way in range(2):
            own = partial.at[y_half_of(group, (y + steps[way]) % NY, way), :]
            remote(
                own, far_in.at[step, way], fs.at[step, way], fr.at[step, way], y_peer(steps[way])
            ).wait_recv()
            near_out[step, way] = product_rounded(
                own[...].astype(F32) + far_in[step, way].astype(F32)
            )
            start_copy(
                near_out.at[step, way], near_in.at[step, way, way],
                ns.at[step, way, way], nr.at[step, way, way], y_peer(steps[way]),
            )

    def reduce_y(step):
        group = z_group(step)
        for half in range(2):
            own = partial.at[y_half_of(group, y, half), :]
            total = own[...].astype(F32)
            for way in range(2):
                remote(
                    own, near_in.at[step, way, half],
                    ns.at[step, way, half], nr.at[step, way, half], y_peer(steps[way]),
                ).wait_recv()
                total += near_in[step, way, half].astype(F32)
            z_out[step, half * PAIR_ROWS : (half + 1) * PAIR_ROWS, :] = product_rounded(total)

        @pl.when(step < GROUPS - 1)
        def _():
            start_copy(
                z_out.at[step], z_in.at[step], zs.at[step], zr.at[step], q_peer(group)
            )

    def product_step(step, carry):
        pl.when(step < GROUPS)(lambda: correlate(step))
        pl.when((step > 0) & (step <= GROUPS))(lambda: relay(step - 1))
        pl.when(step > 1)(lambda: reduce_y(step - 2))
        return carry

    lax.fori_loop(0, GROUPS + 2, product_step, 0)

    total = z_out[GROUPS - 1].astype(F32)
    for n in range(GROUPS - 1):
        remote(z_out.at[n], z_in.at[n], zs.at[n], zr.at[n], z_pair).wait_recv()
        total += z_in[n].astype(F32)
    for half in range(2):
        rows = slice(half * PAIR_ROWS, (half + 1) * PAIR_ROWS)
        pair_out[rows, :] = product_rounded(total[rows, :])
    send(pair_out, pair_in, zps, zpr, z_pair)
    sums[...] = jnp.zeros_like(sums)
    remote(pair_out, pair_in, zps, zpr, z_pair).wait_recv()
    mine = total + pair_in[...].astype(F32)

    shape = (TURN_ROWS, ALL_CLASSES)
    valid = (lax.broadcasted_iota(jnp.int32, shape, 0) < ANGLES) & (
        lax.broadcasted_iota(jnp.int32, shape, 1) % BLOCK < CLASSES_HERE
    )
    products = walsh(mine, walsh_ref) * (1.0 / ALL_CLASSES)
    pieces = []
    for e in range(4):
        rows = mine[e * TURN_ROWS : (e + 1) * TURN_ROWS, :]
        ref_row = rows[36:37, :] + rows[37:38, :]
        part_row = rows[38:39, :] + rows[39:40, :]
        scaling = lax.rsqrt(part_row + EPSILON) * lax.rsqrt(ref_row + EPSILON)
        scores = jnp.where(
            valid, SHARPNESS * products[e * TURN_ROWS : (e + 1) * TURN_ROWS, :] * scaling, 0.0
        )
        raised = jnp.where(valid, jnp.exp(scores), 0.0)
        total = jnp.sum(jnp.sum(raised, axis=0, keepdims=True), axis=1, keepdims=True)
        pieces.append(raised / total)

    group_rows = weights.at[y_rows_of(q, y), :]
    group_rows[...] = jnp.concatenate(pieces, axis=0).astype(BF16)
    for d in (1, 3, 2):
        send(group_rows, group_rows, wzs.at[d], wzr.at[d], q_peer((q + d) % 4))

    def w_group(step):
        return (q + GROUPS - step) % GROUPS

    def spread(step):
        group = w_group(step)
        rows = weights.at[y_rows_of(group, y), :]

        @pl.when(step > 0)
        def _():
            remote(rows, rows, wzs.at[step], wzr.at[step], z_pair).wait_recv()

        for way in range(2):
            start_copy(rows, rows, wys.at[step, way], wyr.at[step, way], y_peer(steps[way]))

    def pass_on(step):
        group = w_group(step)
        for way in range(2):
            y_of = (y + NY - steps[way]) % NY
            rows = weights.at[y_rows_of(group, y_of), :]
            remote(
                rows, rows, wys.at[step, way], wyr.at[step, way], y_peer(steps[way])
            ).wait_recv()
            half = weights.at[y_half_of(group, y_of, way), :]
            start_copy(half, half, wfs.at[step, way], wfr.at[step, way], y_peer(steps[way]))

    def add_group(step):
        group = w_group(step)
        for way in range(2):
            half = weights.at[y_half_of(group, (y + 2) % NY, way), :]
            remote(
                half, half, wfs.at[step, way], wfr.at[step, way], y_peer(steps[way])
            ).wait_recv()
        rows = pl.ds(pl.multiple_of(group * GROUP_ROWS, GROUP_ROWS), GROUP_ROWS)
        picked_weights = weights[rows, :].T
        sums[:, 0:SIDE] += lax.dot_general(
            picked_weights, turned[rows, 0:SIDE], NN, preferred_element_type=F32
        )
        for r in range(CYCLES_HERE):
            lanes = slice(SIDE + r * 512, SIDE + (r + 1) * 512)
            sums[:, lanes] += lax.dot_general(
                picked_weights, turned[rows, lanes], NN, preferred_element_type=F32
            )

    def weight_step(step, carry):
        pl.when(step < GROUPS)(lambda: spread(step))
        pl.when((step > 0) & (step <= GROUPS))(lambda: pass_on(step - 1))
        pl.when(step > 1)(lambda: add_group(step - 2))
        return carry

    lax.fori_loop(0, GROUPS + 2, weight_step, 0)

    HALF = BLOCK // 2
    parts = (0, 1)
    part_lanes = (slice(0, SIDE + 1024), slice(SIDE + 1024, ROW_WIDTH))
    widths = (SIDE + 1024, 1024)

    def cut(part, buffer, *index):
        return buffer.at[(part, *index, slice(None), slice(0, widths[part]))]

    def rounded(part, total):
        if part == 1:
            return total.astype(BF16)
        whole = total[:, 0:SIDE]
        half_lane = lax.broadcasted_iota(jnp.int32, whole.shape, 1)
        whole = whole + pltpu.roll(whole, SIDE - CYCLES_HERE, 1)
        high = whole.astype(BF16).astype(F32)
        low = pltpu.roll(whole - high, CYCLES_HERE, 1)
        side = jnp.where(half_lane < CYCLES_HERE, high, jnp.where(half_lane < 2 * CYCLES_HERE, low, 0.0))
        return jnp.concatenate([side, total[:, SIDE:]], axis=1).astype(BF16)

    for part in parts:
        out_buf, in_buf = cut(part, core_out), cut(part, core_in)
        for d in range(NX):
            out_buf[d * BLOCK : (d + 1) * BLOCK, :] = rounded(
                part, sums[class_rows(d, other), part_lanes[part]]
            )
        send(out_buf, in_buf, cs.at[part], cr.at[part], sibling)

    def core_sum(part, x_to, half):
        start = pl.multiple_of(x_to * BLOCK + half * HALF, HALF)
        return (
            sums[half_rows(x_to, core, half), part_lanes[part]]
            + core_in[part, pl.ds(start, HALF), 0 : widths[part]].astype(F32)
        )

    for part in parts:
        remote(
            cut(part, core_out), cut(part, core_in), cs.at[part], cr.at[part], sibling
        ).wait_recv()
        for way in range(2):
            far = cut(part, xfar_out, way)
            far[...] = rounded(part, core_sum(part, (x + 2) % NX, way))
            send(
                far, cut(part, xfar_in, way), xfs.at[part, way], xfr.at[part, way],
                x_peer(steps[way]),
            )
        for way in range(2):
            near = cut(part, xnear_out, way, 1 - way)
            near[...] = rounded(part, core_sum(part, (x + steps[way]) % NX, 1 - way))
            send(
                near, cut(part, xnear_in, way, 1 - way),
                xns.at[part, way, 1 - way], xnr.at[part, way, 1 - way], x_peer(steps[way]),
            )

    for part in parts:
        for way in range(2):
            far = cut(part, xfar_in, way)
            remote(
                cut(part, xfar_out, way), far, xfs.at[part, way], xfr.at[part, way],
                x_peer(steps[way]),
            ).wait_recv()
            near = cut(part, xnear_out, way, way)
            near[...] = rounded(
                part, core_sum(part, (x + steps[way]) % NX, way) + far[...].astype(F32)
            )
            send(
                near, cut(part, xnear_in, way, way),
                xns.at[part, way, way], xnr.at[part, way, way], x_peer(steps[way]),
            )

    for part in parts:
        for half in range(2):
            total = core_sum(part, x, half)
            for way in range(2):
                near = cut(part, xnear_in, way, half)
                remote(
                    cut(part, xnear_out, way, half), near,
                    xns.at[part, way, half], xnr.at[part, way, half], x_peer(steps[way]),
                ).wait_recv()
                total += near[...].astype(F32)
            out_buf = cut(part, rep_out, half)
            out_buf[...] = rounded(part, total)
            send(
                out_buf, cut(part, rep_via, half),
                p1s.at[part, half], p1r.at[part, half], via[half],
            )

    for part in parts:
        for half in range(2):
            via_buf = cut(part, rep_via, half)
            remote(
                cut(part, rep_out, half), via_buf,
                p1s.at[part, half], p1r.at[part, half], via[half],
            ).wait_recv()
            send(
                via_buf, cut(part, rep_in, half), p2s.at[part, half], p2r.at[part, half], via[half]
            )

    density = None
    for part in parts:
        halves = []
        for half in range(2):
            in_buf = cut(part, rep_in, half)
            remote(
                cut(part, rep_via, half), in_buf,
                p2s.at[part, half], p2r.at[part, half], via[half],
            ).wait_recv()
            halves.append(cut(part, rep_out, half)[...].astype(F32) + in_buf[...].astype(F32))
        total = jnp.concatenate(halves, axis=0)
        if part == 0:
            density = total[:, 0:SIDE]
            total = total[:, SIDE:]
        flipped = []
        for n in range(2):
            r = part * 2 + n
            whole = density[:, r : r + 1] + density[:, r + 4 : r + 5]
            piece = total[:, n * 512 : (n + 1) * 512] / (whole + PRIOR_WEIGHT)
            flipped.append(jnp.concatenate([piece[:, 0:256], -piece[:, 256:512]], axis=1))
        result = dft(jnp.concatenate(flipped, axis=0), high_ref, low_ref)
        for n in range(2):
            for p in range(2):
                for h in range(2):
                    lanes = slice(p * 256 + h * 128, p * 256 + h * 128 + 128)
                    piece = result[n * BLOCK : (n + 1) * BLOCK, lanes]
                    start = (part * 2 + n) * 4 + h * 2 + p
                    padded[pl.ds(start, BLOCK, stride=16), :] = piece if p == 0 else -piece
    out_ref[...] = padded[0 : CLASSES_HERE * 16, :]

    for copy in sent:
        copy.wait_send()

    def drain(step, carry):
        for way in range(2):
            piece = near_out.at[step, way]
            remote(piece, piece, fs.at[step, way], fr.at[step, way], z_pair).wait_send()
            for half in range(2):
                remote(
                    piece, piece, ns.at[step, way, half], nr.at[step, way, half], z_pair
                ).wait_send()
            rows = weights.at[0:Y_ROWS, :]
            remote(rows, rows, wys.at[step, way], wyr.at[step, way], z_pair).wait_send()
            half = weights.at[0:PAIR_ROWS, :]
            remote(half, half, wfs.at[step, way], wfr.at[step, way], z_pair).wait_send()

        @pl.when(step < GROUPS - 1)
        def _():
            remote(z_out.at[step], z_in.at[step], zs.at[step], zr.at[step], z_pair).wait_send()

        return carry

    lax.fori_loop(0, GROUPS, drain, 0)


def to_rows(values):
    count = values.shape[0]
    return values.reshape(count, CYCLES_HERE, 2, 2, 128).transpose(0, 1, 3, 2, 4).reshape(count * 16, 128)


def from_rows(rows):
    return (
        rows.reshape(CLASSES_HERE, CYCLES_HERE, 2, 2, 128)
        .transpose(0, 1, 3, 2, 4)
        .reshape(CLASSES_HERE, CYCLES_HERE, 2, 256)
    )


def per_device(particles, references, ctf_table, defocus_ids, rotation_ids):
    vmem = pl.BlockSpec(memory_space=pltpu.VMEM)
    dma = pltpu.SemaphoreType.DMA
    out = pl.pallas_call(
        body,
        out_shape=jax.ShapeDtypeStruct((CLASSES_HERE * 16, 128), F32),
        in_specs=[pl.BlockSpec(memory_space=pl.ANY)] * 7,
        out_specs=vmem,
        scratch_shapes=[
            pltpu.VMEM((PARTICLES_HERE * 16, 128), F32),
            pltpu.VMEM((CLASSES_HERE * 16, 128), F32),
            pltpu.VMEM((512, 512), F32),
            pltpu.VMEM((ALL_CLASSES, ALL_CLASSES), F32),
            pltpu.VMEM((CYCLES_HERE, DEFOCI), F32),
            pltpu.VMEM((1, PARTICLES_HERE), jnp.int32),
            pltpu.VMEM((1, ANGLES), jnp.int32),
            pltpu.VMEM((512, 512), BF16),
            pltpu.VMEM((512, 512), BF16),
            pltpu.VMEM((ALL_CLASSES, ALL_CLASSES), BF16),
            pltpu.VMEM((DEFOCI, 128), F32),
            pltpu.VMEM((2 * TURN_ROWS, SAMPLES), F32),
            pltpu.VMEM((BLOCK * 16, 128), F32),
            pltpu.VMEM((CYCLES_HERE * PARTICLES_HERE, 512), F32),
            pltpu.VMEM((CYCLES_HERE * BLOCK, 512), F32),
            pltpu.VMEM((ALL_CLASSES, ROW_WIDTH), BF16),
            pltpu.VMEM((ALL_CLASSES, ROW_WIDTH - SIDE), BF16),
            pltpu.VMEM((PARTICLES_HERE, ROW_WIDTH - SIDE), F32),
            pltpu.VMEM((PARTICLES_HERE, 128), F32),
            pltpu.VMEM((4, PARTICLES_HERE, ALL_CLASSES), F32),
            pltpu.VMEM((ALL_ROWS, ROW_WIDTH), BF16),
            pltpu.VMEM((GROUP_ROWS, ALL_CLASSES), F32),
            pltpu.VMEM((ALL_ROWS, ALL_CLASSES), BF16),
            pltpu.VMEM((GROUPS, 2, PAIR_ROWS, ALL_CLASSES), BF16),
            pltpu.VMEM((GROUPS, 2, 2, PAIR_ROWS, ALL_CLASSES), BF16),
            pltpu.VMEM((GROUPS, 2, PAIR_ROWS, ALL_CLASSES), BF16),
            pltpu.VMEM((GROUPS, Y_ROWS, ALL_CLASSES), BF16),
            pltpu.VMEM((GROUPS - 1, Y_ROWS, ALL_CLASSES), BF16),
            pltpu.VMEM((Y_ROWS, ALL_CLASSES), BF16),
            pltpu.VMEM((Y_ROWS, ALL_CLASSES), BF16),
            pltpu.VMEM((ALL_ROWS, ALL_CLASSES), BF16),
            pltpu.VMEM((ALL_CLASSES, ROW_WIDTH), F32),
            pltpu.VMEM((2, NX * BLOCK, SIDE + 1024), BF16),
            pltpu.VMEM((2, NX * BLOCK, SIDE + 1024), BF16),
            pltpu.VMEM((2, 2, BLOCK // 2, SIDE + 1024), BF16),
            pltpu.VMEM((2, 2, BLOCK // 2, SIDE + 1024), BF16),
            pltpu.VMEM((2, 2, 2, BLOCK // 2, SIDE + 1024), BF16),
            pltpu.VMEM((2, 2, 2, BLOCK // 2, SIDE + 1024), BF16),
            pltpu.VMEM((2, 2, BLOCK // 2, SIDE + 1024), BF16),
            pltpu.VMEM((2, 2, BLOCK // 2, SIDE + 1024), BF16),
            pltpu.VMEM((2, 2, BLOCK // 2, SIDE + 1024), BF16),
            dma((7,)),
            dma((2,)), dma((2,)), dma((2,)), dma((2,)),
            dma((NX,)), dma((NX,)),
            dma((GROUPS, 2)), dma((GROUPS, 2)),
            dma((GROUPS, 2, 2)), dma((GROUPS, 2, 2)),
            dma((GROUPS - 1,)), dma((GROUPS - 1,)),
            dma(()), dma(()),
            dma((GROUPS,)), dma((GROUPS,)),
            dma((GROUPS, 2)), dma((GROUPS, 2)),
            dma((GROUPS, 2)), dma((GROUPS, 2)),
            dma((2,)), dma((2,)),
            dma((2, 2)), dma((2, 2)),
            dma((2, 2, 2)), dma((2, 2, 2)),
            dma((2, 2)), dma((2, 2)), dma((2, 2)), dma((2, 2)),
        ],
        compiler_params=pltpu.CompilerParams(
            collective_id=0, has_side_effects=True, vmem_limit_bytes=56 * 1024 * 1024
        ),
    )(
        to_rows(particles), to_rows(references), jnp.asarray(dft_matrix()), jnp.asarray(walsh_matrix()),
        ctf_table.T, defocus_ids.reshape(1, PARTICLES_HERE), rotation_ids.reshape(1, ANGLES),
    )
    return from_rows(out)


def solution(mesh):
    in_specs = (
        P(("cls", "rep"), "pix", None, None),
        P("cls", "pix", None, None),
        P(None, "pix"),
        P(("cls", "rep")),
        P(),
    )
    out_specs = P("cls", "pix", None, None)
    return jax.shard_map(
        per_device, mesh=mesh, in_specs=in_specs, out_specs=out_specs, check_vma=False
    )
```

```python
import math

import jax
import jax.numpy as jnp
import numpy as np
from jax import lax
from jax.experimental import pallas as pl
from jax.experimental.pallas import tpu as pltpu
from jax.sharding import PartitionSpec as P

TURN_STEPS = 360
DEFOCI = 16
EPSILON = 1e-06
SHARPNESS = 30.0
PRIOR_WEIGHT = 1.0

F32 = jnp.float32
BF16 = jnp.bfloat16
MESH = pl.DeviceIdType.MESH

SAMPLES = 256
ANGLES = 36
TURN_ROWS = 40
PAIR_ROWS = 2 * TURN_ROWS
PARTICLES_HERE = 64
CYCLES_HERE = 4
CLASSES_HERE = 25
BLOCK = 32
NX, NY, NZ = 4, 4, 8
ALL_CLASSES = 2 * NX * BLOCK
SIDE = 128
ROW_WIDTH = SIDE + CYCLES_HERE * 2 * SAMPLES
GROUPS = 4
Y_ROWS = 2 * PAIR_ROWS
GROUP_ROWS = NY * Y_ROWS
ALL_ROWS = GROUPS * GROUP_ROWS

NN = (((1,), (0,)), ((), ()))
NT = (((1,), (1,)), ((), ()))
TN = (((0,), (0,)), ((), ()))


def dft_matrix():
    positions = np.arange(SAMPLES)
    radians = (positions[:, None] * positions[None, :] % SAMPLES) * (2.0 * math.pi / SAMPLES)
    cosine = np.cos(radians) / math.sqrt(SAMPLES)
    sine = np.sin(radians) / math.sqrt(SAMPLES)
    return np.block([[cosine, -sine], [sine, cosine]]).astype(np.float32)


def walsh_matrix():
    matrix = np.ones((1, 1), np.float32)
    while matrix.shape[0] < ALL_CLASSES:
        matrix = np.block([[matrix, matrix], [matrix, -matrix]])
    return matrix


def split(values):
    high = values.astype(BF16)
    return high, (values - high.astype(F32)).astype(BF16)


def walsh(values, walsh_ref):
    high, low = split(values)
    return lax.dot_general(high, walsh_ref[...], NN, preferred_element_type=F32) + lax.dot_general(
        low, walsh_ref[...], NN, preferred_element_type=F32
    )


def dft(values, high_ref, low_ref):
    high, low = split(values)
    return (
        lax.dot_general(high, high_ref[...], NN, preferred_element_type=F32)
        + lax.dot_general(low, high_ref[...], NN, preferred_element_type=F32)
        + lax.dot_general(high, low_ref[...], NN, preferred_element_type=F32)
    )


def body(
    x_hbm, r_hbm, dft_hbm, walsh_hbm, ctf_hbm, ids_hbm, turns_hbm, out_ref,
    x_ref, r_ref, dft_ref, walsh_f, ctf_in, ids_ref, turns_ref,
    high_ref, low_ref, walsh_ref, ctf_ref, phase_ref,
    padded, x_rows, r_rows, spectra, mixed, weighted, power_rows, norm_rows, turned,
    partial_f, partial, far_in, near_in, near_out, z_out, z_in, pair_out, pair_in, weights,
    sums, core_out, core_in, xfar_out, xfar_in, xnear_out, xnear_in, rep_out, rep_via, rep_in,
    in_sem, rx_s, rx_r, rf_s, rf_r, rc_s, rc_r,
    fs, fr, ns, nr, zs, zr, zps, zpr, wzs, wzr, wys, wyr, wfs, wfr,
    cs, cr, xfs, xfr, xns, xnr, p1s, p1r, p2s, p2r,
):
    loads = [
        pltpu.make_async_copy(src, dst, in_sem.at[n])
        for n, (src, dst) in enumerate(
            [
                (r_hbm, r_ref), (dft_hbm, dft_ref), (x_hbm, x_ref), (ids_hbm, ids_ref),
                (turns_hbm, turns_ref), (ctf_hbm, ctf_in), (walsh_hbm, walsh_f),
            ]
        )
    ]
    for load in loads:
        load.start()
    cls = lax.axis_index("cls")
    pix = lax.axis_index("pix")
    rep = lax.axis_index("rep")
    x, core = cls // 2, cls % 2
    z, y = pix // NY, pix % NY
    other = 1 - core
    sibling = {"cls": x * 2 + other}

    def x_peer(d):
        return {"cls": (x + d) % NX * 2 + core}

    def y_peer(d):
        return {"pix": z * NY + (y + d) % NY}

    q, zh = z % 4, z // 4

    def q_peer(q_to):
        return {"pix": (zh * 4 + q_to) * NY + y}

    z_pair = {"pix": (z + 4) % NZ * NY + y}

    far_z = (z + 4) % NZ
    up = (z + 4) // NZ
    via = (
        {"pix": far_z * NY + y, "rep": (rep + up) % 2},
        {"pix": far_z * NY + y, "rep": (rep + 1 - up) % 2},
    )
    partners = (
        [sibling, {"pix": far_z * NY + y, "rep": 1 - rep}]
        + [x_peer(d) for d in (1, 3)]
        + [y_peer(d) for d in (1, 3)]
        + [q_peer((q + d) % 4) for d in range(1, 4)]
        + [z_pair]
    )

    def remote(src, dst, send, recv, device):
        return pltpu.make_async_remote_copy(
            src_ref=src, dst_ref=dst, send_sem=send, recv_sem=recv,
            device_id=device, device_id_type=MESH,
        )

    sent = []

    def start_copy(*args):
        remote(*args).start()

    def send(*args):
        copy = remote(*args)
        copy.start()
        sent.append(copy)

    barrier = pltpu.get_barrier_semaphore()
    for partner in partners:
        pl.semaphore_signal(barrier, inc=1, device_id=partner, device_id_type=MESH)

    loads[0].wait()
    loads[1].wait()
    high, low = split(dft_ref[...])
    high_ref[...] = high
    low_ref[...] = low
    padded[...] = jnp.zeros_like(padded)
    padded[0 : CLASSES_HERE * 16, :] = r_ref[...]
    for r in range(CYCLES_HERE):
        for p in range(2):
            for h in range(2):
                r_rows[r * BLOCK : (r + 1) * BLOCK, p * 256 + h * 128 : p * 256 + h * 128 + 128] = padded[
                    pl.ds(r * 4 + h * 2 + p, BLOCK, stride=16), :
                ]
    own = dft(r_rows[...], high_ref, low_ref).astype(BF16)
    own_rows = pl.ds(pl.multiple_of(cls * BLOCK, BLOCK), BLOCK)
    wide = own.astype(F32)
    power = jnp.sum(wide * wide, axis=1, keepdims=True)
    power_high, power_low = split(power)
    side_lane = lax.broadcasted_iota(jnp.int32, (BLOCK, SIDE), 1)
    side = jnp.zeros((BLOCK, SIDE), F32)
    for r in range(CYCLES_HERE):
        rows = slice(r * BLOCK, (r + 1) * BLOCK)
        spectra[own_rows, SIDE + r * 512 : SIDE + (r + 1) * 512] = own[rows, :]
        side = jnp.where(side_lane == r, power_high.astype(F32)[rows, :], side)
        side = jnp.where(side_lane == CYCLES_HERE + r, power_low.astype(F32)[rows, :], side)
    spectra[own_rows, 0:SIDE] = side.astype(BF16)

    pl.semaphore_wait(barrier, len(partners))
    steps = (1, 3)
    for way in range(2):
        send(
            spectra.at[own_rows, :], spectra.at[own_rows, :],
            rx_s.at[way], rx_r.at[way], x_peer(steps[way]),
        )
    send(spectra.at[own_rows, :], spectra.at[own_rows, :], rc_s.at[0], rc_r.at[0], sibling)

    def class_rows(x_of, core_of):
        return pl.ds(pl.multiple_of((x_of * 2 + core_of) * BLOCK, BLOCK), BLOCK)

    def half_rows(x_of, core_of, half):
        start = (x_of * 2 + core_of) * BLOCK + half * (BLOCK // 2)
        return pl.ds(pl.multiple_of(start, BLOCK // 2), BLOCK // 2)

    for load in loads[2:]:
        load.wait()
    walsh_ref[...] = walsh_f[...].astype(BF16)
    select = (
        lax.broadcasted_iota(jnp.int32, (CYCLES_HERE, 128), 1)
        - lax.broadcasted_iota(jnp.int32, (CYCLES_HERE, 128), 0)
    )
    select = ((select == 0) | (select == CYCLES_HERE)).astype(F32)
    ctf_ref[...] = lax.dot_general(
        ctf_in[...], select, TN, precision=lax.Precision.HIGHEST, preferred_element_type=F32
    )
    shape = (TURN_ROWS, ANGLES)
    on_row = lax.broadcasted_iota(jnp.int32, shape, 0) == lax.broadcasted_iota(jnp.int32, shape, 1)
    turns = jnp.sum(
        jnp.where(on_row, jnp.broadcast_to(turns_ref[...].astype(F32), shape), 0.0),
        axis=1, keepdims=True,
    )
    place = lax.broadcasted_iota(jnp.int32, (TURN_ROWS, SAMPLES), 1)
    signed = jnp.where(place < SAMPLES // 2, place, place - SAMPLES).astype(F32)
    count = turns * signed
    count = count - TURN_STEPS * jnp.floor(count * (1.0 / TURN_STEPS))
    count = jnp.where(count < 0, count + TURN_STEPS, count)
    count = jnp.where(count >= TURN_STEPS, count - TURN_STEPS, count)
    radians = count * (2.0 * math.pi / TURN_STEPS)
    phase_ref[0:TURN_ROWS, :] = jnp.cos(radians)
    phase_ref[TURN_ROWS : 2 * TURN_ROWS, :] = jnp.sin(radians)

    for r in range(CYCLES_HERE):
        for p in range(2):
            for h in range(2):
                x_rows[r * 64 : (r + 1) * 64, p * 256 + h * 128 : p * 256 + h * 128 + 128] = x_ref[
                    pl.ds(r * 4 + h * 2 + p, PARTICLES_HERE, stride=16), :
                ]
    part_square = jnp.zeros((PARTICLES_HERE, 128), F32)
    for r in range(CYCLES_HERE):
        for h in range(4):
            piece = x_rows[r * 64 : (r + 1) * 64, h * 128 : (h + 1) * 128]
            part_square += piece * piece
    part_norm = jnp.sum(part_square, axis=1, keepdims=True)
    picks = (
        lax.broadcasted_iota(jnp.int32, (DEFOCI, PARTICLES_HERE), 0) == ids_ref[...]
    ).astype(F32)
    ctf_rows = lax.dot_general(
        picks, ctf_ref[...], TN, precision=lax.Precision.HIGHEST, preferred_element_type=F32
    )
    particle_spectra = dft(x_rows[...], high_ref, low_ref)
    for r in range(CYCLES_HERE):
        weighted[:, r * 512 : (r + 1) * 512] = (
            ctf_rows[:, r : r + 1] * particle_spectra[r * 64 : (r + 1) * 64, :]
        )
    squared = ctf_rows * ctf_rows
    square_high = squared.astype(BF16).astype(F32)
    lane = lax.broadcasted_iota(jnp.int32, squared.shape, 1)
    power_rows[...] = jnp.where(lane < CYCLES_HERE, square_high, squared - square_high)

    for way in range(2):
        x_of = (x + NX - steps[way]) % NX
        rows = spectra.at[class_rows(x_of, core), :]
        remote(rows, rows, rx_s.at[way], rx_r.at[way], x_peer(steps[way])).wait_recv()
        half = spectra.at[half_rows(x_of, core, way), :]
        send(half, half, rf_s.at[way], rf_r.at[way], x_peer(steps[way]))
        send(rows, rows, rc_s.at[way + 1], rc_r.at[way + 1], sibling)

    cosine = phase_ref[0:TURN_ROWS, :]
    sine = phase_ref[TURN_ROWS : 2 * TURN_ROWS, :]

    def turn_pair(pair, carry):
        rows = pl.ds(pl.multiple_of(pair * PAIR_ROWS, 16), PAIR_ROWS)
        for r in range(CYCLES_HERE):
            real, imag = [], []
            for e in range(2):
                w_re = weighted[pl.ds(pair * 2 + e, 1), r * 512 : r * 512 + 256]
                w_im = weighted[pl.ds(pair * 2 + e, 1), r * 512 + 256 : r * 512 + 512]
                real.append(w_re * cosine - w_im * sine)
                imag.append(w_re * sine + w_im * cosine)
            start = SIDE + r * 512
            turned[rows, start : start + 256] = jnp.concatenate(real, axis=0).astype(BF16)
            turned[rows, start + 256 : start + 512] = jnp.concatenate(imag, axis=0).astype(BF16)
        tail = [
            jnp.broadcast_to(power_rows[pl.ds(pair * 2 + e, 1), :], (TURN_ROWS, 128)) for e in range(2)
        ]
        turned[rows, 0:SIDE] = jnp.concatenate(tail, axis=0).astype(BF16)
        return carry

    lax.fori_loop(0, PARTICLES_HERE // 4, turn_pair, 0)
    x_far = (x + 2) % NX
    for way in range(2):
        half = spectra.at[half_rows(x_far, core, way), :]
        remote(half, half, rf_s.at[way], rf_r.at[way], x_peer(steps[way])).wait_recv()
    rows = spectra.at[class_rows(x_far, core), :]
    send(rows, rows, rc_s.at[3], rc_r.at[3], sibling)
    lax.fori_loop(PARTICLES_HERE // 4, PARTICLES_HERE // 2, turn_pair, 0)

    wide_norm = jnp.broadcast_to(part_norm, (PARTICLES_HERE, ALL_CLASSES))
    wide_high = wide_norm.astype(BF16).astype(F32)
    norm_rows[2] = wide_high
    norm_rows[3] = wide_norm - wide_high
    ctf_high, ctf_low = split(ctf_ref[...] * ctf_ref[...])

    for n, x_of in enumerate((x, (x + 3) % NX, (x + 1) % NX, x_far)):
        rows = spectra.at[class_rows(x_of, other), :]
        remote(rows, rows, rc_s.at[n], rc_r.at[n], sibling).wait_recv()

    for r in range(CYCLES_HERE):
        mixed[:, r * 512 : (r + 1) * 512] = lax.dot_general(
            walsh_ref[...], spectra[:, SIDE + r * 512 : SIDE + (r + 1) * 512], NN,
            preferred_element_type=F32,
        ).astype(BF16)

    ref_norm = lax.dot_general(
        ctf_high, spectra[:, 0:SIDE], NT, preferred_element_type=F32
    ) + lax.dot_general(ctf_low, spectra[:, 0:SIDE], NT, preferred_element_type=F32)
    picked = lax.dot_general(
        picks, ref_norm, TN, precision=lax.Precision.HIGHEST, preferred_element_type=F32
    )
    picked_high = picked.astype(BF16).astype(F32)
    norm_rows[0] = picked_high
    norm_rows[1] = picked - picked_high
    sub = lax.broadcasted_iota(jnp.int32, (8, ALL_CLASSES), 0)

    def z_group(step):
        return (q + 1 + step) % GROUPS

    def y_rows_of(group, y_to):
        return pl.ds(pl.multiple_of(group * GROUP_ROWS + y_to * Y_ROWS, Y_ROWS), Y_ROWS)

    def y_half_of(group, y_to, half):
        start = group * GROUP_ROWS + y_to * Y_ROWS + half * PAIR_ROWS
        return pl.ds(pl.multiple_of(start, PAIR_ROWS), PAIR_ROWS)

    def correlate(step):
        group = z_group(step)
        rows = pl.ds(pl.multiple_of(group * GROUP_ROWS, GROUP_ROWS), GROUP_ROWS)
        partial_f[...] = lax.dot_general(
            turned[rows, SIDE:], mixed[...], NT, preferred_element_type=F32
        )

        def patch(pair, carry):
            pieces = []
            for e in range(2):
                start = pl.multiple_of(pair * PAIR_ROWS + e * TURN_ROWS, 8)
                pieces.append(partial_f[pl.ds(start, 32), :])
                last = partial_f[pl.ds(start + 32, 8), :]
                particle = group * 16 + pair * 2 + e
                for n in range(4):
                    last = jnp.where(sub == 4 + n, norm_rows[n, pl.ds(particle, 1), :], last)
                pieces.append(last)
            start = pl.multiple_of(group * GROUP_ROWS + pair * PAIR_ROWS, 16)
            partial[pl.ds(start, PAIR_ROWS), :] = jnp.concatenate(pieces, axis=0).astype(BF16)
            return carry

        lax.fori_loop(0, NY * 2, patch, 0)
        for way in range(2):
            start_copy(
                partial.at[y_half_of(group, (y + 2) % NY, way), :],
                far_in.at[step, way], fs.at[step, way], fr.at[step, way], y_peer(steps[way]),
            )
        for way in range(2):
            start_copy(
                partial.at[y_half_of(group, (y + steps[way]) % NY, 1 - way), :],
                near_in.at[step, way, 1 - way],
                ns.at[step, way, 1 - way], nr.at[step, way, 1 - way], y_peer(steps[way]),
            )

    odd_row = sub % 2 == 1

    def product_rounded(total):
        pieces = []
        for e in range(2):
            start = e * TURN_ROWS
            pieces.append(total[start : start + 32, :])
            last = total[start + 32 : start + 40, :]
            whole = last + pltpu.roll(last, 7, 0)
            high = whole.astype(BF16).astype(F32)
            low = pltpu.roll(whole - high, 1, 0)
            pieces.append(jnp.where(sub < 4, last, jnp.where(odd_row, low, high)))
        return jnp.concatenate(pieces, axis=0).astype(BF16)

    def relay(step):
        group = z_group(step)
        for way in range(2):
            own = partial.at[y_half_of(group, (y + steps[way]) % NY, way), :]
            remote(
                own, far_in.at[step, way], fs.at[step, way], fr.at[step, way], y_peer(steps[way])
            ).wait_recv()
            near_out[step, way] = product_rounded(
                own[...].astype(F32) + far_in[step, way].astype(F32)
            )
            start_copy(
                near_out.at[step, way], near_in.at[step, way, way],
                ns.at[step, way, way], nr.at[step, way, way], y_peer(steps[way]),
            )

    def reduce_y(step):
        group = z_group(step)
        for half in range(2):
            own = partial.at[y_half_of(group, y, half), :]
            total = own[...].astype(F32)
            for way in range(2):
                remote(
                    own, near_in.at[step, way, half],
                    ns.at[step, way, half], nr.at[step, way, half], y_peer(steps[way]),
                ).wait_recv()
                total += near_in[step, way, half].astype(F32)
            z_out[step, half * PAIR_ROWS : (half + 1) * PAIR_ROWS, :] = product_rounded(total)

        @pl.when(step < GROUPS - 1)
        def _():
            start_copy(
                z_out.at[step], z_in.at[step], zs.at[step], zr.at[step], q_peer(group)
            )

    def product_step(step, carry):
        pl.when(step < GROUPS)(lambda: correlate(step))
        pl.when((step > 0) & (step <= GROUPS))(lambda: relay(step - 1))
        pl.when(step > 1)(lambda: reduce_y(step - 2))
        return carry

    lax.fori_loop(0, GROUPS + 2, product_step, 0)

    total = z_out[GROUPS - 1].astype(F32)
    for n in range(GROUPS - 1):
        remote(z_out.at[n], z_in.at[n], zs.at[n], zr.at[n], z_pair).wait_recv()
        total += z_in[n].astype(F32)
    for half in range(2):
        rows = slice(half * PAIR_ROWS, (half + 1) * PAIR_ROWS)
        pair_out[rows, :] = product_rounded(total[rows, :])
    send(pair_out, pair_in, zps, zpr, z_pair)
    sums[...] = jnp.zeros_like(sums)
    remote(pair_out, pair_in, zps, zpr, z_pair).wait_recv()
    mine = total + pair_in[...].astype(F32)

    shape = (TURN_ROWS, ALL_CLASSES)
    valid = (lax.broadcasted_iota(jnp.int32, shape, 0) < ANGLES) & (
        lax.broadcasted_iota(jnp.int32, shape, 1) % BLOCK < CLASSES_HERE
    )
    products = walsh(mine, walsh_ref) * (1.0 / ALL_CLASSES)
    pieces = []
    for e in range(4):
        rows = mine[e * TURN_ROWS : (e + 1) * TURN_ROWS, :]
        ref_row = rows[36:37, :] + rows[37:38, :]
        part_row = rows[38:39, :] + rows[39:40, :]
        scaling = lax.rsqrt(part_row + EPSILON) * lax.rsqrt(ref_row + EPSILON)
        scores = jnp.where(
            valid, SHARPNESS * products[e * TURN_ROWS : (e + 1) * TURN_ROWS, :] * scaling, 0.0
        )
        raised = jnp.where(valid, jnp.exp(scores), 0.0)
        total = jnp.sum(jnp.sum(raised, axis=0, keepdims=True), axis=1, keepdims=True)
        pieces.append(raised / total)

    group_rows = weights.at[y_rows_of(q, y), :]
    group_rows[...] = jnp.concatenate(pieces, axis=0).astype(BF16)
    for d in (1, 3, 2):
        send(group_rows, group_rows, wzs.at[d], wzr.at[d], q_peer((q + d) % 4))

    def w_group(step):
        return (q + GROUPS - step) % GROUPS

    def spread(step):
        group = w_group(step)
        rows = weights.at[y_rows_of(group, y), :]

        @pl.when(step > 0)
        def _():
            remote(rows, rows, wzs.at[step], wzr.at[step], z_pair).wait_recv()

        for way in range(2):
            start_copy(rows, rows, wys.at[step, way], wyr.at[step, way], y_peer(steps[way]))

    def pass_on(step):
        group = w_group(step)
        for way in range(2):
            y_of = (y + NY - steps[way]) % NY
            rows = weights.at[y_rows_of(group, y_of), :]
            remote(
                rows, rows, wys.at[step, way], wyr.at[step, way], y_peer(steps[way])
            ).wait_recv()
            half = weights.at[y_half_of(group, y_of, way), :]
            start_copy(half, half, wfs.at[step, way], wfr.at[step, way], y_peer(steps[way]))

    def add_group(step):
        group = w_group(step)
        for way in range(2):
            half = weights.at[y_half_of(group, (y + 2) % NY, way), :]
            remote(
                half, half, wfs.at[step, way], wfr.at[step, way], y_peer(steps[way])
            ).wait_recv()
        rows = pl.ds(pl.multiple_of(group * GROUP_ROWS, GROUP_ROWS), GROUP_ROWS)
        picked_weights = weights[rows, :].T
        sums[:, 0:SIDE] += lax.dot_general(
            picked_weights, turned[rows, 0:SIDE], NN, preferred_element_type=F32
        )
        for r in range(CYCLES_HERE):
            lanes = slice(SIDE + r * 512, SIDE + (r + 1) * 512)
            sums[:, lanes] += lax.dot_general(
                picked_weights, turned[rows, lanes], NN, preferred_element_type=F32
            )

    def weight_step(step, carry):
        pl.when(step < GROUPS)(lambda: spread(step))
        pl.when((step > 0) & (step <= GROUPS))(lambda: pass_on(step - 1))
        pl.when(step > 1)(lambda: add_group(step - 2))
        return carry

    lax.fori_loop(0, GROUPS + 2, weight_step, 0)

    HALF = BLOCK // 2
    parts = (0, 1)
    part_lanes = (slice(0, SIDE + 1024), slice(SIDE + 1024, ROW_WIDTH))
    widths = (SIDE + 1024, 1024)

    def cut(part, buffer, *index):
        return buffer.at[(part, *index, slice(None), slice(0, widths[part]))]

    def rounded(part, total):
        if part == 1:
            return total.astype(BF16)
        whole = total[:, 0:SIDE]
        half_lane = lax.broadcasted_iota(jnp.int32, whole.shape, 1)
        whole = whole + pltpu.roll(whole, SIDE - CYCLES_HERE, 1)
        high = whole.astype(BF16).astype(F32)
        low = pltpu.roll(whole - high, CYCLES_HERE, 1)
        side = jnp.where(half_lane < CYCLES_HERE, high, jnp.where(half_lane < 2 * CYCLES_HERE, low, 0.0))
        return jnp.concatenate([side, total[:, SIDE:]], axis=1).astype(BF16)

    for part in parts:
        out_buf, in_buf = cut(part, core_out), cut(part, core_in)
        for d in range(NX):
            out_buf[d * BLOCK : (d + 1) * BLOCK, :] = rounded(
                part, sums[class_rows(d, other), part_lanes[part]]
            )
        send(out_buf, in_buf, cs.at[part], cr.at[part], sibling)

    def core_sum(part, x_to, half):
        start = pl.multiple_of(x_to * BLOCK + half * HALF, HALF)
        return (
            sums[half_rows(x_to, core, half), part_lanes[part]]
            + core_in[part, pl.ds(start, HALF), 0 : widths[part]].astype(F32)
        )

    for part in parts:
        remote(
            cut(part, core_out), cut(part, core_in), cs.at[part], cr.at[part], sibling
        ).wait_recv()
        for way in range(2):
            far = cut(part, xfar_out, way)
            far[...] = rounded(part, core_sum(part, (x + 2) % NX, way))
            send(
                far, cut(part, xfar_in, way), xfs.at[part, way], xfr.at[part, way],
                x_peer(steps[way]),
            )
        for way in range(2):
            near = cut(part, xnear_out, way, 1 - way)
            near[...] = rounded(part, core_sum(part, (x + steps[way]) % NX, 1 - way))
            send(
                near, cut(part, xnear_in, way, 1 - way),
                xns.at[part, way, 1 - way], xnr.at[part, way, 1 - way], x_peer(steps[way]),
            )

    for part in parts:
        for way in range(2):
            far = cut(part, xfar_in, way)
            remote(
                cut(part, xfar_out, way), far, xfs.at[part, way], xfr.at[part, way],
                x_peer(steps[way]),
            ).wait_recv()
            near = cut(part, xnear_out, way, way)
            near[...] = rounded(
                part, core_sum(part, (x + steps[way]) % NX, way) + far[...].astype(F32)
            )
            send(
                near, cut(part, xnear_in, way, way),
                xns.at[part, way, way], xnr.at[part, way, way], x_peer(steps[way]),
            )

    for part in parts:
        for half in range(2):
            total = core_sum(part, x, half)
            for way in range(2):
                near = cut(part, xnear_in, way, half)
                remote(
                    cut(part, xnear_out, way, half), near,
                    xns.at[part, way, half], xnr.at[part, way, half], x_peer(steps[way]),
                ).wait_recv()
                total += near[...].astype(F32)
            out_buf = cut(part, rep_out, half)
            out_buf[...] = rounded(part, total)
            send(
                out_buf, cut(part, rep_via, half),
                p1s.at[part, half], p1r.at[part, half], via[half],
            )

    for part in parts:
        for half in range(2):
            via_buf = cut(part, rep_via, half)
            remote(
                cut(part, rep_out, half), via_buf,
                p1s.at[part, half], p1r.at[part, half], via[half],
            ).wait_recv()
            send(
                via_buf, cut(part, rep_in, half), p2s.at[part, half], p2r.at[part, half], via[half]
            )

    for copy in sent[:-4]:
        copy.wait_send()

    def drain(step, carry):
        for way in range(2):
            piece = near_out.at[step, way]
            remote(piece, piece, fs.at[step, way], fr.at[step, way], z_pair).wait_send()
            for half in range(2):
                remote(
                    piece, piece, ns.at[step, way, half], nr.at[step, way, half], z_pair
                ).wait_send()
            rows = weights.at[0:Y_ROWS, :]
            remote(rows, rows, wys.at[step, way], wyr.at[step, way], z_pair).wait_send()
            half = weights.at[0:PAIR_ROWS, :]
            remote(half, half, wfs.at[step, way], wfr.at[step, way], z_pair).wait_send()

        @pl.when(step < GROUPS - 1)
        def _():
            remote(z_out.at[step], z_in.at[step], zs.at[step], zr.at[step], z_pair).wait_send()

        return carry

    lax.fori_loop(0, GROUPS, drain, 0)

    density = None
    for part in parts:
        halves = []
        for half in range(2):
            in_buf = cut(part, rep_in, half)
            remote(
                cut(part, rep_via, half), in_buf,
                p2s.at[part, half], p2r.at[part, half], via[half],
            ).wait_recv()
            halves.append(cut(part, rep_out, half)[...].astype(F32) + in_buf[...].astype(F32))
        total = jnp.concatenate(halves, axis=0)
        if part == 0:
            density = total[:, 0:SIDE]
            total = total[:, SIDE:]
        flipped = []
        for n in range(2):
            r = part * 2 + n
            whole = density[:, r : r + 1] + density[:, r + 4 : r + 5]
            piece = total[:, n * 512 : (n + 1) * 512] / (whole + PRIOR_WEIGHT)
            flipped.append(jnp.concatenate([piece[:, 0:256], -piece[:, 256:512]], axis=1))
        result = dft(jnp.concatenate(flipped, axis=0), high_ref, low_ref)
        for n in range(2):
            for p in range(2):
                for h in range(2):
                    lanes = slice(p * 256 + h * 128, p * 256 + h * 128 + 128)
                    piece = result[n * BLOCK : (n + 1) * BLOCK, lanes]
                    start = (part * 2 + n) * 4 + h * 2 + p
                    padded[pl.ds(start, BLOCK, stride=16), :] = piece if p == 0 else -piece
    out_ref[...] = padded[0 : CLASSES_HERE * 16, :]

    for copy in sent[-4:]:
        copy.wait_send()


def to_rows(values):
    count = values.shape[0]
    return values.reshape(count, CYCLES_HERE, 2, 2, 128).transpose(0, 1, 3, 2, 4).reshape(count * 16, 128)


def from_rows(rows):
    return (
        rows.reshape(CLASSES_HERE, CYCLES_HERE, 2, 2, 128)
        .transpose(0, 1, 3, 2, 4)
        .reshape(CLASSES_HERE, CYCLES_HERE, 2, 256)
    )


def per_device(particles, references, ctf_table, defocus_ids, rotation_ids):
    vmem = pl.BlockSpec(memory_space=pltpu.VMEM)
    dma = pltpu.SemaphoreType.DMA
    out = pl.pallas_call(
        body,
        out_shape=jax.ShapeDtypeStruct((CLASSES_HERE * 16, 128), F32),
        in_specs=[pl.BlockSpec(memory_space=pl.ANY)] * 7,
        out_specs=vmem,
        scratch_shapes=[
            pltpu.VMEM((PARTICLES_HERE * 16, 128), F32),
            pltpu.VMEM((CLASSES_HERE * 16, 128), F32),
            pltpu.VMEM((512, 512), F32),
            pltpu.VMEM((ALL_CLASSES, ALL_CLASSES), F32),
            pltpu.VMEM((CYCLES_HERE, DEFOCI), F32),
            pltpu.VMEM((1, PARTICLES_HERE), jnp.int32),
            pltpu.VMEM((1, ANGLES), jnp.int32),
            pltpu.VMEM((512, 512), BF16),
            pltpu.VMEM((512, 512), BF16),
            pltpu.VMEM((ALL_CLASSES, ALL_CLASSES), BF16),
            pltpu.VMEM((DEFOCI, 128), F32),
            pltpu.VMEM((2 * TURN_ROWS, SAMPLES), F32),
            pltpu.VMEM((BLOCK * 16, 128), F32),
            pltpu.VMEM((CYCLES_HERE * PARTICLES_HERE, 512), F32),
            pltpu.VMEM((CYCLES_HERE * BLOCK, 512), F32),
            pltpu.VMEM((ALL_CLASSES, ROW_WIDTH), BF16),
            pltpu.VMEM((ALL_CLASSES, ROW_WIDTH - SIDE), BF16),
            pltpu.VMEM((PARTICLES_HERE, ROW_WIDTH - SIDE), F32),
            pltpu.VMEM((PARTICLES_HERE, 128), F32),
            pltpu.VMEM((4, PARTICLES_HERE, ALL_CLASSES), F32),
            pltpu.VMEM((ALL_ROWS, ROW_WIDTH), BF16),
            pltpu.VMEM((GROUP_ROWS, ALL_CLASSES), F32),
            pltpu.VMEM((ALL_ROWS, ALL_CLASSES), BF16),
            pltpu.VMEM((GROUPS, 2, PAIR_ROWS, ALL_CLASSES), BF16),
            pltpu.VMEM((GROUPS, 2, 2, PAIR_ROWS, ALL_CLASSES), BF16),
            pltpu.VMEM((GROUPS, 2, PAIR_ROWS, ALL_CLASSES), BF16),
            pltpu.VMEM((GROUPS, Y_ROWS, ALL_CLASSES), BF16),
            pltpu.VMEM((GROUPS - 1, Y_ROWS, ALL_CLASSES), BF16),
            pltpu.VMEM((Y_ROWS, ALL_CLASSES), BF16),
            pltpu.VMEM((Y_ROWS, ALL_CLASSES), BF16),
            pltpu.VMEM((ALL_ROWS, ALL_CLASSES), BF16),
            pltpu.VMEM((ALL_CLASSES, ROW_WIDTH), F32),
            pltpu.VMEM((2, NX * BLOCK, SIDE + 1024), BF16),
            pltpu.VMEM((2, NX * BLOCK, SIDE + 1024), BF16),
            pltpu.VMEM((2, 2, BLOCK // 2, SIDE + 1024), BF16),
            pltpu.VMEM((2, 2, BLOCK // 2, SIDE + 1024), BF16),
            pltpu.VMEM((2, 2, 2, BLOCK // 2, SIDE + 1024), BF16),
            pltpu.VMEM((2, 2, 2, BLOCK // 2, SIDE + 1024), BF16),
            pltpu.VMEM((2, 2, BLOCK // 2, SIDE + 1024), BF16),
            pltpu.VMEM((2, 2, BLOCK // 2, SIDE + 1024), BF16),
            pltpu.VMEM((2, 2, BLOCK // 2, SIDE + 1024), BF16),
            dma((7,)),
            dma((2,)), dma((2,)), dma((2,)), dma((2,)),
            dma((NX,)), dma((NX,)),
            dma((GROUPS, 2)), dma((GROUPS, 2)),
            dma((GROUPS, 2, 2)), dma((GROUPS, 2, 2)),
            dma((GROUPS - 1,)), dma((GROUPS - 1,)),
            dma(()), dma(()),
            dma((GROUPS,)), dma((GROUPS,)),
            dma((GROUPS, 2)), dma((GROUPS, 2)),
            dma((GROUPS, 2)), dma((GROUPS, 2)),
            dma((2,)), dma((2,)),
            dma((2, 2)), dma((2, 2)),
            dma((2, 2, 2)), dma((2, 2, 2)),
            dma((2, 2)), dma((2, 2)), dma((2, 2)), dma((2, 2)),
        ],
        compiler_params=pltpu.CompilerParams(
            collective_id=0, has_side_effects=True, vmem_limit_bytes=56 * 1024 * 1024
        ),
    )(
        to_rows(particles), to_rows(references), jnp.asarray(dft_matrix()), jnp.asarray(walsh_matrix()),
        ctf_table.T, defocus_ids.reshape(1, PARTICLES_HERE), rotation_ids.reshape(1, ANGLES),
    )
    return from_rows(out)


def solution(mesh):
    in_specs = (
        P(("cls", "rep"), "pix", None, None),
        P("cls", "pix", None, None),
        P(None, "pix"),
        P(("cls", "rep")),
        P(),
    )
    out_specs = P("cls", "pix", None, None)
    return jax.shard_map(
        per_device, mesh=mesh, in_specs=in_specs, out_specs=out_specs, check_vma=False
    )
```

```python
import math

import jax
import jax.numpy as jnp
import numpy as np
from jax import lax
from jax.experimental import pallas as pl
from jax.experimental.pallas import tpu as pltpu
from jax.sharding import PartitionSpec as P

TURN_STEPS = 360
DEFOCI = 16
EPSILON = 1e-06
SHARPNESS = 30.0
PRIOR_WEIGHT = 1.0

F32 = jnp.float32
BF16 = jnp.bfloat16
MESH = pl.DeviceIdType.MESH

SAMPLES = 256
ANGLES = 36
TURN_ROWS = 40
PAIR_ROWS = 2 * TURN_ROWS
PARTICLES_HERE = 64
CYCLES_HERE = 4
CLASSES_HERE = 25
BLOCK = 32
NX, NY, NZ = 4, 4, 8
ALL_CLASSES = 2 * NX * BLOCK
SIDE = 128
ROW_WIDTH = SIDE + CYCLES_HERE * 2 * SAMPLES
GROUPS = 4
Y_ROWS = 2 * PAIR_ROWS
GROUP_ROWS = NY * Y_ROWS
ALL_ROWS = GROUPS * GROUP_ROWS

NN = (((1,), (0,)), ((), ()))
NT = (((1,), (1,)), ((), ()))
TN = (((0,), (0,)), ((), ()))


def dft_matrix():
    positions = np.arange(SAMPLES)
    radians = (positions[:, None] * positions[None, :] % SAMPLES) * (2.0 * math.pi / SAMPLES)
    cosine = np.cos(radians) / math.sqrt(SAMPLES)
    sine = np.sin(radians) / math.sqrt(SAMPLES)
    return np.block([[cosine, -sine], [sine, cosine]]).astype(np.float32)


def walsh_matrix():
    matrix = np.ones((1, 1), np.float32)
    while matrix.shape[0] < ALL_CLASSES:
        matrix = np.block([[matrix, matrix], [matrix, -matrix]])
    return matrix


def split(values):
    high = values.astype(BF16)
    return high, (values - high.astype(F32)).astype(BF16)


def walsh(values, walsh_ref):
    high, low = split(values)
    return lax.dot_general(high, walsh_ref[...], NN, preferred_element_type=F32) + lax.dot_general(
        low, walsh_ref[...], NN, preferred_element_type=F32
    )


def dft(values, high_ref, low_ref):
    high, low = split(values)
    return (
        lax.dot_general(high, high_ref[...], NN, preferred_element_type=F32)
        + lax.dot_general(low, high_ref[...], NN, preferred_element_type=F32)
        + lax.dot_general(high, low_ref[...], NN, preferred_element_type=F32)
    )


def body(
    x_hbm, r_hbm, dft_hbm, walsh_hbm, ctf_hbm, ids_hbm, turns_hbm, out_ref,
    x_ref, r_ref, dft_ref, walsh_f, ctf_in, ids_ref, turns_ref,
    high_ref, low_ref, walsh_ref, ctf_ref, phase_ref,
    padded, x_rows, r_rows, spectra, mixed, weighted, power_rows, norm_rows, turned,
    partial_f, partial, far_in, near_in, near_out, z_out, z_in, pair_out, pair_in, weights,
    sums, core_out, core_in, xfar_out, xfar_in, xnear_out, xnear_in, rep_out, rep_via, rep_in,
    in_sem, rx_s, rx_r, rf_s, rf_r, rc_s, rc_r,
    fs, fr, ns, nr, zs, zr, zps, zpr, wzs, wzr, wys, wyr, wfs, wfr,
    cs, cr, xfs, xfr, xns, xnr, p1s, p1r, p2s, p2r,
):
    loads = [
        pltpu.make_async_copy(src, dst, in_sem.at[n])
        for n, (src, dst) in enumerate(
            [
                (r_hbm, r_ref), (dft_hbm, dft_ref), (x_hbm, x_ref), (ids_hbm, ids_ref),
                (turns_hbm, turns_ref), (ctf_hbm, ctf_in), (walsh_hbm, walsh_f),
            ]
        )
    ]
    for load in loads:
        load.start()
    cls = lax.axis_index("cls")
    pix = lax.axis_index("pix")
    rep = lax.axis_index("rep")
    x, core = cls // 2, cls % 2
    z, y = pix // NY, pix % NY
    other = 1 - core
    sibling = {"cls": x * 2 + other}

    def x_peer(d):
        return {"cls": (x + d) % NX * 2 + core}

    def y_peer(d):
        return {"pix": z * NY + (y + d) % NY}

    q, zh = z % 4, z // 4

    def q_peer(q_to):
        return {"pix": (zh * 4 + q_to) * NY + y}

    z_pair = {"pix": (z + 4) % NZ * NY + y}

    far_z = (z + 4) % NZ
    up = (z + 4) // NZ
    via = (
        {"pix": far_z * NY + y, "rep": (rep + up) % 2},
        {"pix": far_z * NY + y, "rep": (rep + 1 - up) % 2},
    )
    partners = (
        [sibling, {"pix": far_z * NY + y, "rep": 1 - rep}]
        + [x_peer(d) for d in (1, 3)]
        + [y_peer(d) for d in (1, 3)]
        + [q_peer((q + d) % 4) for d in range(1, 4)]
        + [z_pair]
    )

    def remote(src, dst, send, recv, device):
        return pltpu.make_async_remote_copy(
            src_ref=src, dst_ref=dst, send_sem=send, recv_sem=recv,
            device_id=device, device_id_type=MESH,
        )

    sent = []

    def start_copy(*args):
        remote(*args).start()

    def send(*args):
        copy = remote(*args)
        copy.start()
        sent.append(copy)

    barrier = pltpu.get_barrier_semaphore()
    for partner in partners:
        pl.semaphore_signal(barrier, inc=1, device_id=partner, device_id_type=MESH)

    loads[0].wait()
    loads[1].wait()
    high, low = split(dft_ref[...])
    high_ref[...] = high
    low_ref[...] = low
    padded[...] = jnp.zeros_like(padded)
    padded[0 : CLASSES_HERE * 16, :] = r_ref[...]
    for r in range(CYCLES_HERE):
        for p in range(2):
            for h in range(2):
                r_rows[r * BLOCK : (r + 1) * BLOCK, p * 256 + h * 128 : p * 256 + h * 128 + 128] = padded[
                    pl.ds(r * 4 + h * 2 + p, BLOCK, stride=16), :
                ]
    own = dft(r_rows[...], high_ref, low_ref).astype(BF16)
    own_rows = pl.ds(pl.multiple_of(cls * BLOCK, BLOCK), BLOCK)
    wide = own.astype(F32)
    power = jnp.sum(wide * wide, axis=1, keepdims=True)
    power_high, power_low = split(power)
    side_lane = lax.broadcasted_iota(jnp.int32, (BLOCK, SIDE), 1)
    side = jnp.zeros((BLOCK, SIDE), F32)
    for r in range(CYCLES_HERE):
        rows = slice(r * BLOCK, (r + 1) * BLOCK)
        spectra[own_rows, SIDE + r * 512 : SIDE + (r + 1) * 512] = own[rows, :]
        side = jnp.where(side_lane == r, power_high.astype(F32)[rows, :], side)
        side = jnp.where(side_lane == CYCLES_HERE + r, power_low.astype(F32)[rows, :], side)
    spectra[own_rows, 0:SIDE] = side.astype(BF16)

    pl.semaphore_wait(barrier, len(partners))
    steps = (1, 3)
    for way in range(2):
        send(
            spectra.at[own_rows, :], spectra.at[own_rows, :],
            rx_s.at[way], rx_r.at[way], x_peer(steps[way]),
        )
    send(spectra.at[own_rows, :], spectra.at[own_rows, :], rc_s.at[0], rc_r.at[0], sibling)

    def class_rows(x_of, core_of):
        return pl.ds(pl.multiple_of((x_of * 2 + core_of) * BLOCK, BLOCK), BLOCK)

    def half_rows(x_of, core_of, half):
        start = (x_of * 2 + core_of) * BLOCK + half * (BLOCK // 2)
        return pl.ds(pl.multiple_of(start, BLOCK // 2), BLOCK // 2)

    for load in loads[2:]:
        load.wait()
    walsh_ref[...] = walsh_f[...].astype(BF16)
    select = (
        lax.broadcasted_iota(jnp.int32, (CYCLES_HERE, 128), 1)
        - lax.broadcasted_iota(jnp.int32, (CYCLES_HERE, 128), 0)
    )
    select = ((select == 0) | (select == CYCLES_HERE)).astype(F32)
    ctf_ref[...] = lax.dot_general(
        ctf_in[...], select, TN, precision=lax.Precision.HIGHEST, preferred_element_type=F32
    )
    shape = (TURN_ROWS, ANGLES)
    on_row = lax.broadcasted_iota(jnp.int32, shape, 0) == lax.broadcasted_iota(jnp.int32, shape, 1)
    turns = jnp.sum(
        jnp.where(on_row, jnp.broadcast_to(turns_ref[...].astype(F32), shape), 0.0),
        axis=1, keepdims=True,
    )
    place = lax.broadcasted_iota(jnp.int32, (TURN_ROWS, SAMPLES), 1)
    signed = jnp.where(place < SAMPLES // 2, place, place - SAMPLES).astype(F32)
    count = turns * signed
    count = count - TURN_STEPS * jnp.floor(count * (1.0 / TURN_STEPS))
    count = jnp.where(count < 0, count + TURN_STEPS, count)
    count = jnp.where(count >= TURN_STEPS, count - TURN_STEPS, count)
    radians = count * (2.0 * math.pi / TURN_STEPS)
    phase_ref[0:TURN_ROWS, :] = jnp.cos(radians)
    phase_ref[TURN_ROWS : 2 * TURN_ROWS, :] = jnp.sin(radians)

    for r in range(CYCLES_HERE):
        for p in range(2):
            for h in range(2):
                x_rows[r * 64 : (r + 1) * 64, p * 256 + h * 128 : p * 256 + h * 128 + 128] = x_ref[
                    pl.ds(r * 4 + h * 2 + p, PARTICLES_HERE, stride=16), :
                ]
    part_square = jnp.zeros((PARTICLES_HERE, 128), F32)
    for r in range(CYCLES_HERE):
        for h in range(4):
            piece = x_rows[r * 64 : (r + 1) * 64, h * 128 : (h + 1) * 128]
            part_square += piece * piece
    part_norm = jnp.sum(part_square, axis=1, keepdims=True)
    picks = (
        lax.broadcasted_iota(jnp.int32, (DEFOCI, PARTICLES_HERE), 0) == ids_ref[...]
    ).astype(F32)
    ctf_rows = lax.dot_general(
        picks, ctf_ref[...], TN, precision=lax.Precision.HIGHEST, preferred_element_type=F32
    )
    particle_spectra = dft(x_rows[...], high_ref, low_ref)
    for r in range(CYCLES_HERE):
        weighted[:, r * 512 : (r + 1) * 512] = (
            ctf_rows[:, r : r + 1] * particle_spectra[r * 64 : (r + 1) * 64, :]
        )
    squared = ctf_rows * ctf_rows
    square_high = squared.astype(BF16).astype(F32)
    lane = lax.broadcasted_iota(jnp.int32, squared.shape, 1)
    power_rows[...] = jnp.where(lane < CYCLES_HERE, square_high, squared - square_high)

    for way in range(2):
        x_of = (x + NX - steps[way]) % NX
        rows = spectra.at[class_rows(x_of, core), :]
        remote(rows, rows, rx_s.at[way], rx_r.at[way], x_peer(steps[way])).wait_recv()
        half = spectra.at[half_rows(x_of, core, way), :]
        send(half, half, rf_s.at[way], rf_r.at[way], x_peer(steps[way]))
        send(rows, rows, rc_s.at[way + 1], rc_r.at[way + 1], sibling)

    cosine = phase_ref[0:TURN_ROWS, :]
    sine = phase_ref[TURN_ROWS : 2 * TURN_ROWS, :]

    def turn_pair(pair, carry):
        rows = pl.ds(pl.multiple_of(pair * PAIR_ROWS, 16), PAIR_ROWS)
        for r in range(CYCLES_HERE):
            real, imag = [], []
            for e in range(2):
                w_re = weighted[pl.ds(pair * 2 + e, 1), r * 512 : r * 512 + 256]
                w_im = weighted[pl.ds(pair * 2 + e, 1), r * 512 + 256 : r * 512 + 512]
                real.append(w_re * cosine - w_im * sine)
                imag.append(w_re * sine + w_im * cosine)
            start = SIDE + r * 512
            turned[rows, start : start + 256] = jnp.concatenate(real, axis=0).astype(BF16)
            turned[rows, start + 256 : start + 512] = jnp.concatenate(imag, axis=0).astype(BF16)
        tail = [
            jnp.broadcast_to(power_rows[pl.ds(pair * 2 + e, 1), :], (TURN_ROWS, 128)) for e in range(2)
        ]
        turned[rows, 0:SIDE] = jnp.concatenate(tail, axis=0).astype(BF16)
        return carry

    lax.fori_loop(0, PARTICLES_HERE // 4, turn_pair, 0)
    x_far = (x + 2) % NX
    for way in range(2):
        half = spectra.at[half_rows(x_far, core, way), :]
        remote(half, half, rf_s.at[way], rf_r.at[way], x_peer(steps[way])).wait_recv()
    rows = spectra.at[class_rows(x_far, core), :]
    send(rows, rows, rc_s.at[3], rc_r.at[3], sibling)
    lax.fori_loop(PARTICLES_HERE // 4, PARTICLES_HERE // 2, turn_pair, 0)

    wide_norm = jnp.broadcast_to(part_norm, (PARTICLES_HERE, ALL_CLASSES))
    wide_high = wide_norm.astype(BF16).astype(F32)
    norm_rows[2] = wide_high
    norm_rows[3] = wide_norm - wide_high
    ctf_high, ctf_low = split(ctf_ref[...] * ctf_ref[...])

    for n, x_of in enumerate((x, (x + 3) % NX, (x + 1) % NX, x_far)):
        rows = spectra.at[class_rows(x_of, other), :]
        remote(rows, rows, rc_s.at[n], rc_r.at[n], sibling).wait_recv()

    for r in range(CYCLES_HERE):
        mixed[:, r * 512 : (r + 1) * 512] = lax.dot_general(
            walsh_ref[...], spectra[:, SIDE + r * 512 : SIDE + (r + 1) * 512], NN,
            preferred_element_type=F32,
        ).astype(BF16)

    ref_norm = lax.dot_general(
        ctf_high, spectra[:, 0:SIDE], NT, preferred_element_type=F32
    ) + lax.dot_general(ctf_low, spectra[:, 0:SIDE], NT, preferred_element_type=F32)
    picked = lax.dot_general(
        picks, ref_norm, TN, precision=lax.Precision.HIGHEST, preferred_element_type=F32
    )
    picked_high = picked.astype(BF16).astype(F32)
    norm_rows[0] = picked_high
    norm_rows[1] = picked - picked_high
    sub = lax.broadcasted_iota(jnp.int32, (8, ALL_CLASSES), 0)

    def z_group(step):
        return (q + 1 + step) % GROUPS

    def y_rows_of(group, y_to):
        return pl.ds(pl.multiple_of(group * GROUP_ROWS + y_to * Y_ROWS, Y_ROWS), Y_ROWS)

    def y_half_of(group, y_to, half):
        start = group * GROUP_ROWS + y_to * Y_ROWS + half * PAIR_ROWS
        return pl.ds(pl.multiple_of(start, PAIR_ROWS), PAIR_ROWS)

    def correlate(step):
        group = z_group(step)
        rows = pl.ds(pl.multiple_of(group * GROUP_ROWS, GROUP_ROWS), GROUP_ROWS)
        partial_f[...] = lax.dot_general(
            turned[rows, SIDE:], mixed[...], NT, preferred_element_type=F32
        )

        def patch(pair, carry):
            pieces = []
            for e in range(2):
                start = pl.multiple_of(pair * PAIR_ROWS + e * TURN_ROWS, 8)
                pieces.append(partial_f[pl.ds(start, 32), :])
                last = partial_f[pl.ds(start + 32, 8), :]
                particle = group * 16 + pair * 2 + e
                for n in range(4):
                    last = jnp.where(sub == 4 + n, norm_rows[n, pl.ds(particle, 1), :], last)
                pieces.append(last)
            start = pl.multiple_of(group * GROUP_ROWS + pair * PAIR_ROWS, 16)
            partial[pl.ds(start, PAIR_ROWS), :] = jnp.concatenate(pieces, axis=0).astype(BF16)
            return carry

        lax.fori_loop(0, NY * 2, patch, 0)
        for way in range(2):
            start_copy(
                partial.at[y_half_of(group, (y + 2) % NY, way), :],
                far_in.at[step, way], fs.at[step, way], fr.at[step, way], y_peer(steps[way]),
            )
        for way in range(2):
            start_copy(
                partial.at[y_half_of(group, (y + steps[way]) % NY, 1 - way), :],
                near_in.at[step, way, 1 - way],
                ns.at[step, way, 1 - way], nr.at[step, way, 1 - way], y_peer(steps[way]),
            )

    odd_row = sub % 2 == 1

    def product_rounded(total):
        pieces = []
        for e in range(2):
            start = e * TURN_ROWS
            pieces.append(total[start : start + 32, :])
            last = total[start + 32 : start + 40, :]
            whole = last + pltpu.roll(last, 7, 0)
            high = whole.astype(BF16).astype(F32)
            low = pltpu.roll(whole - high, 1, 0)
            pieces.append(jnp.where(sub < 4, last, jnp.where(odd_row, low, high)))
        return jnp.concatenate(pieces, axis=0).astype(BF16)

    def relay(step):
        group = z_group(step)
        for way in range(2):
            own = partial.at[y_half_of(group, (y + steps[way]) % NY, way), :]
            remote(
                own, far_in.at[step, way], fs.at[step, way], fr.at[step, way], y_peer(steps[way])
            ).wait_recv()
            near_out[step, way] = product_rounded(
                own[...].astype(F32) + far_in[step, way].astype(F32)
            )
            start_copy(
                near_out.at[step, way], near_in.at[step, way, way],
                ns.at[step, way, way], nr.at[step, way, way], y_peer(steps[way]),
            )

    def reduce_y(step):
        group = z_group(step)
        for half in range(2):
            own = partial.at[y_half_of(group, y, half), :]
            total = own[...].astype(F32)
            for way in range(2):
                remote(
                    own, near_in.at[step, way, half],
                    ns.at[step, way, half], nr.at[step, way, half], y_peer(steps[way]),
                ).wait_recv()
                total += near_in[step, way, half].astype(F32)
            z_out[step, half * PAIR_ROWS : (half + 1) * PAIR_ROWS, :] = product_rounded(total)

        @pl.when(step < GROUPS - 1)
        def _():
            start_copy(
                z_out.at[step], z_in.at[step], zs.at[step], zr.at[step], q_peer(group)
            )

    def product_step(step, carry):
        pl.when(step < GROUPS)(lambda: correlate(step))
        pl.when((step > 0) & (step <= GROUPS))(lambda: relay(step - 1))
        pl.when(step > 1)(lambda: reduce_y(step - 2))
        return carry

    lax.fori_loop(0, GROUPS + 2, product_step, 0)

    total = z_out[GROUPS - 1].astype(F32)
    for n in range(GROUPS - 1):
        remote(z_out.at[n], z_in.at[n], zs.at[n], zr.at[n], z_pair).wait_recv()
        total += z_in[n].astype(F32)
    for half in range(2):
        rows = slice(half * PAIR_ROWS, (half + 1) * PAIR_ROWS)
        pair_out[rows, :] = product_rounded(total[rows, :])
    send(pair_out, pair_in, zps, zpr, z_pair)
    sums[...] = jnp.zeros_like(sums)
    remote(pair_out, pair_in, zps, zpr, z_pair).wait_recv()
    mine = total + pair_in[...].astype(F32)

    shape = (TURN_ROWS, ALL_CLASSES)
    valid = (lax.broadcasted_iota(jnp.int32, shape, 0) < ANGLES) & (
        lax.broadcasted_iota(jnp.int32, shape, 1) % BLOCK < CLASSES_HERE
    )
    products = walsh(mine, walsh_ref) * (1.0 / ALL_CLASSES)
    pieces = []
    for e in range(4):
        rows = mine[e * TURN_ROWS : (e + 1) * TURN_ROWS, :]
        ref_row = rows[36:37, :] + rows[37:38, :]
        part_row = rows[38:39, :] + rows[39:40, :]
        scaling = lax.rsqrt(part_row + EPSILON) * lax.rsqrt(ref_row + EPSILON)
        scores = jnp.where(
            valid, SHARPNESS * products[e * TURN_ROWS : (e + 1) * TURN_ROWS, :] * scaling, 0.0
        )
        raised = jnp.where(valid, jnp.exp(scores), 0.0)
        total = jnp.sum(jnp.sum(raised, axis=0, keepdims=True), axis=1, keepdims=True)
        pieces.append(raised / total)

    group_rows = weights.at[y_rows_of(q, y), :]
    group_rows[...] = jnp.concatenate(pieces, axis=0).astype(BF16)
    for d in (1, 3, 2):
        send(group_rows, group_rows, wzs.at[d], wzr.at[d], q_peer((q + d) % 4))

    def w_group(step):
        return (q + GROUPS - step) % GROUPS

    def spread(step):
        group = w_group(step)
        rows = weights.at[y_rows_of(group, y), :]

        @pl.when(step > 0)
        def _():
            remote(rows, rows, wzs.at[step], wzr.at[step], z_pair).wait_recv()

        for way in range(2):
            start_copy(rows, rows, wys.at[step, way], wyr.at[step, way], y_peer(steps[way]))

    def pass_on(step):
        group = w_group(step)
        for way in range(2):
            y_of = (y + NY - steps[way]) % NY
            rows = weights.at[y_rows_of(group, y_of), :]
            remote(
                rows, rows, wys.at[step, way], wyr.at[step, way], y_peer(steps[way])
            ).wait_recv()
            half = weights.at[y_half_of(group, y_of, way), :]
            start_copy(half, half, wfs.at[step, way], wfr.at[step, way], y_peer(steps[way]))

    def await_group(step):
        group = w_group(step)
        for way in range(2):
            half = weights.at[y_half_of(group, (y + 2) % NY, way), :]
            remote(
                half, half, wfs.at[step, way], wfr.at[step, way], y_peer(steps[way])
            ).wait_recv()
        return pl.ds(pl.multiple_of(group * GROUP_ROWS, GROUP_ROWS), GROUP_ROWS)

    def add_group(step):
        rows = await_group(step)
        picked_weights = weights[rows, :].T
        sums[:, 0:SIDE] += lax.dot_general(
            picked_weights, turned[rows, 0:SIDE], NN, preferred_element_type=F32
        )
        for r in range(CYCLES_HERE):
            lanes = slice(SIDE + r * 512, SIDE + (r + 1) * 512)
            sums[:, lanes] += lax.dot_general(
                picked_weights, turned[rows, lanes], NN, preferred_element_type=F32
            )

    def weight_step(step, carry):
        pl.when(step < GROUPS)(lambda: spread(step))
        pl.when((step > 0) & (step <= GROUPS))(lambda: pass_on(step - 1))
        pl.when(step > 1)(lambda: add_group(step - 2))
        return carry

    lax.fori_loop(0, GROUPS + 1, weight_step, 0)
    last_rows = await_group(GROUPS - 1)
    last_weights = weights[last_rows, :].T

    HALF = BLOCK // 2
    parts = (0, 1)
    part_lanes = (slice(0, SIDE + 1024), slice(SIDE + 1024, ROW_WIDTH))
    widths = (SIDE + 1024, 1024)

    def cut(part, buffer, *index):
        return buffer.at[(part, *index, slice(None), slice(0, widths[part]))]

    def rounded(part, total):
        if part == 1:
            return total.astype(BF16)
        whole = total[:, 0:SIDE]
        half_lane = lax.broadcasted_iota(jnp.int32, whole.shape, 1)
        whole = whole + pltpu.roll(whole, SIDE - CYCLES_HERE, 1)
        high = whole.astype(BF16).astype(F32)
        low = pltpu.roll(whole - high, CYCLES_HERE, 1)
        side = jnp.where(half_lane < CYCLES_HERE, high, jnp.where(half_lane < 2 * CYCLES_HERE, low, 0.0))
        return jnp.concatenate([side, total[:, SIDE:]], axis=1).astype(BF16)

    for part in parts:
        out_buf, in_buf = cut(part, core_out), cut(part, core_in)
        for n in range(2):
            first = SIDE + (part * 2 + n) * 512
            lanes = slice(first if first > SIDE else 0, first + 512)
            sums[:, lanes] += lax.dot_general(
                last_weights, turned[last_rows, lanes], NN, preferred_element_type=F32
            )
        for d in range(NX):
            out_buf[d * BLOCK : (d + 1) * BLOCK, :] = rounded(
                part, sums[class_rows(d, other), part_lanes[part]]
            )
        send(out_buf, in_buf, cs.at[part], cr.at[part], sibling)

    def core_sum(part, x_to, half):
        start = pl.multiple_of(x_to * BLOCK + half * HALF, HALF)
        return (
            sums[half_rows(x_to, core, half), part_lanes[part]]
            + core_in[part, pl.ds(start, HALF), 0 : widths[part]].astype(F32)
        )

    for part in parts:
        remote(
            cut(part, core_out), cut(part, core_in), cs.at[part], cr.at[part], sibling
        ).wait_recv()
        for way in range(2):
            far = cut(part, xfar_out, way)
            far[...] = rounded(part, core_sum(part, (x + 2) % NX, way))
            send(
                far, cut(part, xfar_in, way), xfs.at[part, way], xfr.at[part, way],
                x_peer(steps[way]),
            )
        for way in range(2):
            near = cut(part, xnear_out, way, 1 - way)
            near[...] = rounded(part, core_sum(part, (x + steps[way]) % NX, 1 - way))
            send(
                near, cut(part, xnear_in, way, 1 - way),
                xns.at[part, way, 1 - way], xnr.at[part, way, 1 - way], x_peer(steps[way]),
            )

    for part in parts:
        for way in range(2):
            far = cut(part, xfar_in, way)
            remote(
                cut(part, xfar_out, way), far, xfs.at[part, way], xfr.at[part, way],
                x_peer(steps[way]),
            ).wait_recv()
            near = cut(part, xnear_out, way, way)
            near[...] = rounded(
                part, core_sum(part, (x + steps[way]) % NX, way) + far[...].astype(F32)
            )
            send(
                near, cut(part, xnear_in, way, way),
                xns.at[part, way, way], xnr.at[part, way, way], x_peer(steps[way]),
            )

    for part in parts:
        for half in range(2):
            total = core_sum(part, x, half)
            for way in range(2):
                near = cut(part, xnear_in, way, half)
                remote(
                    cut(part, xnear_out, way, half), near,
                    xns.at[part, way, half], xnr.at[part, way, half], x_peer(steps[way]),
                ).wait_recv()
                total += near[...].astype(F32)
            out_buf = cut(part, rep_out, half)
            out_buf[...] = rounded(part, total)
            send(
                out_buf, cut(part, rep_via, half),
                p1s.at[part, half], p1r.at[part, half], via[half],
            )

    for part in parts:
        for half in range(2):
            via_buf = cut(part, rep_via, half)
            remote(
                cut(part, rep_out, half), via_buf,
                p1s.at[part, half], p1r.at[part, half], via[half],
            ).wait_recv()
            send(
                via_buf, cut(part, rep_in, half), p2s.at[part, half], p2r.at[part, half], via[half]
            )

    for copy in sent[:-4]:
        copy.wait_send()

    def drain(step, carry):
        for way in range(2):
            piece = near_out.at[step, way]
            remote(piece, piece, fs.at[step, way], fr.at[step, way], z_pair).wait_send()
            for half in range(2):
                remote(
                    piece, piece, ns.at[step, way, half], nr.at[step, way, half], z_pair
                ).wait_send()
            rows = weights.at[0:Y_ROWS, :]
            remote(rows, rows, wys.at[step, way], wyr.at[step, way], z_pair).wait_send()
            half = weights.at[0:PAIR_ROWS, :]
            remote(half, half, wfs.at[step, way], wfr.at[step, way], z_pair).wait_send()

        @pl.when(step < GROUPS - 1)
        def _():
            remote(z_out.at[step], z_in.at[step], zs.at[step], zr.at[step], z_pair).wait_send()

        return carry

    lax.fori_loop(0, GROUPS, drain, 0)

    density = None
    for part in parts:
        halves = []
        for half in range(2):
            in_buf = cut(part, rep_in, half)
            remote(
                cut(part, rep_via, half), in_buf,
                p2s.at[part, half], p2r.at[part, half], via[half],
            ).wait_recv()
            halves.append(cut(part, rep_out, half)[...].astype(F32) + in_buf[...].astype(F32))
        total = jnp.concatenate(halves, axis=0)
        if part == 0:
            density = total[:, 0:SIDE]
            total = total[:, SIDE:]
        flipped = []
        for n in range(2):
            r = part * 2 + n
            whole = density[:, r : r + 1] + density[:, r + 4 : r + 5]
            piece = total[:, n * 512 : (n + 1) * 512] / (whole + PRIOR_WEIGHT)
            flipped.append(jnp.concatenate([piece[:, 0:256], -piece[:, 256:512]], axis=1))
        result = dft(jnp.concatenate(flipped, axis=0), high_ref, low_ref)
        for n in range(2):
            for p in range(2):
                for h in range(2):
                    lanes = slice(p * 256 + h * 128, p * 256 + h * 128 + 128)
                    piece = result[n * BLOCK : (n + 1) * BLOCK, lanes]
                    start = (part * 2 + n) * 4 + h * 2 + p
                    padded[pl.ds(start, BLOCK, stride=16), :] = piece if p == 0 else -piece
    out_ref[...] = padded[0 : CLASSES_HERE * 16, :]

    for copy in sent[-4:]:
        copy.wait_send()


def to_rows(values):
    count = values.shape[0]
    return values.reshape(count, CYCLES_HERE, 2, 2, 128).transpose(0, 1, 3, 2, 4).reshape(count * 16, 128)


def from_rows(rows):
    return (
        rows.reshape(CLASSES_HERE, CYCLES_HERE, 2, 2, 128)
        .transpose(0, 1, 3, 2, 4)
        .reshape(CLASSES_HERE, CYCLES_HERE, 2, 256)
    )


def per_device(particles, references, ctf_table, defocus_ids, rotation_ids):
    vmem = pl.BlockSpec(memory_space=pltpu.VMEM)
    dma = pltpu.SemaphoreType.DMA
    out = pl.pallas_call(
        body,
        out_shape=jax.ShapeDtypeStruct((CLASSES_HERE * 16, 128), F32),
        in_specs=[pl.BlockSpec(memory_space=pl.ANY)] * 7,
        out_specs=vmem,
        scratch_shapes=[
            pltpu.VMEM((PARTICLES_HERE * 16, 128), F32),
            pltpu.VMEM((CLASSES_HERE * 16, 128), F32),
            pltpu.VMEM((512, 512), F32),
            pltpu.VMEM((ALL_CLASSES, ALL_CLASSES), F32),
            pltpu.VMEM((CYCLES_HERE, DEFOCI), F32),
            pltpu.VMEM((1, PARTICLES_HERE), jnp.int32),
            pltpu.VMEM((1, ANGLES), jnp.int32),
            pltpu.VMEM((512, 512), BF16),
            pltpu.VMEM((512, 512), BF16),
            pltpu.VMEM((ALL_CLASSES, ALL_CLASSES), BF16),
            pltpu.VMEM((DEFOCI, 128), F32),
            pltpu.VMEM((2 * TURN_ROWS, SAMPLES), F32),
            pltpu.VMEM((BLOCK * 16, 128), F32),
            pltpu.VMEM((CYCLES_HERE * PARTICLES_HERE, 512), F32),
            pltpu.VMEM((CYCLES_HERE * BLOCK, 512), F32),
            pltpu.VMEM((ALL_CLASSES, ROW_WIDTH), BF16),
            pltpu.VMEM((ALL_CLASSES, ROW_WIDTH - SIDE), BF16),
            pltpu.VMEM((PARTICLES_HERE, ROW_WIDTH - SIDE), F32),
            pltpu.VMEM((PARTICLES_HERE, 128), F32),
            pltpu.VMEM((4, PARTICLES_HERE, ALL_CLASSES), F32),
            pltpu.VMEM((ALL_ROWS, ROW_WIDTH), BF16),
            pltpu.VMEM((GROUP_ROWS, ALL_CLASSES), F32),
            pltpu.VMEM((ALL_ROWS, ALL_CLASSES), BF16),
            pltpu.VMEM((GROUPS, 2, PAIR_ROWS, ALL_CLASSES), BF16),
            pltpu.VMEM((GROUPS, 2, 2, PAIR_ROWS, ALL_CLASSES), BF16),
            pltpu.VMEM((GROUPS, 2, PAIR_ROWS, ALL_CLASSES), BF16),
            pltpu.VMEM((GROUPS, Y_ROWS, ALL_CLASSES), BF16),
            pltpu.VMEM((GROUPS - 1, Y_ROWS, ALL_CLASSES), BF16),
            pltpu.VMEM((Y_ROWS, ALL_CLASSES), BF16),
            pltpu.VMEM((Y_ROWS, ALL_CLASSES), BF16),
            pltpu.VMEM((ALL_ROWS, ALL_CLASSES), BF16),
            pltpu.VMEM((ALL_CLASSES, ROW_WIDTH), F32),
            pltpu.VMEM((2, NX * BLOCK, SIDE + 1024), BF16),
            pltpu.VMEM((2, NX * BLOCK, SIDE + 1024), BF16),
            pltpu.VMEM((2, 2, BLOCK // 2, SIDE + 1024), BF16),
            pltpu.VMEM((2, 2, BLOCK // 2, SIDE + 1024), BF16),
            pltpu.VMEM((2, 2, 2, BLOCK // 2, SIDE + 1024), BF16),
            pltpu.VMEM((2, 2, 2, BLOCK // 2, SIDE + 1024), BF16),
            pltpu.VMEM((2, 2, BLOCK // 2, SIDE + 1024), BF16),
            pltpu.VMEM((2, 2, BLOCK // 2, SIDE + 1024), BF16),
            pltpu.VMEM((2, 2, BLOCK // 2, SIDE + 1024), BF16),
            dma((7,)),
            dma((2,)), dma((2,)), dma((2,)), dma((2,)),
            dma((NX,)), dma((NX,)),
            dma((GROUPS, 2)), dma((GROUPS, 2)),
            dma((GROUPS, 2, 2)), dma((GROUPS, 2, 2)),
            dma((GROUPS - 1,)), dma((GROUPS - 1,)),
            dma(()), dma(()),
            dma((GROUPS,)), dma((GROUPS,)),
            dma((GROUPS, 2)), dma((GROUPS, 2)),
            dma((GROUPS, 2)), dma((GROUPS, 2)),
            dma((2,)), dma((2,)),
            dma((2, 2)), dma((2, 2)),
            dma((2, 2, 2)), dma((2, 2, 2)),
            dma((2, 2)), dma((2, 2)), dma((2, 2)), dma((2, 2)),
        ],
        compiler_params=pltpu.CompilerParams(
            collective_id=0, has_side_effects=True, vmem_limit_bytes=56 * 1024 * 1024
        ),
    )(
        to_rows(particles), to_rows(references), jnp.asarray(dft_matrix()), jnp.asarray(walsh_matrix()),
        ctf_table.T, defocus_ids.reshape(1, PARTICLES_HERE), rotation_ids.reshape(1, ANGLES),
    )
    return from_rows(out)


def solution(mesh):
    in_specs = (
        P(("cls", "rep"), "pix", None, None),
        P("cls", "pix", None, None),
        P(None, "pix"),
        P(("cls", "rep")),
        P(),
    )
    out_specs = P("cls", "pix", None, None)
    return jax.shard_map(
        per_device, mesh=mesh, in_specs=in_specs, out_specs=out_specs, check_vma=False
    )
```

```python
import math

import jax
import jax.numpy as jnp
import numpy as np
from jax import lax
from jax.experimental import pallas as pl
from jax.experimental.pallas import tpu as pltpu
from jax.sharding import PartitionSpec as P

TURN_STEPS = 360
DEFOCI = 16
EPSILON = 1e-06
SHARPNESS = 30.0
PRIOR_WEIGHT = 1.0

F32 = jnp.float32
BF16 = jnp.bfloat16
MESH = pl.DeviceIdType.MESH

SAMPLES = 256
ANGLES = 36
TURN_ROWS = 40
PAIR_ROWS = 2 * TURN_ROWS
PARTICLES_HERE = 64
CYCLES_HERE = 4
CLASSES_HERE = 25
BLOCK = 32
NX, NY, NZ = 4, 4, 8
ALL_CLASSES = 2 * NX * BLOCK
SIDE = 128
ROW_WIDTH = SIDE + CYCLES_HERE * 2 * SAMPLES
GROUPS = 4
Y_ROWS = 2 * PAIR_ROWS
GROUP_ROWS = NY * Y_ROWS
ALL_ROWS = GROUPS * GROUP_ROWS

NN = (((1,), (0,)), ((), ()))
NT = (((1,), (1,)), ((), ()))
TN = (((0,), (0,)), ((), ()))


def dft_matrix():
    positions = np.arange(SAMPLES)
    radians = (positions[:, None] * positions[None, :] % SAMPLES) * (2.0 * math.pi / SAMPLES)
    cosine = np.cos(radians) / math.sqrt(SAMPLES)
    sine = np.sin(radians) / math.sqrt(SAMPLES)
    return np.block([[cosine, -sine], [sine, cosine]]).astype(np.float32)


def walsh_matrix():
    matrix = np.ones((1, 1), np.float32)
    while matrix.shape[0] < ALL_CLASSES:
        matrix = np.block([[matrix, matrix], [matrix, -matrix]])
    return matrix


def split(values):
    high = values.astype(BF16)
    return high, (values - high.astype(F32)).astype(BF16)


def walsh(values, walsh_ref):
    high, low = split(values)
    return lax.dot_general(high, walsh_ref[...], NN, preferred_element_type=F32) + lax.dot_general(
        low, walsh_ref[...], NN, preferred_element_type=F32
    )


def dft(values, high_ref, low_ref):
    high, low = split(values)
    return (
        lax.dot_general(high, high_ref[...], NN, preferred_element_type=F32)
        + lax.dot_general(low, high_ref[...], NN, preferred_element_type=F32)
        + lax.dot_general(high, low_ref[...], NN, preferred_element_type=F32)
    )


def body(
    x_hbm, r_hbm, dft_hbm, walsh_hbm, ctf_hbm, ids_hbm, turns_hbm, out_ref,
    x_ref, r_ref, dft_ref, walsh_f, ctf_in, ids_ref, turns_ref,
    high_ref, low_ref, walsh_ref, ctf_ref, phase_ref,
    padded, x_rows, r_rows, spectra, mixed, weighted, power_rows, norm_rows, turned,
    partial_f, partial, far_in, near_in, near_out, z_out, z_in, pair_out, pair_in, weights,
    sums, core_out, core_in, xfar_out, xfar_in, xnear_out, xnear_in, rep_out, rep_via, rep_in,
    in_sem, rx_s, rx_r, rf_s, rf_r, rc_s, rc_r,
    fs, fr, ns, nr, zs, zr, zps, zpr, wzs, wzr, wys, wyr, wfs, wfr,
    cs, cr, xfs, xfr, xns, xnr, p1s, p1r, p2s, p2r,
):
    loads = [
        pltpu.make_async_copy(src, dst, in_sem.at[n])
        for n, (src, dst) in enumerate(
            [
                (r_hbm, r_ref), (dft_hbm, dft_ref), (x_hbm, x_ref), (ids_hbm, ids_ref),
                (turns_hbm, turns_ref), (ctf_hbm, ctf_in), (walsh_hbm, walsh_f),
            ]
        )
    ]
    for load in loads:
        load.start()
    cls = lax.axis_index("cls")
    pix = lax.axis_index("pix")
    rep = lax.axis_index("rep")
    x, core = cls // 2, cls % 2
    z, y = pix // NY, pix % NY
    other = 1 - core
    sibling = {"cls": x * 2 + other}

    def x_peer(d):
        return {"cls": (x + d) % NX * 2 + core}

    def y_peer(d):
        return {"pix": z * NY + (y + d) % NY}

    q, zh = z % 4, z // 4

    def q_peer(q_to):
        return {"pix": (zh * 4 + q_to) * NY + y}

    z_pair = {"pix": (z + 4) % NZ * NY + y}

    far_z = (z + 4) % NZ
    up = (z + 4) // NZ
    via = (
        {"pix": far_z * NY + y, "rep": (rep + up) % 2},
        {"pix": far_z * NY + y, "rep": (rep + 1 - up) % 2},
    )
    partners = (
        [sibling, {"pix": far_z * NY + y, "rep": 1 - rep}]
        + [x_peer(d) for d in (1, 3)]
        + [y_peer(d) for d in (1, 3)]
        + [q_peer((q + d) % 4) for d in range(1, 4)]
        + [z_pair]
    )

    def remote(src, dst, send, recv, device):
        return pltpu.make_async_remote_copy(
            src_ref=src, dst_ref=dst, send_sem=send, recv_sem=recv,
            device_id=device, device_id_type=MESH,
        )

    sent = []

    def start_copy(*args):
        remote(*args).start()

    def send(*args):
        copy = remote(*args)
        copy.start()
        sent.append(copy)

    barrier = pltpu.get_barrier_semaphore()
    for partner in partners:
        pl.semaphore_signal(barrier, inc=1, device_id=partner, device_id_type=MESH)

    loads[0].wait()
    loads[1].wait()
    high, low = split(dft_ref[...])
    high_ref[...] = high
    low_ref[...] = low
    padded[...] = jnp.zeros_like(padded)
    padded[0 : CLASSES_HERE * 16, :] = r_ref[...]
    for r in range(CYCLES_HERE):
        for p in range(2):
            for h in range(2):
                r_rows[r * BLOCK : (r + 1) * BLOCK, p * 256 + h * 128 : p * 256 + h * 128 + 128] = padded[
                    pl.ds(r * 4 + h * 2 + p, BLOCK, stride=16), :
                ]
    own = dft(r_rows[...], high_ref, low_ref).astype(BF16)
    own_rows = pl.ds(pl.multiple_of(cls * BLOCK, BLOCK), BLOCK)
    wide = own.astype(F32)
    power = jnp.sum(wide * wide, axis=1, keepdims=True)
    power_high, power_low = split(power)
    side_lane = lax.broadcasted_iota(jnp.int32, (BLOCK, SIDE), 1)
    side = jnp.zeros((BLOCK, SIDE), F32)
    for r in range(CYCLES_HERE):
        rows = slice(r * BLOCK, (r + 1) * BLOCK)
        spectra[own_rows, SIDE + r * 512 : SIDE + (r + 1) * 512] = own[rows, :]
        side = jnp.where(side_lane == r, power_high.astype(F32)[rows, :], side)
        side = jnp.where(side_lane == CYCLES_HERE + r, power_low.astype(F32)[rows, :], side)
    spectra[own_rows, 0:SIDE] = side.astype(BF16)

    pl.semaphore_wait(barrier, len(partners))
    steps = (1, 3)
    for way in range(2):
        send(
            spectra.at[own_rows, :], spectra.at[own_rows, :],
            rx_s.at[way], rx_r.at[way], x_peer(steps[way]),
        )
    send(spectra.at[own_rows, :], spectra.at[own_rows, :], rc_s.at[0], rc_r.at[0], sibling)

    def class_rows(x_of, core_of):
        return pl.ds(pl.multiple_of((x_of * 2 + core_of) * BLOCK, BLOCK), BLOCK)

    def half_rows(x_of, core_of, half):
        start = (x_of * 2 + core_of) * BLOCK + half * (BLOCK // 2)
        return pl.ds(pl.multiple_of(start, BLOCK // 2), BLOCK // 2)

    for load in loads[2:]:
        load.wait()
    walsh_ref[...] = walsh_f[...].astype(BF16)
    select = (
        lax.broadcasted_iota(jnp.int32, (CYCLES_HERE, 128), 1)
        - lax.broadcasted_iota(jnp.int32, (CYCLES_HERE, 128), 0)
    )
    select = ((select == 0) | (select == CYCLES_HERE)).astype(F32)
    ctf_ref[...] = lax.dot_general(
        ctf_in[...], select, TN, precision=lax.Precision.HIGHEST, preferred_element_type=F32
    )
    shape = (TURN_ROWS, ANGLES)
    on_row = lax.broadcasted_iota(jnp.int32, shape, 0) == lax.broadcasted_iota(jnp.int32, shape, 1)
    turns = jnp.sum(
        jnp.where(on_row, jnp.broadcast_to(turns_ref[...].astype(F32), shape), 0.0),
        axis=1, keepdims=True,
    )
    place = lax.broadcasted_iota(jnp.int32, (TURN_ROWS, SAMPLES), 1)
    signed = jnp.where(place < SAMPLES // 2, place, place - SAMPLES).astype(F32)
    count = turns * signed
    count = count - TURN_STEPS * jnp.floor(count * (1.0 / TURN_STEPS))
    count = jnp.where(count < 0, count + TURN_STEPS, count)
    count = jnp.where(count >= TURN_STEPS, count - TURN_STEPS, count)
    radians = count * (2.0 * math.pi / TURN_STEPS)
    phase_ref[0:TURN_ROWS, :] = jnp.cos(radians)
    phase_ref[TURN_ROWS : 2 * TURN_ROWS, :] = jnp.sin(radians)

    for r in range(CYCLES_HERE):
        for p in range(2):
            for h in range(2):
                x_rows[r * 64 : (r + 1) * 64, p * 256 + h * 128 : p * 256 + h * 128 + 128] = x_ref[
                    pl.ds(r * 4 + h * 2 + p, PARTICLES_HERE, stride=16), :
                ]
    part_square = jnp.zeros((PARTICLES_HERE, 128), F32)
    for r in range(CYCLES_HERE):
        for h in range(4):
            piece = x_rows[r * 64 : (r + 1) * 64, h * 128 : (h + 1) * 128]
            part_square += piece * piece
    part_norm = jnp.sum(part_square, axis=1, keepdims=True)
    picks = (
        lax.broadcasted_iota(jnp.int32, (DEFOCI, PARTICLES_HERE), 0) == ids_ref[...]
    ).astype(F32)
    ctf_rows = lax.dot_general(
        picks, ctf_ref[...], TN, precision=lax.Precision.HIGHEST, preferred_element_type=F32
    )
    particle_spectra = dft(x_rows[...], high_ref, low_ref)
    for r in range(CYCLES_HERE):
        weighted[:, r * 512 : (r + 1) * 512] = (
            ctf_rows[:, r : r + 1] * particle_spectra[r * 64 : (r + 1) * 64, :]
        )
    squared = ctf_rows * ctf_rows
    square_high = squared.astype(BF16).astype(F32)
    lane = lax.broadcasted_iota(jnp.int32, squared.shape, 1)
    power_rows[...] = jnp.where(lane < CYCLES_HERE, square_high, squared - square_high)

    for way in range(2):
        x_of = (x + NX - steps[way]) % NX
        rows = spectra.at[class_rows(x_of, core), :]
        remote(rows, rows, rx_s.at[way], rx_r.at[way], x_peer(steps[way])).wait_recv()
        half = spectra.at[half_rows(x_of, core, way), :]
        send(half, half, rf_s.at[way], rf_r.at[way], x_peer(steps[way]))
        send(rows, rows, rc_s.at[way + 1], rc_r.at[way + 1], sibling)

    cosine = phase_ref[0:TURN_ROWS, :]
    sine = phase_ref[TURN_ROWS : 2 * TURN_ROWS, :]

    def turn_pair(pair, carry):
        rows = pl.ds(pl.multiple_of(pair * PAIR_ROWS, 16), PAIR_ROWS)
        for r in range(CYCLES_HERE):
            real, imag = [], []
            for e in range(2):
                w_re = weighted[pl.ds(pair * 2 + e, 1), r * 512 : r * 512 + 256]
                w_im = weighted[pl.ds(pair * 2 + e, 1), r * 512 + 256 : r * 512 + 512]
                real.append(w_re * cosine - w_im * sine)
                imag.append(w_re * sine + w_im * cosine)
            start = SIDE + r * 512
            turned[rows, start : start + 256] = jnp.concatenate(real, axis=0).astype(BF16)
            turned[rows, start + 256 : start + 512] = jnp.concatenate(imag, axis=0).astype(BF16)
        tail = [
            jnp.broadcast_to(power_rows[pl.ds(pair * 2 + e, 1), :], (TURN_ROWS, 128)) for e in range(2)
        ]
        turned[rows, 0:SIDE] = jnp.concatenate(tail, axis=0).astype(BF16)
        return carry

    lax.fori_loop(0, PARTICLES_HERE // 4, turn_pair, 0)
    x_far = (x + 2) % NX
    for way in range(2):
        half = spectra.at[half_rows(x_far, core, way), :]
        remote(half, half, rf_s.at[way], rf_r.at[way], x_peer(steps[way])).wait_recv()
    rows = spectra.at[class_rows(x_far, core), :]
    send(rows, rows, rc_s.at[3], rc_r.at[3], sibling)
    lax.fori_loop(PARTICLES_HERE // 4, PARTICLES_HERE // 2, turn_pair, 0)

    wide_norm = jnp.broadcast_to(part_norm, (PARTICLES_HERE, ALL_CLASSES))
    wide_high = wide_norm.astype(BF16).astype(F32)
    norm_rows[2] = wide_high
    norm_rows[3] = wide_norm - wide_high
    ctf_high, ctf_low = split(ctf_ref[...] * ctf_ref[...])

    for n, x_of in enumerate((x, (x + 3) % NX, (x + 1) % NX, x_far)):
        rows = spectra.at[class_rows(x_of, other), :]
        remote(rows, rows, rc_s.at[n], rc_r.at[n], sibling).wait_recv()

    for r in range(CYCLES_HERE):
        mixed[:, r * 512 : (r + 1) * 512] = lax.dot_general(
            walsh_ref[...], spectra[:, SIDE + r * 512 : SIDE + (r + 1) * 512], NN,
            preferred_element_type=F32,
        ).astype(BF16)

    ref_norm = lax.dot_general(
        ctf_high, spectra[:, 0:SIDE], NT, preferred_element_type=F32
    ) + lax.dot_general(ctf_low, spectra[:, 0:SIDE], NT, preferred_element_type=F32)
    picked = lax.dot_general(
        picks, ref_norm, TN, precision=lax.Precision.HIGHEST, preferred_element_type=F32
    )
    picked_high = picked.astype(BF16).astype(F32)
    norm_rows[0] = picked_high
    norm_rows[1] = picked - picked_high
    sub = lax.broadcasted_iota(jnp.int32, (8, ALL_CLASSES), 0)

    def z_group(step):
        return (q + 1 + step) % GROUPS

    def y_rows_of(group, y_to):
        return pl.ds(pl.multiple_of(group * GROUP_ROWS + y_to * Y_ROWS, Y_ROWS), Y_ROWS)

    def y_half_of(group, y_to, half):
        start = group * GROUP_ROWS + y_to * Y_ROWS + half * PAIR_ROWS
        return pl.ds(pl.multiple_of(start, PAIR_ROWS), PAIR_ROWS)

    def correlate(step):
        group = z_group(step)
        rows = pl.ds(pl.multiple_of(group * GROUP_ROWS, GROUP_ROWS), GROUP_ROWS)
        partial_f[...] = lax.dot_general(
            turned[rows, SIDE:], mixed[...], NT, preferred_element_type=F32
        )

        def patch(pair, carry):
            pieces = []
            for e in range(2):
                start = pl.multiple_of(pair * PAIR_ROWS + e * TURN_ROWS, 8)
                pieces.append(partial_f[pl.ds(start, 32), :])
                last = partial_f[pl.ds(start + 32, 8), :]
                particle = group * 16 + pair * 2 + e
                for n in range(4):
                    last = jnp.where(sub == 4 + n, norm_rows[n, pl.ds(particle, 1), :], last)
                pieces.append(last)
            start = pl.multiple_of(group * GROUP_ROWS + pair * PAIR_ROWS, 16)
            partial[pl.ds(start, PAIR_ROWS), :] = jnp.concatenate(pieces, axis=0).astype(BF16)
            return carry

        lax.fori_loop(0, NY * 2, patch, 0)
        for way in range(2):
            start_copy(
                partial.at[y_half_of(group, (y + 2) % NY, way), :],
                far_in.at[step, way], fs.at[step, way], fr.at[step, way], y_peer(steps[way]),
            )

    odd_row = sub % 2 == 1

    def product_rounded(total):
        pieces = []
        for e in range(2):
            start = e * TURN_ROWS
            pieces.append(total[start : start + 32, :])
            last = total[start + 32 : start + 40, :]
            whole = last + pltpu.roll(last, 7, 0)
            high = whole.astype(BF16).astype(F32)
            low = pltpu.roll(whole - high, 1, 0)
            pieces.append(jnp.where(sub < 4, last, jnp.where(odd_row, low, high)))
        return jnp.concatenate(pieces, axis=0).astype(BF16)

    def relay(step):
        group = z_group(step)
        for way in range(2):
            own = partial.at[y_half_of(group, (y + steps[way]) % NY, way), :]
            remote(
                own, far_in.at[step, way], fs.at[step, way], fr.at[step, way], y_peer(steps[way])
            ).wait_recv()
            near_out[step, way, way] = product_rounded(
                own[...].astype(F32) + far_in[step, way].astype(F32)
            )
            near_out[step, way, 1 - way] = partial[
                y_half_of(group, (y + steps[way]) % NY, 1 - way), :
            ]
            start_copy(
                near_out.at[step, way], near_in.at[step, way],
                ns.at[step, way], nr.at[step, way], y_peer(steps[way]),
            )

    def reduce_y(step):
        group = z_group(step)
        for way in range(2):
            remote(
                near_out.at[step, way], near_in.at[step, way],
                ns.at[step, way], nr.at[step, way], y_peer(steps[way]),
            ).wait_recv()
        for half in range(2):
            total = partial[y_half_of(group, y, half), :].astype(F32)
            for way in range(2):
                total += near_in[step, way, half].astype(F32)
            z_out[step, half * PAIR_ROWS : (half + 1) * PAIR_ROWS, :] = product_rounded(total)

        @pl.when(step < GROUPS - 1)
        def _():
            start_copy(
                z_out.at[step], z_in.at[step], zs.at[step], zr.at[step], q_peer(group)
            )

    def product_step(step, carry):
        pl.when(step < GROUPS)(lambda: correlate(step))
        pl.when((step > 0) & (step <= GROUPS))(lambda: relay(step - 1))
        pl.when(step > 1)(lambda: reduce_y(step - 2))
        return carry

    lax.fori_loop(0, GROUPS + 2, product_step, 0)

    total = z_out[GROUPS - 1].astype(F32)
    for n in range(GROUPS - 1):
        remote(z_out.at[n], z_in.at[n], zs.at[n], zr.at[n], z_pair).wait_recv()
        total += z_in[n].astype(F32)
    for half in range(2):
        rows = slice(half * PAIR_ROWS, (half + 1) * PAIR_ROWS)
        pair_out[rows, :] = product_rounded(total[rows, :])
    send(pair_out, pair_in, zps, zpr, z_pair)
    sums[...] = jnp.zeros_like(sums)
    remote(pair_out, pair_in, zps, zpr, z_pair).wait_recv()
    mine = total + pair_in[...].astype(F32)

    shape = (TURN_ROWS, ALL_CLASSES)
    valid = (lax.broadcasted_iota(jnp.int32, shape, 0) < ANGLES) & (
        lax.broadcasted_iota(jnp.int32, shape, 1) % BLOCK < CLASSES_HERE
    )
    products = walsh(mine, walsh_ref) * (1.0 / ALL_CLASSES)
    pieces = []
    for e in range(4):
        rows = mine[e * TURN_ROWS : (e + 1) * TURN_ROWS, :]
        ref_row = rows[36:37, :] + rows[37:38, :]
        part_row = rows[38:39, :] + rows[39:40, :]
        scaling = lax.rsqrt(part_row + EPSILON) * lax.rsqrt(ref_row + EPSILON)
        scores = jnp.where(
            valid, SHARPNESS * products[e * TURN_ROWS : (e + 1) * TURN_ROWS, :] * scaling, 0.0
        )
        raised = jnp.where(valid, jnp.exp(scores), 0.0)
        total = jnp.sum(jnp.sum(raised, axis=0, keepdims=True), axis=1, keepdims=True)
        pieces.append(raised / total)

    group_rows = weights.at[y_rows_of(q, y), :]
    group_rows[...] = jnp.concatenate(pieces, axis=0).astype(BF16)
    for d in (1, 3, 2):
        send(group_rows, group_rows, wzs.at[d], wzr.at[d], q_peer((q + d) % 4))

    def w_group(step):
        return (q + GROUPS - step) % GROUPS

    def spread(step):
        group = w_group(step)
        rows = weights.at[y_rows_of(group, y), :]

        @pl.when(step > 0)
        def _():
            remote(rows, rows, wzs.at[step], wzr.at[step], z_pair).wait_recv()

        for way in range(2):
            start_copy(rows, rows, wys.at[step, way], wyr.at[step, way], y_peer(steps[way]))

    def pass_on(step):
        group = w_group(step)
        for way in range(2):
            y_of = (y + NY - steps[way]) % NY
            rows = weights.at[y_rows_of(group, y_of), :]
            remote(
                rows, rows, wys.at[step, way], wyr.at[step, way], y_peer(steps[way])
            ).wait_recv()
            half = weights.at[y_half_of(group, y_of, way), :]
            start_copy(half, half, wfs.at[step, way], wfr.at[step, way], y_peer(steps[way]))

    def await_group(step):
        group = w_group(step)
        for way in range(2):
            half = weights.at[y_half_of(group, (y + 2) % NY, way), :]
            remote(
                half, half, wfs.at[step, way], wfr.at[step, way], y_peer(steps[way])
            ).wait_recv()
        return pl.ds(pl.multiple_of(group * GROUP_ROWS, GROUP_ROWS), GROUP_ROWS)

    def add_group(step):
        rows = await_group(step)
        picked_weights = weights[rows, :].T
        sums[:, 0:SIDE] += lax.dot_general(
            picked_weights, turned[rows, 0:SIDE], NN, preferred_element_type=F32
        )
        for r in range(CYCLES_HERE):
            lanes = slice(SIDE + r * 512, SIDE + (r + 1) * 512)
            sums[:, lanes] += lax.dot_general(
                picked_weights, turned[rows, lanes], NN, preferred_element_type=F32
            )

    def weight_step(step, carry):
        pl.when(step < GROUPS)(lambda: spread(step))
        pl.when((step > 0) & (step <= GROUPS))(lambda: pass_on(step - 1))
        pl.when(step > 1)(lambda: add_group(step - 2))
        return carry

    lax.fori_loop(0, GROUPS + 1, weight_step, 0)
    last_rows = await_group(GROUPS - 1)
    last_weights = weights[last_rows, :].T

    HALF = BLOCK // 2
    parts = (0, 1)
    part_lanes = (slice(0, SIDE + 1024), slice(SIDE + 1024, ROW_WIDTH))
    widths = (SIDE + 1024, 1024)

    def cut(part, buffer, *index):
        return buffer.at[(part, *index, slice(None), slice(0, widths[part]))]

    def rounded(part, total):
        if part == 1:
            return total.astype(BF16)
        whole = total[:, 0:SIDE]
        half_lane = lax.broadcasted_iota(jnp.int32, whole.shape, 1)
        whole = whole + pltpu.roll(whole, SIDE - CYCLES_HERE, 1)
        high = whole.astype(BF16).astype(F32)
        low = pltpu.roll(whole - high, CYCLES_HERE, 1)
        side = jnp.where(half_lane < CYCLES_HERE, high, jnp.where(half_lane < 2 * CYCLES_HERE, low, 0.0))
        return jnp.concatenate([side, total[:, SIDE:]], axis=1).astype(BF16)

    for part in parts:
        out_buf, in_buf = cut(part, core_out), cut(part, core_in)
        for n in range(2):
            first = SIDE + (part * 2 + n) * 512
            lanes = slice(first if first > SIDE else 0, first + 512)
            sums[:, lanes] += lax.dot_general(
                last_weights, turned[last_rows, lanes], NN, preferred_element_type=F32
            )
        for d in range(NX):
            out_buf[d * BLOCK : (d + 1) * BLOCK, :] = rounded(
                part, sums[class_rows(d, other), part_lanes[part]]
            )
        send(out_buf, in_buf, cs.at[part], cr.at[part], sibling)

    def core_sum(part, x_to, half):
        start = pl.multiple_of(x_to * BLOCK + half * HALF, HALF)
        return (
            sums[half_rows(x_to, core, half), part_lanes[part]]
            + core_in[part, pl.ds(start, HALF), 0 : widths[part]].astype(F32)
        )

    for part in parts:
        remote(
            cut(part, core_out), cut(part, core_in), cs.at[part], cr.at[part], sibling
        ).wait_recv()
        for way in range(2):
            far = cut(part, xfar_out, way)
            far[...] = rounded(part, core_sum(part, (x + 2) % NX, way))
            send(
                far, cut(part, xfar_in, way), xfs.at[part, way], xfr.at[part, way],
                x_peer(steps[way]),
            )
        for way in range(2):
            near = cut(part, xnear_out, way, 1 - way)
            near[...] = rounded(part, core_sum(part, (x + steps[way]) % NX, 1 - way))
            send(
                near, cut(part, xnear_in, way, 1 - way),
                xns.at[part, way, 1 - way], xnr.at[part, way, 1 - way], x_peer(steps[way]),
            )

    for part in parts:
        for way in range(2):
            far = cut(part, xfar_in, way)
            remote(
                cut(part, xfar_out, way), far, xfs.at[part, way], xfr.at[part, way],
                x_peer(steps[way]),
            ).wait_recv()
            near = cut(part, xnear_out, way, way)
            near[...] = rounded(
                part, core_sum(part, (x + steps[way]) % NX, way) + far[...].astype(F32)
            )
            send(
                near, cut(part, xnear_in, way, way),
                xns.at[part, way, way], xnr.at[part, way, way], x_peer(steps[way]),
            )

    for part in parts:
        for half in range(2):
            total = core_sum(part, x, half)
            for way in range(2):
                near = cut(part, xnear_in, way, half)
                remote(
                    cut(part, xnear_out, way, half), near,
                    xns.at[part, way, half], xnr.at[part, way, half], x_peer(steps[way]),
                ).wait_recv()
                total += near[...].astype(F32)
            out_buf = cut(part, rep_out, half)
            out_buf[...] = rounded(part, total)
            send(
                out_buf, cut(part, rep_via, half),
                p1s.at[part, half], p1r.at[part, half], via[half],
            )

    for part in parts:
        for half in range(2):
            via_buf = cut(part, rep_via, half)
            remote(
                cut(part, rep_out, half), via_buf,
                p1s.at[part, half], p1r.at[part, half], via[half],
            ).wait_recv()
            send(
                via_buf, cut(part, rep_in, half), p2s.at[part, half], p2r.at[part, half], via[half]
            )

    for copy in sent[:-4]:
        copy.wait_send()

    def drain(step, carry):
        for way in range(2):
            piece = far_in.at[step, way]
            remote(piece, piece, fs.at[step, way], fr.at[step, way], z_pair).wait_send()
            piece = near_out.at[step, way]
            remote(piece, piece, ns.at[step, way], nr.at[step, way], z_pair).wait_send()
            rows = weights.at[0:Y_ROWS, :]
            remote(rows, rows, wys.at[step, way], wyr.at[step, way], z_pair).wait_send()
            half = weights.at[0:PAIR_ROWS, :]
            remote(half, half, wfs.at[step, way], wfr.at[step, way], z_pair).wait_send()

        @pl.when(step < GROUPS - 1)
        def _():
            remote(z_out.at[step], z_in.at[step], zs.at[step], zr.at[step], z_pair).wait_send()

        return carry

    lax.fori_loop(0, GROUPS, drain, 0)

    density = None
    for part in parts:
        halves = []
        for half in range(2):
            in_buf = cut(part, rep_in, half)
            remote(
                cut(part, rep_via, half), in_buf,
                p2s.at[part, half], p2r.at[part, half], via[half],
            ).wait_recv()
            halves.append(cut(part, rep_out, half)[...].astype(F32) + in_buf[...].astype(F32))
        total = jnp.concatenate(halves, axis=0)
        if part == 0:
            density = total[:, 0:SIDE]
            total = total[:, SIDE:]
        flipped = []
        for n in range(2):
            r = part * 2 + n
            whole = density[:, r : r + 1] + density[:, r + 4 : r + 5]
            piece = total[:, n * 512 : (n + 1) * 512] / (whole + PRIOR_WEIGHT)
            flipped.append(jnp.concatenate([piece[:, 0:256], -piece[:, 256:512]], axis=1))
        result = dft(jnp.concatenate(flipped, axis=0), high_ref, low_ref)
        for n in range(2):
            for p in range(2):
                for h in range(2):
                    lanes = slice(p * 256 + h * 128, p * 256 + h * 128 + 128)
                    piece = result[n * BLOCK : (n + 1) * BLOCK, lanes]
                    start = (part * 2 + n) * 4 + h * 2 + p
                    padded[pl.ds(start, BLOCK, stride=16), :] = piece if p == 0 else -piece
    out_ref[...] = padded[0 : CLASSES_HERE * 16, :]

    for copy in sent[-4:]:
        copy.wait_send()


def to_rows(values):
    count = values.shape[0]
    return values.reshape(count, CYCLES_HERE, 2, 2, 128).transpose(0, 1, 3, 2, 4).reshape(count * 16, 128)


def from_rows(rows):
    return (
        rows.reshape(CLASSES_HERE, CYCLES_HERE, 2, 2, 128)
        .transpose(0, 1, 3, 2, 4)
        .reshape(CLASSES_HERE, CYCLES_HERE, 2, 256)
    )


def per_device(particles, references, ctf_table, defocus_ids, rotation_ids):
    vmem = pl.BlockSpec(memory_space=pltpu.VMEM)
    dma = pltpu.SemaphoreType.DMA
    out = pl.pallas_call(
        body,
        out_shape=jax.ShapeDtypeStruct((CLASSES_HERE * 16, 128), F32),
        in_specs=[pl.BlockSpec(memory_space=pl.ANY)] * 7,
        out_specs=vmem,
        scratch_shapes=[
            pltpu.VMEM((PARTICLES_HERE * 16, 128), F32),
            pltpu.VMEM((CLASSES_HERE * 16, 128), F32),
            pltpu.VMEM((512, 512), F32),
            pltpu.VMEM((ALL_CLASSES, ALL_CLASSES), F32),
            pltpu.VMEM((CYCLES_HERE, DEFOCI), F32),
            pltpu.VMEM((1, PARTICLES_HERE), jnp.int32),
            pltpu.VMEM((1, ANGLES), jnp.int32),
            pltpu.VMEM((512, 512), BF16),
            pltpu.VMEM((512, 512), BF16),
            pltpu.VMEM((ALL_CLASSES, ALL_CLASSES), BF16),
            pltpu.VMEM((DEFOCI, 128), F32),
            pltpu.VMEM((2 * TURN_ROWS, SAMPLES), F32),
            pltpu.VMEM((BLOCK * 16, 128), F32),
            pltpu.VMEM((CYCLES_HERE * PARTICLES_HERE, 512), F32),
            pltpu.VMEM((CYCLES_HERE * BLOCK, 512), F32),
            pltpu.VMEM((ALL_CLASSES, ROW_WIDTH), BF16),
            pltpu.VMEM((ALL_CLASSES, ROW_WIDTH - SIDE), BF16),
            pltpu.VMEM((PARTICLES_HERE, ROW_WIDTH - SIDE), F32),
            pltpu.VMEM((PARTICLES_HERE, 128), F32),
            pltpu.VMEM((4, PARTICLES_HERE, ALL_CLASSES), F32),
            pltpu.VMEM((ALL_ROWS, ROW_WIDTH), BF16),
            pltpu.VMEM((GROUP_ROWS, ALL_CLASSES), F32),
            pltpu.VMEM((ALL_ROWS, ALL_CLASSES), BF16),
            pltpu.VMEM((GROUPS, 2, PAIR_ROWS, ALL_CLASSES), BF16),
            pltpu.VMEM((GROUPS, 2, 2, PAIR_ROWS, ALL_CLASSES), BF16),
            pltpu.VMEM((GROUPS, 2, 2, PAIR_ROWS, ALL_CLASSES), BF16),
            pltpu.VMEM((GROUPS, Y_ROWS, ALL_CLASSES), BF16),
            pltpu.VMEM((GROUPS - 1, Y_ROWS, ALL_CLASSES), BF16),
            pltpu.VMEM((Y_ROWS, ALL_CLASSES), BF16),
            pltpu.VMEM((Y_ROWS, ALL_CLASSES), BF16),
            pltpu.VMEM((ALL_ROWS, ALL_CLASSES), BF16),
            pltpu.VMEM((ALL_CLASSES, ROW_WIDTH), F32),
            pltpu.VMEM((2, NX * BLOCK, SIDE + 1024), BF16),
            pltpu.VMEM((2, NX * BLOCK, SIDE + 1024), BF16),
            pltpu.VMEM((2, 2, BLOCK // 2, SIDE + 1024), BF16),
            pltpu.VMEM((2, 2, BLOCK // 2, SIDE + 1024), BF16),
            pltpu.VMEM((2, 2, 2, BLOCK // 2, SIDE + 1024), BF16),
            pltpu.VMEM((2, 2, 2, BLOCK // 2, SIDE + 1024), BF16),
            pltpu.VMEM((2, 2, BLOCK // 2, SIDE + 1024), BF16),
            pltpu.VMEM((2, 2, BLOCK // 2, SIDE + 1024), BF16),
            pltpu.VMEM((2, 2, BLOCK // 2, SIDE + 1024), BF16),
            dma((7,)),
            dma((2,)), dma((2,)), dma((2,)), dma((2,)),
            dma((NX,)), dma((NX,)),
            dma((GROUPS, 2)), dma((GROUPS, 2)),
            dma((GROUPS, 2)), dma((GROUPS, 2)),
            dma((GROUPS - 1,)), dma((GROUPS - 1,)),
            dma(()), dma(()),
            dma((GROUPS,)), dma((GROUPS,)),
            dma((GROUPS, 2)), dma((GROUPS, 2)),
            dma((GROUPS, 2)), dma((GROUPS, 2)),
            dma((2,)), dma((2,)),
            dma((2, 2)), dma((2, 2)),
            dma((2, 2, 2)), dma((2, 2, 2)),
            dma((2, 2)), dma((2, 2)), dma((2, 2)), dma((2, 2)),
        ],
        compiler_params=pltpu.CompilerParams(
            collective_id=0, has_side_effects=True, vmem_limit_bytes=56 * 1024 * 1024
        ),
    )(
        to_rows(particles), to_rows(references), jnp.asarray(dft_matrix()), jnp.asarray(walsh_matrix()),
        ctf_table.T, defocus_ids.reshape(1, PARTICLES_HERE), rotation_ids.reshape(1, ANGLES),
    )
    return from_rows(out)


def solution(mesh):
    in_specs = (
        P(("cls", "rep"), "pix", None, None),
        P("cls", "pix", None, None),
        P(None, "pix"),
        P(("cls", "rep")),
        P(),
    )
    out_specs = P("cls", "pix", None, None)
    return jax.shard_map(
        per_device, mesh=mesh, in_specs=in_specs, out_specs=out_specs, check_vma=False
    )
```
